128 devices in a mesh: dp: 16 (over x_lo, y, core), tensor: 8 (over z, x_hi).
Axes of the slice: x: 4 (x_hi: 2, x_lo: 2; x = x_hi * 2 + x_lo), y: 4, z: 4, core: 2. Of those that a mesh axis runs over, the one named last changes fastest.
Arguments:
- tokens: bfloat16 [16384, 2048], P(('dp', 'tensor')), may hold values from -24 to 24
- cotangent: bfloat16 [16384, 2048], P(('dp', 'tensor')), may hold values from -24 to 24
- attn_weight: float32 [4, 2048, 2048], P(None, 'dp', 'tensor'), may hold values from -1.41421356 to 1.41421356
- mlp_weight: float32 [2, 2048, 8192], P(None, 'dp', 'tensor'), may hold values from -0.088388348 to 0.088388348
- qkv_bias: float32 [3, 2048], P(None, 'tensor'), may hold values from -1.25 to 1.25
- fc1_bias: float32 [8192], P('tensor'), may hold values from -1.25 to 1.25
- vectors: float32 [4, 2048], replicated, may hold values from -0.4 to 1.4
- attn_first: float32 [4, 2048, 2048], P(None, 'dp', 'tensor'), may hold values from -24 to 24
- mlp_first: float32 [2, 2048, 8192], P(None, 'dp', 'tensor'), may hold values from -24 to 24
- qkv_first: float32 [3, 2048], P(None, 'tensor'), may hold values from -1280 to 1280
- fc1_first: float32 [8192], P('tensor'), may hold values from -24 to 24
- vector_first: float32 [4, 2048], replicated, may hold values from -1280 to 1280
- attn_second: float32 [4, 2048, 2048], P(None, 'dp', 'tensor'), may hold values from 0.8192 to 11.4688
- mlp_second: float32 [2, 2048, 8192], P(None, 'dp', 'tensor'), may hold values from 0.8192 to 11.4688
- qkv_second: float32 [3, 2048], P(None, 'tensor'), may hold values from 4194.304 to 16777.217
- fc1_second: float32 [8192], P('tensor'), may hold values from 0.8192 to 11.4688
- vector_second: float32 [4, 2048], replicated, may hold values from 4194.304 to 16777.217
Outputs:
- out: bfloat16 [16384, 2048], P(('dp', 'tensor'))
- input_grad: float32 [16384, 2048], P(('dp', 'tensor'))
- attn_grad: float32 [4, 2048, 2048], P(None, 'dp', 'tensor')
- attn_first_new: float32 [4, 2048, 2048], P(None, 'dp', 'tensor')
- attn_second_new: float32 [4, 2048, 2048], P(None, 'dp', 'tensor')
- attn_new: float32 [4, 2048, 2048], P(None, 'dp', 'tensor')
- mlp_grad: float32 [2, 2048, 8192], P(None, 'dp', 'tensor')
- mlp_first_new: float32 [2, 2048, 8192], P(None, 'dp', 'tensor')
- mlp_second_new: float32 [2, 2048, 8192], P(None, 'dp', 'tensor')
- mlp_new: float32 [2, 2048, 8192], P(None, 'dp', 'tensor')
- qkv_grad: float32 [3, 2048], P(None, 'tensor')
- qkv_first_new: float32 [3, 2048], P(None, 'tensor')
- qkv_second_new: float32 [3, 2048], P(None, 'tensor')
- qkv_new: float32 [3, 2048], P(None, 'tensor')
- fc1_grad: float32 [8192], P('tensor')
- fc1_first_new: float32 [8192], P('tensor')
- fc1_second_new: float32 [8192], P('tensor')
- fc1_new: float32 [8192], P('tensor')
- vector_grad: float32 [4, 2048], replicated
- vector_first_new: float32 [4, 2048], replicated
- vector_second_new: float32 [4, 2048], replicated
- vector_new: float32 [4, 2048], replicated
The draws below stay inside these ranges and needn't reach their ends.
All inputs are finite; a program needn't handle non-finite values.
Results may differ from the reference program's by a relative error of at most 0.012.
Values may be sent and summed in bfloat16 or wider, within the bound.
No kernel may reach another device: no remote copies, remote signals or barrier semaphores. Data moves between devices by JAX's collectives and lax.ppermute only.
A program may use at most 192 MiB of HBM per device.

```python
import math
import jax
import jax.numpy as jnp
from jax import lax

D = 2048
H = 32
HD = 64
ROT = 32
FF = 8192
LEN = 1024
STEP = 10
TOKENS = 16384


def draw_attn_weight(key, part):
    key = jax.random.fold_in(key, 11)
    base = jax.random.truncated_normal(key, -4.0, 4.0, (4, D, D), jnp.float32)
    factor = jnp.where(jnp.arange(4) == 3, 0.5 * LEN ** 0.5, 1.0) * D ** (-0.5)
    return base * factor.astype(jnp.float32)[:, None, None]


def draw_mlp_weight(key, part):
    key = jax.random.fold_in(key, 23)
    base = jax.random.truncated_normal(key, -4.0, 4.0, (2, D, FF), jnp.float32)
    factor = jnp.where(jnp.arange(2) == 0, D ** (-0.5), FF ** (-0.5))
    return base * factor.astype(jnp.float32)[:, None, None]


def draw_vectors(key, part):
    key = jax.random.fold_in(key, 37)
    base = jax.random.truncated_normal(key, -4.0, 4.0, (4, D), jnp.float32)
    offset = jnp.where(jnp.arange(4) == 0, 1.0, 0.0).astype(jnp.float32)
    return base * 0.1 + offset[:, None]


def raised(entries, own_key, source, target, parts, factor):
    owner, partner = [(jnp.arange(entries.shape[axis_at]) // (entries.shape[axis_at] // parts)).reshape([-1 if axis == axis_at else 1 for axis in range(entries.ndim)]) for axis_at in (source, target)]
    chosen = jax.random.permutation(own_key, parts)[partner]
    strong = (owner == chosen) | (owner == (partner + parts // 2) % parts)
    return jnp.where(strong, factor * entries, entries)


def steps_of(stream_key, shape, pieces, least, high):
    gain = 1.0
    for dim, shards_of in pieces:
        steps = jax.random.uniform(jax.random.fold_in(jax.random.fold_in(stream_key, 6), dim), (shards_of,), jnp.float32, least / len(pieces), high / len(pieces))
        gain = gain * jnp.repeat(jnp.exp(steps), shape[dim] // shards_of).reshape((-1,) + (1,) * (len(shape) - 1 - dim))
    return gain


def scatter_about(key, dims, width, most, shards=(), held_as=jnp.bfloat16):
    loudness = steps_of(key, dims, shards, -0.22, 0.18) if shards else 1.0
    entries = jax.random.normal(key, dims, jnp.float32) * width * loudness
    return jnp.minimum(jnp.maximum(entries, -most), most).astype(held_as)


def heavy_noise(own_key, dims, spread, limit, shards, heavy, held_as=jnp.bfloat16):
    entries = spread * jax.random.normal(own_key, dims, jnp.float32)
    if shards:
        entries = entries * steps_of(own_key, dims, shards, -0.22, 0.18)
    return jnp.clip(raised(entries, jax.random.fold_in(own_key, 3), *heavy), -limit, limit).astype(held_as)


def setup_inputs(seed: int = 0) -> dict:
    key_list = jax.random.split(jax.random.key(seed), 18)
    return {
        "tokens": heavy_noise(key_list[0], (TOKENS, D), 1.0, 24.0, ((0, 128),), (0, 1, 128, 5.5)),
        "cotangent": heavy_noise(key_list[1], (TOKENS, D), 1.0, 24.0, ((0, 128),), (0, 1, 128, 5.5)),
        "attn_weight": draw_attn_weight(jax.random.fold_in(key_list[17], 71), 0),
        "mlp_weight": draw_mlp_weight(jax.random.fold_in(key_list[17], 71), 0),
        "qkv_bias": scatter_about(key_list[4], (3, D), 0.2, 1.25, ((1, 8),), jnp.float32),
        "fc1_bias": scatter_about(key_list[5], (FF,), 0.2, 1.25, ((0, 8),), jnp.float32),
        "vectors": draw_vectors(jax.random.fold_in(key_list[17], 71), 0),
        "attn_first": scatter_about(key_list[7], (4, D, D), (0.03 * TOKENS ** 0.5), 24.0, ((1, 16), (2, 8)), jnp.float32),
        "mlp_first": scatter_about(key_list[8], (2, D, FF), (0.03 * TOKENS ** 0.5), 24.0, ((1, 16), (2, 8)), jnp.float32),
        "qkv_first": scatter_about(key_list[9], (3, D), (0.05 * (TOKENS * LEN) ** 0.5), 1280.0, ((1, 8),), jnp.float32),
        "fc1_first": scatter_about(key_list[10], (FF,), (0.03 * TOKENS ** 0.5), 24.0, ((0, 8),), jnp.float32),
        "vector_first": scatter_about(key_list[11], (4, D), (0.05 * (TOKENS * LEN) ** 0.5), 1280.0, (), jnp.float32),
        "attn_second": jnp.clip(jnp.exp(math.log(11.4688) - 2.6390573 * jax.random.uniform(key_list[12], (4, D, D), jnp.float32) ** steps_of(key_list[12], (4, D, D), ((1, 16), (2, 8)), -0.2, 0.2)), 0.8192, 11.4688),
        "mlp_second": jnp.clip(jnp.exp(math.log(11.4688) - 2.6390573 * jax.random.uniform(key_list[13], (2, D, FF), jnp.float32) ** steps_of(key_list[13], (2, D, FF), ((1, 16), (2, 8)), -0.2, 0.2)), 0.8192, 11.4688),
        "qkv_second": jnp.clip(jnp.exp(math.log(16777.217) - 1.3862944 * jax.random.uniform(key_list[14], (3, D), jnp.float32) ** steps_of(key_list[14], (3, D), ((1, 8),), -0.2, 0.2)), 4194.304, 16777.217),
        "fc1_second": jnp.clip(jnp.exp(math.log(11.4688) - 2.6390573 * jax.random.uniform(key_list[15], (FF,), jnp.float32) ** steps_of(key_list[15], (FF,), ((0, 8),), -0.2, 0.2)), 0.8192, 11.4688),
        "vector_second": jnp.clip(jnp.exp(jax.random.uniform(key_list[16], (4, D), jnp.float32, math.log(4194.304), math.log(16777.217))), 4194.304, 16777.217),
    }


@jax.custom_vjp
def low(v):
    return lax.optimization_barrier(v.astype(jnp.bfloat16)).astype(jnp.float32)

@jax.custom_vjp
def low_back(v):
    return v

def low_keep(v):
    return (low(v), None)

def low_pass(kept, grad):
    return (grad,)

def back_keep(v):
    return (v, None)

def back_low(kept, grad):
    return (low(grad),)
low.defvjp(low_keep, low_pass)
low_back.defvjp(back_keep, back_low)
EPSILON = 1e-05
SCALE = 0.125
MASKED = -1000000000.0
HIGHEST = lax.Precision.HIGHEST
BETA_ONE = 0.9
BETA_TWO = 0.999
ADAM_EPSILON = 1e-08

def matmul(left, right):
    return jnp.dot(left, right, precision=HIGHEST, preferred_element_type=jnp.float32)

def rotary(values, length):
    half_rot = ROT // 2
    position = jnp.arange(length, dtype=jnp.float32)
    frequency = 10000.0 ** (-jnp.arange(half_rot, dtype=jnp.float32) * 2.0 / ROT)
    angle = position[:, None] * frequency[None, :]
    cosine = jnp.cos(angle)[:, None, :]
    sine = jnp.sin(angle)[:, None, :]
    first_half = values[..., :half_rot]
    second_half = values[..., half_rot:ROT]
    return jnp.concatenate([first_half * cosine - second_half * sine, second_half * cosine + first_half * sine, values[..., ROT:]], -1)

def attend(queries, keys, values):
    block_rows = min(512, LEN)
    block_count = LEN // block_rows
    query_blocks = queries.reshape(block_count, block_rows, H, HD)
    starts = jnp.arange(block_count, dtype=jnp.int32) * block_rows
    columns = jnp.arange(LEN, dtype=jnp.int32)

    def one_block(inputs_pair):
        query_rows, start = inputs_pair
        scores = low_back(jnp.einsum('qhd,khd->hqk', query_rows, keys, precision=HIGHEST) * SCALE)
        positions = start + jnp.arange(block_rows, dtype=jnp.int32)
        scores = jnp.where(columns[None, None, :] <= positions[None, :, None], scores, MASKED)
        largest = lax.optimization_barrier(jnp.max(scores, -1, keepdims=True))
        powers = jnp.exp(scores - largest)
        probs = low(powers / lax.optimization_barrier(jnp.sum(powers, -1, keepdims=True)))
        return jnp.einsum('hqk,khd->qhd', probs, values, precision=HIGHEST)
    return lax.map(jax.checkpoint(one_block), (query_blocks, starts)).reshape(LEN, D)

def layer(inputs, attn_weight, mlp_weight, qkv_bias, fc1_bias, vectors):
    centred = inputs - lax.optimization_barrier(jnp.mean(inputs, -1, keepdims=True))
    variance = lax.optimization_barrier(jnp.mean(centred * centred, -1, keepdims=True))
    normed = low(centred * lax.rsqrt(variance + EPSILON) * vectors[0] + vectors[1])
    attn_low = low(attn_weight)
    mlp_low = low(mlp_weight)
    queries = low_back(matmul(normed, attn_low[0]) + qkv_bias[0])
    keys = low_back(matmul(normed, attn_low[1]) + qkv_bias[1])
    values = low_back(low(matmul(normed, attn_low[2]) + qkv_bias[2]))
    queries = low(rotary(queries.reshape(LEN, H, HD), LEN))
    keys = low(rotary(keys.reshape(LEN, H, HD), LEN))
    attended = low_back(low(attend(queries, keys, values.reshape(LEN, H, HD))))
    hidden = low_back(matmul(normed, mlp_low[0]) + fc1_bias)
    activated = low(jax.nn.gelu(hidden, approximate=True))
    branch = matmul(attended, attn_low[3].T) + matmul(activated, mlp_low[1].T)
    return inputs + branch + vectors[2] + vectors[3]

def adamw(param, grad, first, second, rate, decay):
    first_new = BETA_ONE * first + (1.0 - BETA_ONE) * grad
    second_new = BETA_TWO * second + (1.0 - BETA_TWO) * grad * grad
    ratio = first_new / (1.0 - BETA_ONE ** STEP) / (jnp.sqrt(second_new / (1.0 - BETA_TWO ** STEP)) + ADAM_EPSILON)
    return (grad, first_new, second_new, param - rate * (ratio + decay * param))

def reference(tokens, cotangent, attn_weight, mlp_weight, qkv_bias, fc1_bias, vectors, attn_first, mlp_first, qkv_first, fc1_first, vector_first, attn_second, mlp_second, qkv_second, fc1_second, vector_second):
    seq_count = tokens.shape[0] // LEN
    inputs = tokens.astype(jnp.float32).reshape(seq_count, LEN, D)
    backs = cotangent.astype(jnp.float32).reshape(seq_count, LEN, D)
    params = (attn_weight, mlp_weight, qkv_bias, fc1_bias, vectors)

    def accumulate(totals, pair_item):
        seq_input, seq_back = pair_item
        result, pullback = jax.vjp(layer, seq_input, *params)
        grads = pullback(seq_back)
        new_totals = tuple((total + grad for total, grad in zip(totals, grads[1:])))
        return (new_totals, (result.astype(jnp.bfloat16), grads[0]))
    zeros = tuple((jnp.zeros_like(param) for param in params))
    totals, (outputs, input_grads) = lax.scan(accumulate, zeros, (inputs, backs))
    attn_out = adamw(attn_weight, totals[0], attn_first, attn_second, 0.04, 0.1)
    mlp_out = adamw(mlp_weight, totals[1], mlp_first, mlp_second, 0.04, 0.1)
    qkv_out = adamw(qkv_bias, totals[2], qkv_first, qkv_second, 0.3, 0.0)
    fc1_out = adamw(fc1_bias, totals[3], fc1_first, fc1_second, 0.3, 0.0)
    vector_out = adamw(vectors, totals[4], vector_first, vector_second, 0.2, 0.0)
    return (outputs.reshape(seq_count * LEN, D), input_grads.reshape(seq_count * LEN, D), attn_out[0], attn_out[1], attn_out[2], attn_out[3], mlp_out[0], mlp_out[1], mlp_out[2], mlp_out[3], qkv_out[0], qkv_out[1], qkv_out[2], qkv_out[3], fc1_out[0], fc1_out[1], fc1_out[2], fc1_out[3], vector_out[0], vector_out[1], vector_out[2], vector_out[3])
```

```python
import functools

import jax
import jax.numpy as jnp
from jax import lax
from jax.experimental import pallas as pl
from jax.experimental.pallas import tpu as pltpu
from jax.sharding import PartitionSpec as P

D = 2048
HD = 64
ROT = 32
LEN = 1024
STEP = 10
HEADS = 4
HC = HEADS * HD
FC = 1024
ROWS = 128
BQ = 256

EPSILON = 1e-05
SCALE = 0.125
BETA_ONE = 0.9
BETA_TWO = 0.999
ADAM_EPSILON = 1e-08
BF = jnp.bfloat16
F32 = jnp.float32
VMEM_LIMIT = 60 * 1024 * 1024


def dp_perm(move):
    pairs = []
    for x in range(2):
        for y in range(4):
            for c in range(2):
                nx, ny, nc = move(x, y, c)
                pairs.append(((x * 4 + y) * 2 + c, (nx * 4 + ny % 4) * 2 + nc))
    return pairs


def tensor_perm(move):
    pairs = []
    for z in range(4):
        for h in range(2):
            nz, nh = move(z, h)
            pairs.append((z * 2 + h, (nz % 4) * 2 + nh))
    return pairs


Y_UP = dp_perm(lambda x, y, c: (x, y + 1, c))
Y_DOWN = dp_perm(lambda x, y, c: (x, y - 1, c))
X_SWAP = dp_perm(lambda x, y, c: (1 - x, y, c))
CORE_SWAP = dp_perm(lambda x, y, c: (x, y, 1 - c))
Z_UP = tensor_perm(lambda z, h: (z + 1, h))
Z_DOWN = tensor_perm(lambda z, h: (z - 1, h))
Y_FLIP = dp_perm(lambda x, y, c: (x, y ^ 1, c))
Y_FAR = dp_perm(lambda x, y, c: (x, y + 2, c))
Z_FLIP = tensor_perm(lambda z, h: (z ^ 1, h))
Z_FAR = tensor_perm(lambda z, h: (z + 2, h))
H_SWAP = tensor_perm(lambda z, h: (z, 1 - h))


def at(array, index, axis):
    return lax.dynamic_index_in_dim(array, index, axis, keepdims=False)


def after(value, *others):
    return lax.optimization_barrier((value, *others))[0]


def up_z(v):
    return lax.ppermute(v, "tensor", Z_UP)


def down_z(v):
    return lax.ppermute(v, "tensor", Z_DOWN)


def swap_h(v):
    return lax.ppermute(v, "tensor", H_SWAP)


def up_y(v):
    return lax.ppermute(v, "dp", Y_UP)


def down_y(v):
    return lax.ppermute(v, "dp", Y_DOWN)


def swap_x(v):
    return lax.ppermute(v, "dp", X_SWAP)


def swap_core(v):
    return lax.ppermute(v, "dp", CORE_SWAP)


def params(**more):
    return pltpu.CompilerParams(vmem_limit_bytes=VMEM_LIMIT, **more)


def cost(flops, nbytes, transcendentals=0):
    return pl.CostEstimate(flops=flops, bytes_accessed=nbytes, transcendentals=transcendentals)


ANY = pl.BlockSpec(memory_space=pl.ANY)
SMEM = pl.BlockSpec(memory_space=pltpu.SMEM)


def whole(shape):
    return pl.BlockSpec(shape, lambda i, *_: (0,) * len(shape))


def norm_kernel(places, block, vectors, *refs):
    normed, normed_t, rows, stats = refs[-4:]
    inputs = block[...].astype(F32)
    mean = jnp.mean(inputs, -1, keepdims=True)
    centred = inputs - mean
    inverse = lax.rsqrt(jnp.mean(centred * centred, -1, keepdims=True) + EPSILON)
    value = (centred * inverse * vectors[0:1, :] + vectors[1:2, :]).astype(BF)
    normed[...] = value
    normed_t[...] = value.T
    rows[...] = block[...]
    lane = lax.broadcasted_iota(jnp.int32, (ROWS, 128), 1)
    stats[...] = jnp.where(lane < 64, mean, inverse)


def back_kernel(places, block, *refs):
    rows, rows_t = refs[-2:]
    rows[...] = block[...]
    rows_t[...] = block[...].T


ROW_BLOCK = pl.BlockSpec((ROWS, D), lambda i, places: (places[i], 0))
TURNED_BLOCK = pl.BlockSpec((D, ROWS), lambda i, places: (0, places[i]))
NORM_OUTS = (
    [ROW_BLOCK, TURNED_BLOCK, ROW_BLOCK, pl.BlockSpec((ROWS, 128), lambda i, places: (places[i], 0))],
    [
        jax.ShapeDtypeStruct((LEN, D), BF),
        jax.ShapeDtypeStruct((D, LEN), BF),
        jax.ShapeDtypeStruct((LEN, D), BF),
        jax.ShapeDtypeStruct((LEN, 128), F32),
    ],
)
BACK_OUTS = (
    [ROW_BLOCK, TURNED_BLOCK],
    [jax.ShapeDtypeStruct((LEN, D), BF), jax.ShapeDtypeStruct((D, LEN), BF)],
)


def place(kernel, outs, held, block, places, *more):
    count = block.shape[0] // ROWS
    specs, shapes = outs
    first = 2 + len(more)
    return pl.pallas_call(
        kernel,
        grid_spec=pltpu.PrefetchScalarGridSpec(
            num_scalar_prefetch=1,
            grid=(count,),
            in_specs=[pl.BlockSpec((ROWS, D), lambda i, places: (i, 0))]
            + [whole(m.shape) for m in more]
            + [ANY] * len(held),
            out_specs=specs,
        ),
        out_shape=shapes,
        input_output_aliases={first + i: i for i in range(len(held))},
        compiler_params=params(),
        cost_estimate=cost(0, 10 * count * ROWS * D),
    )(jnp.stack(places).astype(jnp.int32), block, *more, *held)


def place_all(kernel, outs, arrivals, more=()):
    held = ()
    for block, places in arrivals:
        held = place(kernel, outs, held, block, places, *more)
    return held


def gather_pairs(own, z, h, start):
    def at_z(step):
        base = lax.rem(z + step, 4) * 2
        return base + h, base + 1 - h

    if start is None:
        swapped = swap_h(own)
        below_own, above_own = up_z(own), down_z(own)
        below_swapped, above_swapped = up_z(swapped), down_z(swapped)
        arrivals = [
            (own, at_z(0)[:1]),
            (swapped, at_z(0)[1:]),
            (below_own, at_z(3)[:1]),
            (above_own, at_z(1)[:1]),
            (below_swapped, at_z(3)[1:]),
            (above_swapped, at_z(1)[1:]),
        ]
        far_own, far_swapped = up_z(below_own), down_z(above_swapped)
    else:
        swapped = swap_h(after(own, start[0]))
        pair = jnp.concatenate([own, swapped], 0)
        pair = after(pair, *start[1:])
        below, above = up_z(pair), down_z(pair)
        arrivals = [(pair, at_z(0)), (below, at_z(3)), (above, at_z(1))]
        far_own, far_swapped = up_z(below[:ROWS]), down_z(above[ROWS:])
    arrivals += [(far_own, at_z(2)[:1]), (far_swapped, at_z(2)[1:])]
    return arrivals, (swapped, far_own, far_swapped)


def gather_weights(own, swapped, start):
    pair = after(jnp.concatenate([own, swapped], 0), *start)
    below, above = up_y(pair), down_y(pair)
    far_own, far_swapped = up_y(below[:ROWS]), down_y(above[ROWS:])
    mine = jnp.concatenate([pair, above, far_own, far_swapped, below], 0)
    return (mine, swap_core(mine)), (far_own, far_swapped)


def weight_places(x, y, core):
    places = []
    for c in (core, 1 - core):
        for step in range(4):
            yy = lax.rem(y + step, 4)
            places += [(x * 4 + yy) * 2 + c, ((1 - x) * 4 + yy) * 2 + c]
    return jnp.stack(places).astype(jnp.int32)


def load_weights(places, mine, other, held, columns, sems):
    copies = []
    for s, source in enumerate((mine, other)):
        for i in range(8):
            start = pl.multiple_of(places[s * 8 + i] * ROWS, ROWS)
            copies.append(
                pltpu.make_async_copy(
                    source.at[pl.ds(i * ROWS, ROWS)], held.at[pl.ds(start, ROWS), columns], sems.at[s * 8 + i]
                )
            )
    for copy in copies:
        copy.start()
    return copies


def scatter_rows(parts, start):
    h = lax.rem(lax.axis_index("tensor"), 2)
    far = after(parts[0], *start)
    from_below, from_above = up_z(far[:ROWS]), down_z(far[ROWS:])
    none = jnp.zeros((ROWS, D), F32)
    up = (parts[1].astype(F32) + jnp.concatenate([from_below.astype(F32), none], 0)).astype(BF)
    down = (parts[2].astype(F32) + jnp.concatenate([none, from_above.astype(F32)], 0)).astype(BF)
    got_up, got_down = up_z(up), down_z(down)
    total = (parts[3].astype(F32) + got_up.astype(F32) + got_down.astype(F32)).reshape(2, ROWS, D)
    got = swap_h(at(total, 1 - h, 0).astype(BF))
    return at(total, h, 0) + got.astype(F32), (got_up, got_down)


def scatter_weights(other, mine, start):
    x = lax.axis_index("dp") // 8
    columns = mine.shape[2]
    got = swap_core(other)
    sums = mine.astype(F32) + got.astype(F32)
    far = after(sums[0].astype(BF), *start)
    from_below, from_above = up_y(far[:ROWS]), down_y(far[ROWS:])
    none = jnp.zeros((ROWS, columns), F32)
    up = (sums[1] + jnp.concatenate([from_below.astype(F32), none], 0)).astype(BF)
    down = (sums[2] + jnp.concatenate([none, from_above.astype(F32)], 0)).astype(BF)
    got_up, got_down = up_y(up), down_y(down)
    total = (sums[3] + got_up.astype(F32) + got_down.astype(F32)).reshape(2, ROWS, columns)
    got = swap_x(at(total, 1 - x, 0).astype(BF))
    return at(total, x, 0) + got.astype(F32), (got_up, got_down)


def sum_over(v, axis, perms):
    for perm in perms:
        v = v + lax.ppermute(v, axis, perm)
    return v


def rotary_tables():
    half = ROT // 2
    position = jnp.arange(LEN, dtype=F32)
    frequency = 10000.0 ** (-jnp.arange(half, dtype=F32) * 2.0 / ROT)
    angle = position[:, None] * frequency[None, :]
    cosine, sine = jnp.cos(angle), jnp.sin(angle)
    ones = jnp.ones((LEN, HD - ROT), F32)
    zeros = jnp.zeros((LEN, HD - ROT), F32)
    none = jnp.zeros((LEN, half), F32)
    same = jnp.concatenate([cosine, cosine, ones] * 2, 1)
    ahead = jnp.concatenate([-sine, none, zeros] * 2, 1)
    behind = jnp.concatenate([none, sine, zeros] * 2, 1)
    return same, ahead, behind


def rotated(values, same, ahead, behind, sign):
    wide = [jnp.concatenate([t, t], 1) for t in (same, ahead, behind)]
    half = ROT // 2
    return values * wide[0] + sign * (
        pltpu.roll(values, HC - half, 1) * wide[1] + pltpu.roll(values, half, 1) * wide[2]
    )


def qkv_kernel(places, rows, mine, other, bias, same, ahead, behind, queries, keys, values, held, sems):
    @pl.when(pl.program_id(0) == 0)
    def _():
        for copy in load_weights(places, mine, other, held, slice(None), sems):
            copy.wait()

    pre = jnp.dot(rows[...], held[...], preferred_element_type=F32)
    tables = same[...], ahead[...], behind[...]
    queries[...] = rotated(pre[:, :HC] + bias[0:1], *tables, 1.0).astype(BF)
    keys[...] = rotated(pre[:, HC : 2 * HC] + bias[1:2], *tables, 1.0).astype(BF)
    values[...] = (pre[:, 2 * HC :] + bias[2:3]).astype(BF)


def row_spec(columns, block=256):
    return pl.BlockSpec((block, columns), lambda i, *_: (i, 0))


def qkv_call(places, normed, weights, bias, tables):
    return pl.pallas_call(
        qkv_kernel,
        grid=(4,),
        out_shape=[jax.ShapeDtypeStruct((LEN, HC), BF)] * 3,
        in_specs=[SMEM, row_spec(D), ANY, ANY, whole((3, HC))] + [row_spec(2 * HD)] * 3,
        out_specs=[row_spec(HC)] * 3,
        scratch_shapes=[pltpu.VMEM((D, 3 * HC), BF), pltpu.SemaphoreType.DMA((16,))],
        compiler_params=params(),
        cost_estimate=cost(2 * LEN * D * 3 * HC, 2 * (LEN * D + D * 3 * HC + 3 * LEN * HC)),
    )(places, normed, *weights, bias, *tables)


ROOT = 0.7978845608028654
CUBIC = 0.044715


def hidden_kernel(places, rows, mine, other, bias, activated, slope, held, sems):
    @pl.when(pl.program_id(0) == 0)
    def _():
        for copy in load_weights(places, mine, other, held, slice(None), sems):
            copy.wait()

    hidden = jnp.dot(rows[...], held[...], preferred_element_type=F32) + bias[...]
    square = hidden * hidden
    bent = jnp.tanh(ROOT * (hidden + CUBIC * (square * hidden)))
    half = 0.5 * (1.0 + bent)
    activated[...] = (hidden * half).astype(BF)
    slope[...] = half + (0.5 * ROOT) * hidden * (1.0 - bent * bent) * (1.0 + (3.0 * CUBIC) * square)


def hidden_call(places, normed, weights, bias):
    return pl.pallas_call(
        hidden_kernel,
        grid=(4,),
        out_shape=[jax.ShapeDtypeStruct((LEN, FC), BF), jax.ShapeDtypeStruct((LEN, FC), F32)],
        in_specs=[SMEM, row_spec(D), ANY, ANY, whole((1, FC))],
        out_specs=[row_spec(FC)] * 2,
        scratch_shapes=[pltpu.VMEM((D, FC), BF), pltpu.SemaphoreType.DMA((16,))],
        compiler_params=params(),
        cost_estimate=cost(2 * LEN * D * FC, 2 * (LEN * D + D * FC + 3 * LEN * FC), LEN * FC),
    )(places, normed, *weights, bias.reshape(1, FC))


def out_kernel(groups, places, attended, activated, mine, other, parts, held, sems):
    @pl.when(pl.program_id(0) == 0)
    def _():
        for copy in load_weights(places, mine, other, held, slice(None), sems):
            copy.wait()

    rows = jnp.concatenate([attended[...], activated[...]], 1)
    parts[0] = nt(rows, held[...]).astype(BF)


def group_spec(columns):
    return pl.BlockSpec((256, columns), lambda i, groups: (groups[i], 0))


PART_SPEC = pl.BlockSpec((1, 256, D), lambda i, groups: (i, 0, 0))


def out_call(groups, places, attended, activated, weights):
    return pl.pallas_call(
        out_kernel,
        grid_spec=pltpu.PrefetchScalarGridSpec(
            num_scalar_prefetch=1,
            grid=(4,),
            in_specs=[SMEM, group_spec(HC), group_spec(FC), ANY, ANY],
            out_specs=PART_SPEC,
            scratch_shapes=[pltpu.VMEM((D, HC + FC), BF), pltpu.SemaphoreType.DMA((16,))],
        ),
        out_shape=jax.ShapeDtypeStruct((4, 256, D), BF),
        compiler_params=params(),
        cost_estimate=cost(2 * LEN * D * (HC + FC), 2 * (LEN * D + D * (HC + FC) + LEN * (HC + FC))),
    )(groups, places, attended, activated, *weights)


def grad_kernel(places, backs, slope, mine, other, grad_attended, grad_hidden, sums, held, sems):
    @pl.when(pl.program_id(0) == 0)
    def _():
        for copy in load_weights(places, mine, other, held, slice(None), sems):
            copy.wait()
        sums[...] = jnp.zeros_like(sums)

    both = jnp.dot(backs[...], held[...], preferred_element_type=F32)
    grad_attended[...] = both[:, :HC].astype(BF)
    grad = (both[:, HC:] * slope[...]).astype(BF)
    grad_hidden[...] = grad
    sums[...] += jnp.sum(grad.astype(F32), 0, keepdims=True)


def grad_call(places, backs, slope, weights):
    return pl.pallas_call(
        grad_kernel,
        grid=(4,),
        out_shape=[
            jax.ShapeDtypeStruct((LEN, HC), BF),
            jax.ShapeDtypeStruct((LEN, FC), BF),
            jax.ShapeDtypeStruct((1, FC), F32),
        ],
        in_specs=[SMEM, row_spec(D), row_spec(FC), ANY, ANY],
        out_specs=[row_spec(HC), row_spec(FC), whole((1, FC))],
        scratch_shapes=[pltpu.VMEM((D, HC + FC), BF), pltpu.SemaphoreType.DMA((16,))],
        compiler_params=params(),
        cost_estimate=cost(2 * LEN * D * (HC + FC), 2 * (LEN * D + D * (HC + FC) + 4 * LEN * FC)),
    )(places, backs, slope, *weights)


def normed_kernel(
    groups, places, projected, hidden, rows, stats, mine, other, mine2, other2, parts, sums, held, sems, sems2
):
    @pl.when(pl.program_id(0) == 0)
    def _():
        copies = load_weights(places, mine, other, held, slice(0, 3 * HC), sems)
        copies += load_weights(places, mine2, other2, held, slice(3 * HC, 3 * HC + FC), sems2)
        for copy in copies:
            copy.wait()
        sums[...] = jnp.zeros_like(sums)

    grads = jnp.concatenate([projected[...], hidden[...]], 1)
    grad = nt(grads, held[...])
    parts[0] = grad.astype(BF)
    standard = (rows[...].astype(F32) - stats[:, 0:1]) * stats[:, 64:65]
    sums[0:1, :] += jnp.sum(grad * standard, 0, keepdims=True)
    sums[1:2, :] += jnp.sum(grad, 0, keepdims=True)


def normed_call(groups, places, projected, hidden, rows, stats, weights, weights2):
    wide = 3 * HC + FC
    return pl.pallas_call(
        normed_kernel,
        grid_spec=pltpu.PrefetchScalarGridSpec(
            num_scalar_prefetch=1,
            grid=(4,),
            in_specs=[SMEM, group_spec(3 * HC), group_spec(FC), group_spec(D), group_spec(128)] + [ANY] * 4,
            out_specs=[PART_SPEC, whole((2, D))],
            scratch_shapes=[
                pltpu.VMEM((D, wide), BF),
                pltpu.SemaphoreType.DMA((16,)),
                pltpu.SemaphoreType.DMA((16,)),
            ],
        ),
        out_shape=[jax.ShapeDtypeStruct((4, 256, D), BF), jax.ShapeDtypeStruct((2, D), F32)],
        compiler_params=params(),
        cost_estimate=cost(2 * LEN * D * wide, 2 * (2 * LEN * D + D * wide + LEN * wide)),
    )(groups, places, projected, hidden, rows, stats, *weights, *weights2)


def weight_kernel(places, a, b, c, d, *refs):
    other, mine = refs[-2:]
    step = pl.program_id(0)
    left = jnp.concatenate([a[...], b[...], c[...], d[...]], 0)
    right = jnp.concatenate([r[...] for r in refs[:-2]], 1)
    term = jnp.dot(left, right, preferred_element_type=F32).astype(BF)

    @pl.when(step < 2)
    def _():
        other[...] = term.reshape(2, 256, term.shape[1])

    @pl.when(step >= 2)
    def _():
        mine[...] = term.reshape(2, 256, term.shape[1])


def weight_call(places, left_t, *right):
    columns = sum(r.shape[1] for r in right)

    def left_spec(j):
        return pl.BlockSpec((ROWS, LEN), lambda i, places: (places[4 * i + j], 0))

    return pl.pallas_call(
        weight_kernel,
        grid_spec=pltpu.PrefetchScalarGridSpec(
            num_scalar_prefetch=1,
            grid=(4,),
            in_specs=[left_spec(j) for j in range(4)] + [whole(r.shape) for r in right],
            out_specs=[
                pl.BlockSpec((2, 256, columns), lambda i, places: (jnp.minimum(i, 1), 0, 0)),
                pl.BlockSpec((2, 256, columns), lambda i, places: (jnp.maximum(i - 2, 0), 0, 0)),
            ],
        ),
        out_shape=[jax.ShapeDtypeStruct((4, 256, columns), BF)] * 2,
        compiler_params=params(),
        cost_estimate=cost(2 * LEN * D * columns, 2 * (LEN * D + D * columns + LEN * columns)),
    )(places, *([left_t] * 4), *right)


def nt(left, right):
    return lax.dot_general(left, right, (((1,), (1,)), ((), ())), preferred_element_type=F32)


def nn(left, right):
    return lax.dot_general(left, right, (((1,), (0,)), ((), ())), preferred_element_type=F32)


def causal(block):
    key = lax.broadcasted_iota(jnp.int32, (BQ, BQ), 0)
    query = lax.broadcasted_iota(jnp.int32, (BQ, BQ), 1)
    return jnp.where(key <= query, block, -1e9)


def forward_kernel(queries, keys, values, attended, logsum, values_t, out_t, scores):
    values_t[...] = values[...].T
    out_t[...] = jnp.zeros_like(out_t)
    logsum[...] = jnp.zeros_like(logsum)
    lane = lax.broadcasted_iota(jnp.int32, (BQ, HC), 1) // HD
    row = lax.broadcasted_iota(jnp.int32, (HC, BQ), 0) // HD
    stat_row = lax.broadcasted_iota(jnp.int32, (8, BQ), 0)

    def one_head(head, carry):
        for q in range(LEN // BQ):
            here = slice(q * BQ, (q + 1) * BQ)
            query = jnp.where(lane == head, queries[here, :], jnp.zeros((), BF))
            largest = None
            for k in range(q + 1):
                block = nt(keys[k * BQ : (k + 1) * BQ, :], query) * SCALE
                if k == q:
                    block = causal(block)
                scores[k * BQ : (k + 1) * BQ, :] = block
                top = jnp.max(block, 0, keepdims=True)
                largest = top if largest is None else jnp.maximum(largest, top)
            total = jnp.zeros((1, BQ), F32)
            for k in range(q + 1):
                powers = jnp.exp(scores[k * BQ : (k + 1) * BQ, :] - largest)
                scores[k * BQ : (k + 1) * BQ, :] = powers
                total = total + jnp.sum(powers, 0, keepdims=True)
            scale = 1.0 / total
            found = jnp.zeros((HC, BQ), F32)
            for k in range(q + 1):
                probs = (scores[k * BQ : (k + 1) * BQ, :] * scale).astype(BF)
                found = found + nn(values_t[:, k * BQ : (k + 1) * BQ], probs)
            out_t[:, here] = jnp.where(row == head, found, out_t[:, here])
            logsum[:, here] = jnp.where(stat_row == head, largest + jnp.log(total), logsum[:, here])
        return carry

    lax.fori_loop(0, HEADS, one_head, 0)
    attended[...] = out_t[...].T.astype(BF)


def forward_call(queries, keys, values):
    return pl.pallas_call(
        forward_kernel,
        out_shape=[jax.ShapeDtypeStruct((LEN, HC), BF), jax.ShapeDtypeStruct((8, LEN), F32)],
        scratch_shapes=[
            pltpu.VMEM((HC, LEN), BF),
            pltpu.VMEM((HC, LEN), F32),
            pltpu.VMEM((LEN, BQ), F32),
        ],
        compiler_params=pltpu.CompilerParams(vmem_limit_bytes=VMEM_LIMIT),
        cost_estimate=pl.CostEstimate(flops=6 * 10**9, bytes_accessed=4 * LEN * HC * 2, transcendentals=4 * LEN * LEN // 2),
    )(queries, keys, values)


def backward_kernel(
    queries, keys, values, grads, logsum, same, ahead, behind, out, sums, keys_t, query_grads, key_grads, value_grads, probs_all, back_all
):
    keys_t[...] = keys[...].T
    query_grads[...] = jnp.zeros_like(query_grads)
    key_grads[...] = jnp.zeros_like(key_grads)
    value_grads[...] = jnp.zeros_like(value_grads)
    lane = lax.broadcasted_iota(jnp.int32, (BQ, HC), 1) // HD
    row = lax.broadcasted_iota(jnp.int32, (HC, BQ), 0) // HD

    def one_head(head, carry):
        for q in range(LEN // BQ):
            here = slice(q * BQ, (q + 1) * BQ)
            query = jnp.where(lane == head, queries[here, :], jnp.zeros((), BF))
            grad = jnp.where(lane == head, grads[here, :], jnp.zeros((), BF))
            stat_row = lax.broadcasted_iota(jnp.int32, (8, BQ), 0)
            base = jnp.sum(jnp.where(stat_row == head, logsum[:, here], 0.0), 0, keepdims=True)
            dots = jnp.zeros((1, BQ), F32)
            for k in range(q + 1):
                there = slice(k * BQ, (k + 1) * BQ)
                block = nt(keys[there, :], query) * SCALE
                if k == q:
                    block = causal(block)
                probs = jnp.exp(block - base)
                back = nt(values[there, :], grad)
                dots = dots + jnp.sum(back * probs, 0, keepdims=True)
                probs_all[there, :] = probs
                back_all[there, :] = back
                value_grads[there, :] += nn(probs.astype(BF), grad)
            found = jnp.zeros((HC, BQ), F32)
            for k in range(q + 1):
                there = slice(k * BQ, (k + 1) * BQ)
                score_grads = (probs_all[there, :] * (back_all[there, :] - dots)).astype(BF)
                key_grads[there, :] += nn(score_grads, query)
                found = found + nn(keys_t[:, there], score_grads)
            query_grads[:, here] = jnp.where(row == head, found, query_grads[:, here])
        return carry

    lax.fori_loop(0, HEADS, one_head, 0)
    tables = same[...], ahead[...], behind[...]
    parts = (
        rotated(query_grads[...].T * SCALE, *tables, -1.0),
        rotated(key_grads[...] * SCALE, *tables, -1.0),
        value_grads[...],
    )
    for j, part in enumerate(parts):
        low = part.astype(BF)
        out[:, j * HC : (j + 1) * HC] = low
        sums[:, j * HC : (j + 1) * HC] = jnp.sum(low.astype(F32), 0, keepdims=True)


def backward_call(queries, keys, values, grads, logsum, tables):
    return pl.pallas_call(
        backward_kernel,
        out_shape=[jax.ShapeDtypeStruct((LEN, 3 * HC), BF), jax.ShapeDtypeStruct((1, 3 * HC), F32)],
        scratch_shapes=[
            pltpu.VMEM((HC, LEN), BF),
            pltpu.VMEM((HC, LEN), F32),
            pltpu.VMEM((LEN, HC), F32),
            pltpu.VMEM((LEN, HC), F32),
            pltpu.VMEM((LEN, BQ), F32),
            pltpu.VMEM((LEN, BQ), F32),
        ],
        compiler_params=pltpu.CompilerParams(vmem_limit_bytes=VMEM_LIMIT),
        cost_estimate=pl.CostEstimate(flops=12 * 10**9, bytes_accessed=8 * LEN * HC * 2, transcendentals=4 * LEN * LEN // 2),
    )(queries, keys, values, grads, logsum, *tables)


def adamw(param, grad, first, second, rate, decay):
    first_new = BETA_ONE * first + (1.0 - BETA_ONE) * grad
    second_new = BETA_TWO * second + (1.0 - BETA_TWO) * grad * grad
    ratio = (
        first_new
        / (1.0 - BETA_ONE**STEP)
        / (jnp.sqrt(second_new / (1.0 - BETA_TWO**STEP)) + ADAM_EPSILON)
    )
    return (grad, first_new, second_new, param - rate * (ratio + decay * param))


def side_by_side(stack):
    return jnp.concatenate([stack[j] for j in range(stack.shape[0])], 1)


def per_device(
    tokens,
    cotangent,
    attn_weight,
    mlp_weight,
    qkv_bias,
    fc1_bias,
    vectors,
    attn_first,
    mlp_first,
    qkv_first,
    fc1_first,
    vector_first,
    attn_second,
    mlp_second,
    qkv_second,
    fc1_second,
    vector_second,
):
    dp = lax.axis_index("dp")
    tensor = lax.axis_index("tensor")
    x, y, core = dp // 8, lax.rem(dp // 2, 4), lax.rem(dp, 2)
    z, h = tensor // 2, lax.rem(tensor, 2)
    places = weight_places(x, y, core)
    groups = jnp.stack([lax.rem(z + step, 4) for step in (2, 1, 3, 0)]).astype(jnp.int32)
    grad_places = jnp.stack(
        [
            (xx * 4 + lax.rem(y + step, 4)) * 2 + c
            for c in (1 - core, core)
            for step in (2, 1, 3, 0)
            for xx in (0, 1)
        ]
    ).astype(jnp.int32)

    qkv_own = side_by_side(attn_weight[:3].astype(BF))
    rest_own = jnp.concatenate([mlp_weight[0], attn_weight[3], mlp_weight[1]], 1).astype(BF)
    qkv_swapped = swap_x(qkv_own)
    arrivals, marks = gather_pairs(tokens, z, h, None)
    rest_swapped = swap_x(after(rest_own, qkv_swapped))
    qkv_full, qkv_marks = gather_weights(qkv_own, qkv_swapped, ())
    fc1_full, fc1_marks = gather_weights(rest_own[:, :FC], rest_swapped[:, :FC], qkv_marks)
    back_full, back_marks = gather_weights(rest_own[:, FC:], rest_swapped[:, FC:], fc1_marks)
    back_arrivals, back_row_marks = gather_pairs(cotangent, z, h, (rest_swapped, *marks[1:]))
    tables = rotary_tables()

    normed, normed_t, rows, stats = place_all(norm_kernel, NORM_OUTS, arrivals, (vectors,))
    queries, keys, values = qkv_call(places, normed, qkv_full, qkv_bias, tables)
    attended, logsum = forward_call(queries, keys, values)
    activated, slope = hidden_call(places, normed, fc1_full, fc1_bias)
    out_parts = out_call(groups, places, attended, activated, back_full)
    summed, out_marks = scatter_rows(out_parts, back_row_marks[1:])
    local = tokens.astype(F32)
    out = (local + summed + vectors[2] + vectors[3]).astype(BF)

    backs, backs_t = place_all(back_kernel, BACK_OUTS, back_arrivals)
    grad_attended, grad_hidden, hidden_sums = grad_call(places, backs, slope, back_full)
    back_terms = weight_call(grad_places, backs_t, attended, activated)
    back_grad, back_grad_marks = scatter_weights(*back_terms, ())
    projected, projected_sums = backward_call(queries, keys, values, grad_attended, logsum, tables)
    normed_parts, normed_sums = normed_call(
        groups, places, projected, grad_hidden, rows, stats, qkv_full, fc1_full
    )
    grad_normed, normed_marks = scatter_rows(normed_parts, out_marks)
    fc1_terms = weight_call(grad_places, normed_t, grad_hidden)
    fc1_grad_w, fc1_grad_marks = scatter_weights(*fc1_terms, back_grad_marks)
    qkv_terms = weight_call(grad_places, normed_t, projected)
    qkv_grad_w, qkv_grad_marks = scatter_weights(*qkv_terms, fc1_grad_marks)

    local_centred = local - jnp.mean(local, -1, keepdims=True)
    local_inverse = lax.rsqrt(jnp.mean(local_centred * local_centred, -1, keepdims=True) + EPSILON)
    local_standard = local_centred * local_inverse
    back_local = cotangent.astype(F32)
    grad_standard = grad_normed * vectors[0]
    input_grad = back_local + local_inverse * (
        grad_standard
        - jnp.mean(grad_standard, -1, keepdims=True)
        - local_standard * jnp.mean(grad_standard * local_standard, -1, keepdims=True)
    )

    small = jnp.concatenate(
        [normed_sums.reshape(-1), jnp.sum(back_local, 0), projected_sums.reshape(-1), hidden_sums.reshape(-1)]
    ).reshape(-1, 128)
    small = sum_over(small, "dp", (CORE_SWAP, X_SWAP, Y_FLIP, Y_FAR))
    bias_sum = small[3 * D // 128 :].reshape(-1)
    vector_sum = sum_over(small[: 3 * D // 128], "tensor", (H_SWAP, Z_FLIP, Z_FAR)).reshape(3, D)
    vector_grad = jnp.concatenate([vector_sum, vector_sum[2:3]], 0)

    attn_grad = jnp.stack(
        [qkv_grad_w[:, :HC], qkv_grad_w[:, HC : 2 * HC], qkv_grad_w[:, 2 * HC :], back_grad[:, :HC]]
    )
    mlp_grad = jnp.stack([fc1_grad_w, back_grad[:, HC:]])
    qkv_grad = bias_sum[: 3 * HC].reshape(3, HC)
    fc1_grad = bias_sum[3 * HC :]
    attn_out = adamw(attn_weight, attn_grad, attn_first, attn_second, 0.04, 0.1)
    mlp_out = adamw(mlp_weight, mlp_grad, mlp_first, mlp_second, 0.04, 0.1)
    qkv_out = adamw(qkv_bias, qkv_grad, qkv_first, qkv_second, 0.3, 0.0)
    fc1_out = adamw(fc1_bias, fc1_grad, fc1_first, fc1_second, 0.3, 0.0)
    vector_out = adamw(vectors, vector_grad, vector_first, vector_second, 0.2, 0.0)
    return (out, input_grad, *attn_out, *mlp_out, *qkv_out, *fc1_out, *vector_out)


def solution(mesh):
    rows = P(("dp", "tensor"), None)
    weight = P(None, "dp", "tensor")
    qkv = P(None, "tensor")
    fc1 = P("tensor")
    return jax.shard_map(
        per_device,
        mesh=mesh,
        in_specs=(rows, rows, weight, weight, qkv, fc1, P()) + (weight, weight, qkv, fc1, P()) * 2,
        out_specs=(rows, rows) + (weight,) * 8 + (qkv,) * 4 + (fc1,) * 4 + (P(),) * 4,
        check_vma=False,
    )
```

```python
import functools

import jax
import jax.numpy as jnp
import numpy as np
from jax import lax
from jax.experimental import pallas as pl
from jax.experimental.pallas import tpu as pltpu
from jax.sharding import PartitionSpec as P

D = 2048
HD = 64
ROT = 32
LEN = 1024
STEP = 10
HEADS = 4
HC = HEADS * HD
FC = 1024
ROWS = 128
BQ = 256

EPSILON = 1e-05
SCALE = 0.125
BETA_ONE = 0.9
BETA_TWO = 0.999
ADAM_EPSILON = 1e-08
BF = jnp.bfloat16
LIMITS = dict(assemble=12, qkv=12, hidden=16, out=15, grad=16, normed=22, weight=20, forward=14, backward=18)
TIMES = dict(qkv=4.0, hidden=6.0, out=6.0, grad=5.5, normed=9.0, weight=5.0, forward=5.0, backward=8.0)
DECLARED = 0.35
F32 = jnp.float32


def dp_perm(move):
    pairs = []
    for x in range(2):
        for y in range(4):
            for c in range(2):
                nx, ny, nc = move(x, y, c)
                pairs.append(((x * 4 + y) * 2 + c, (nx * 4 + ny % 4) * 2 + nc))
    return pairs


def tensor_perm(move):
    pairs = []
    for z in range(4):
        for h in range(2):
            nz, nh = move(z, h)
            pairs.append((z * 2 + h, (nz % 4) * 2 + nh))
    return pairs


Y_UP = dp_perm(lambda x, y, c: (x, y + 1, c))
Y_DOWN = dp_perm(lambda x, y, c: (x, y - 1, c))
X_SWAP = dp_perm(lambda x, y, c: (1 - x, y, c))
CORE_SWAP = dp_perm(lambda x, y, c: (x, y, 1 - c))
Z_UP = tensor_perm(lambda z, h: (z + 1, h))
Z_DOWN = tensor_perm(lambda z, h: (z - 1, h))
Y_FAR = dp_perm(lambda x, y, c: (x, y + 2, c))
Z_FAR = tensor_perm(lambda z, h: (z + 2, h))
H_SWAP = tensor_perm(lambda z, h: (z, 1 - h))


def at(array, index, axis):
    return lax.dynamic_index_in_dim(array, index, axis, keepdims=False)


def after(value, *others):
    return lax.optimization_barrier((value, *others))[0]


def together(*values):
    return lax.optimization_barrier(values)


def up_z(v):
    return lax.ppermute(v, "tensor", Z_UP)


def down_z(v):
    return lax.ppermute(v, "tensor", Z_DOWN)


def swap_h(v):
    return lax.ppermute(v, "tensor", H_SWAP)


def up_y(v):
    return lax.ppermute(v, "dp", Y_UP)


def down_y(v):
    return lax.ppermute(v, "dp", Y_DOWN)


def swap_x(v):
    return lax.ppermute(v, "dp", X_SWAP)


def swap_core(v):
    return lax.ppermute(v, "dp", CORE_SWAP)


SMEM = pl.BlockSpec(memory_space=pltpu.SMEM)
VMEM = pl.BlockSpec(memory_space=pltpu.VMEM)


def call(kernel, out_shape, mebibytes, in_specs=None, scratch_shapes=(), us=1.0):
    def run(*args):
        return pl.pallas_call(
            kernel,
            out_shape=out_shape,
            out_specs=jax.tree.map(lambda _: VMEM, out_shape),
            in_specs=in_specs or [VMEM] * len(args),
            scratch_shapes=scratch_shapes,
            compiler_params=pltpu.CompilerParams(vmem_limit_bytes=mebibytes * 1024 * 1024),
            cost_estimate=pl.CostEstimate(
                flops=int(us * DECLARED * 1.1e9), bytes_accessed=1000, transcendentals=0
            ),
        )(*args)

    return run


def shape(rows, columns, dtype=BF):
    return jax.ShapeDtypeStruct((rows, columns), dtype)


def normalized(block, vectors, normed, stats, at):
    inputs = block.astype(F32)
    mean = jnp.mean(inputs, -1, keepdims=True)
    centred = inputs - mean
    inverse = lax.rsqrt(jnp.mean(centred * centred, -1, keepdims=True) + EPSILON)
    normed[at, :] = (centred * inverse * vectors[0:1, :] + vectors[1:2, :]).astype(BF)
    lane = lax.broadcasted_iota(jnp.int32, (ROWS, 128), 1)
    stats[at, :] = jnp.where(lane < 64, mean, inverse)


def norm_first_kernel(own, swapped, below, above, vectors, normed, stats):
    for i, block in enumerate((own, swapped, below, above)):
        normalized(block[...], vectors, normed, stats, slice(i * ROWS, (i + 1) * ROWS))


def norm_second_kernel(below, above, vectors, normed, stats):
    far = jnp.concatenate([below[ROWS:, :], above[ROWS:, :]], 0)
    for i, block in enumerate((below[:ROWS, :], above[:ROWS, :], far)):
        normalized(block, vectors, normed, stats, slice(i * ROWS, (i + 1) * ROWS))


def norm_last_kernel(places, first, second, vectors, normed_a, stats_a, normed_b, stats_b, normed, stats):
    at = [pl.ds(pl.multiple_of(places[i] * ROWS, ROWS), ROWS) for i in range(8)]
    normalized(jnp.concatenate([first[...], second[...]], 0), vectors, normed, stats, at[7])
    for i in range(7):
        held, held_stats, k = (normed_a, stats_a, i) if i < 4 else (normed_b, stats_b, i - 4)
        normed[at[i], :] = held[k * ROWS : (k + 1) * ROWS, :]
        stats[at[i], :] = held_stats[k * ROWS : (k + 1) * ROWS, :]


def rows_kernel(places, own, swapped, below, above, below_mid, above_mid, first, second, rows):
    far = jnp.concatenate([below_mid[ROWS:, :], above_mid[ROWS:, :]], 0)
    last = jnp.concatenate([first[...], second[...]], 0)
    blocks = (own[...], swapped[...], below[...], above[...], below_mid[:ROWS, :], above_mid[:ROWS, :], far, last)
    for i, block in enumerate(blocks):
        rows[pl.ds(pl.multiple_of(places[i] * ROWS, ROWS), ROWS), :] = block


def backs_kernel(places, pair, below, above, far, far_swapped, out):
    blocks = [ref[k * ROWS : (k + 1) * ROWS, :] for ref in (pair, below, above) for k in range(2)]
    blocks += [far[...], far_swapped[...]]
    for i, block in enumerate(blocks):
        out[pl.ds(pl.multiple_of(places[i] * ROWS, ROWS), ROWS), :] = block


def place_of(z, h, step):
    base = lax.rem(z + step, 4) * 2
    return base + h, base + 1 - h


def weight_places(x, y, core):
    places = []
    for c in (core, 1 - core):
        for step in range(4):
            yy = lax.rem(y + step, 4)
            places += [(x * 4 + yy) * 2 + c, ((1 - x) * 4 + yy) * 2 + c]
    return jnp.stack(places).astype(jnp.int32)


def beside(wide, rows):
    middle = rows.shape[1] // 2
    return jnp.concatenate([wide, jnp.concatenate([rows[:, :middle], rows[:, middle:]], 0)], 1)


def apart(message, columns):
    return jnp.concatenate([message[:ROWS, columns:], message[ROWS:, columns:]], 1)


def whole_ring(pair, above, far, far_swapped, below):
    return jnp.concatenate([pair, above, far, far_swapped, below], 0)


def near_kernel(above, below, from_below, from_above, up, down):
    up[:ROWS, :] = (above[:ROWS, :].astype(F32) + from_below[...].astype(F32)).astype(BF)
    up[ROWS:, :] = above[ROWS:, :]
    down[:ROWS, :] = below[:ROWS, :]
    down[ROWS:, :] = (below[ROWS:, :].astype(F32) + from_above[...].astype(F32)).astype(BF)


def near(above, below, from_below, from_above):
    columns = above.shape[1]
    return call(near_kernel, [shape(256, columns)] * 2, 8)(above, below, from_below, from_above)


def last_kernel(own, here, got_up, got_down, kept, sent):
    for out, which in ((kept, own[0]), (sent, 1 - own[0])):
        at = pl.ds(pl.multiple_of(which * ROWS, ROWS), ROWS)
        total = here[at, :].astype(F32) + got_up[at, :].astype(F32) + got_down[at, :].astype(F32)
        out[...] = total.astype(out.dtype)


def last(own, here, got_up, got_down):
    columns = here.shape[1]
    return call(
        last_kernel, [shape(ROWS, columns, F32), shape(ROWS, columns)], 8, [SMEM] + [VMEM] * 3
    )(own.reshape(1).astype(jnp.int32), here, got_up, got_down)


def summed_part(mine, got, k):
    return (mine[k].astype(F32) + got[k].astype(F32)).astype(BF)


def rotary_tables():
    half = ROT // 2
    position = np.arange(LEN, dtype=np.float32)
    frequency = np.float32(10000.0) ** (-np.arange(half, dtype=np.float32) * np.float32(2.0 / ROT))
    angle = (position[:, None] * frequency[None, :].astype(np.float32)).astype(np.float32)
    cosine, sine = np.cos(angle), np.sin(angle)
    rest = np.ones((LEN, HD - ROT), np.float32)
    none = np.zeros((LEN, half), np.float32)
    same = np.concatenate([cosine, cosine, rest] * 2, 1)
    ahead = np.concatenate([-sine, none, 0 * rest] * 2, 1)
    behind = np.concatenate([none, sine, 0 * rest] * 2, 1)
    return jnp.asarray(np.concatenate([same, ahead, behind], 1).astype(np.float32))


def rotated(values, tables, sign):
    wide = [jnp.concatenate([tables[:, j * 128 : (j + 1) * 128]] * 2, 1) for j in range(3)]
    half = ROT // 2
    return values * wide[0] + sign * (
        pltpu.roll(values, HC - half, 1) * wide[1] + pltpu.roll(values, half, 1) * wide[2]
    )


WIDE = 256


def assemble_kernel(places, mine, other, out):
    for s, source in enumerate((mine, other)):
        for i in range(8):
            start = pl.multiple_of(places[s * 8 + i] * ROWS, ROWS)
            out[pl.ds(start, ROWS), :] = source[i * ROWS : (i + 1) * ROWS, :]


def assembled(places, mine, other):
    return call(assemble_kernel, shape(D, mine.shape[1]), LIMITS["assemble"], [SMEM, VMEM, VMEM], us=2.0)(
        places, mine, other
    )


def qkv_kernel(rows, weights, bias, tables, heads):
    for j in range(3):
        part = slice(j * HC, (j + 1) * HC)
        pre = nn(rows[...], weights[:, part]) + bias[j : j + 1]
        heads[:, part] = (rotated(pre, tables, 1.0) if j < 2 else pre).astype(BF)


def qkv_call(normed, weights, bias, tables):
    return call(qkv_kernel, shape(LEN, 3 * HC), LIMITS["qkv"], us=TIMES["qkv"])(normed, weights, bias, tables)


ROOT = 0.7978845608028654
CUBIC = 0.044715


def hidden_kernel(rows, weights, bias, activated, slope):
    for j in range(FC // WIDE):
        part = slice(j * WIDE, (j + 1) * WIDE)
        hidden = nn(rows[...], weights[:, part]) + bias[:, part]
        square = hidden * hidden
        bent = jnp.tanh(ROOT * (hidden + CUBIC * (square * hidden)))
        half = 0.5 * (1.0 + bent)
        activated[:, part] = (hidden * half).astype(BF)
        slope[:, part] = (
            half + (0.5 * ROOT) * hidden * (1.0 - bent * bent) * (1.0 + (3.0 * CUBIC) * square)
        ).astype(BF)


def hidden_call(normed, weights, bias):
    return call(hidden_kernel, [shape(LEN, FC)] * 2, LIMITS["hidden"], us=TIMES["hidden"])(
        normed, weights, bias.reshape(1, FC)
    )


PART_SHAPES = [shape(ROWS, D)] * 2 + [shape(256, D)] * 3


def store_part(refs, r, columns, part):
    if r == 0:
        refs[0][:, columns] = part[:ROWS]
        refs[1][:, columns] = part[ROWS:]
    else:
        refs[r + 1][:, columns] = part


def out_kernel(groups, attended, activated, weights, *parts):
    for r in range(4):
        here = pl.ds(pl.multiple_of(groups[r] * 256, 256), 256)
        rows = jnp.concatenate([attended[here, :], activated[here, :]], 1)
        store_part(parts, r, slice(0, D), nt(rows, weights[...]).astype(BF))


def out_call(groups, attended, activated, weights):
    return call(out_kernel, PART_SHAPES, LIMITS["out"], [SMEM] + [VMEM] * 3, us=TIMES["out"])(
        groups, attended, activated, weights
    )


def grad_kernel(backs, slope, weights, grad_attended, grad_hidden, sums):
    for j in range((HC + FC) // WIDE):
        grad = nn(backs[...], weights[:, j * WIDE : (j + 1) * WIDE])
        if j == 0:
            grad_attended[...] = grad.astype(BF)
        else:
            part = slice((j - 1) * WIDE, j * WIDE)
            low = (grad * slope[:, part].astype(F32)).astype(BF)
            grad_hidden[:, part] = low
            sums[:, part] = jnp.sum(low.astype(F32), 0, keepdims=True)


def grad_call(backs, slope, weights):
    return call(
        grad_kernel, [shape(LEN, HC), shape(LEN, FC), shape(1, FC, F32)], LIMITS["grad"], us=TIMES["grad"]
    )(backs, slope, weights)


def normed_kernel(groups, projected, hidden, rows, stats, weights, weights2, *refs):
    parts, sums = refs[:5], refs[5]
    for n in range(2):
        part = slice(n * D // 2, (n + 1) * D // 2)
        first = second = None
        for r in range(4):
            here = pl.ds(pl.multiple_of(groups[r] * 256, 256), 256)
            grad = nt(projected[here, :], weights[part, :]) + nt(hidden[here, :], weights2[part, :])
            store_part(parts, r, part, grad.astype(BF))
            standard = (rows[here, part].astype(F32) - stats[here, 0:1]) * stats[here, 64:65]
            term, plain = jnp.sum(grad * standard, 0, keepdims=True), jnp.sum(grad, 0, keepdims=True)
            first, second = (term, plain) if r == 0 else (first + term, second + plain)
        sums[0:1, part] = first
        sums[1:2, part] = second


def normed_call(groups, projected, hidden, rows, stats, weights, weights2):
    return call(
        normed_kernel,
        PART_SHAPES + [shape(2, D, F32)],
        LIMITS["normed"],
        [SMEM] + [VMEM] * 6,
        us=TIMES["normed"],
    )(groups, projected, hidden, rows, stats, weights, weights2)


def weight_kernel(counts, places, *refs):
    out, refs = refs[-1], list(refs[:-1])
    done = 0
    for count in counts:
        left, rights, refs = refs[0], refs[1 : 1 + count], refs[1 + count :]
        for step in range(2):
            turned = jnp.concatenate(
                [left[:, pl.ds(pl.multiple_of(places[4 * step + j] * ROWS, ROWS), ROWS)] for j in range(4)], 1
            ).T
            column = done
            for right in rights:
                for j in range(right.shape[1] // WIDE):
                    term = nn(turned, right[:, j * WIDE : (j + 1) * WIDE]).astype(BF)
                    out[2 * step, :, column : column + WIDE] = term[:256]
                    out[2 * step + 1, :, column : column + WIDE] = term[256:]
                    column += WIDE
        done = column


def weight_call(places, *terms):
    columns = sum(r.shape[1] for term in terms for r in term[1:])
    flat = [r for term in terms for r in term]
    return call(
        functools.partial(weight_kernel, [len(term) - 1 for term in terms]),
        jax.ShapeDtypeStruct((4, 256, columns), BF),
        LIMITS["weight"],
        [SMEM] + [VMEM] * len(flat),
        us=TIMES["weight"] * columns / 2304,
    )(places, *flat)


def nt(left, right):
    return lax.dot_general(left, right, (((1,), (1,)), ((), ())), preferred_element_type=F32)


def nn(left, right):
    return lax.dot_general(left, right, (((1,), (0,)), ((), ())), preferred_element_type=F32)


POWER = SCALE * 1.4426950408889634


def by_head(block, lane):
    return jnp.concatenate([jnp.where(lane == h, block, jnp.zeros((), BF)) for h in range(HEADS)], 0)


def seen_mask():
    key = lax.broadcasted_iota(jnp.int32, (BQ, BQ), 0)
    query = lax.broadcasted_iota(jnp.int32, (BQ, BQ), 1)
    return jnp.concatenate([key <= query] * HEADS, 1)


def forward_kernel(heads, attended, logsum, out_t, values_t):
    queries, keys, values = (heads.at[:, j * HC : (j + 1) * HC] for j in range(3))
    values_t[...] = values[...].T
    lane = lax.broadcasted_iota(jnp.int32, (BQ, HC), 1) // HD
    seen = seen_mask()
    for q in range(LEN // BQ):
        here = slice(q * BQ, (q + 1) * BQ)
        query = by_head(queries[here, :], lane)
        blocks = []
        largest = None
        for k in range(q + 1):
            block = nt(keys[k * BQ : (k + 1) * BQ, :], query)
            if k == q:
                block = jnp.where(seen, block, -1e30)
            blocks.append(block)
            top = jnp.max(block, 0, keepdims=True)
            largest = top if largest is None else jnp.maximum(largest, top)
        total = jnp.zeros((1, HEADS * BQ), F32)
        found = [jnp.zeros((HD, BQ), F32)] * HEADS
        for k in range(q + 1):
            powers = jnp.exp2((blocks[k] - largest) * POWER)
            total = total + jnp.sum(powers, 0, keepdims=True)
            low = powers.astype(BF)
            for h in range(HEADS):
                found[h] = found[h] + nn(
                    values_t[h * HD : (h + 1) * HD, k * BQ : (k + 1) * BQ], low[:, h * BQ : (h + 1) * BQ]
                )
        scale = 1.0 / total
        base = largest * POWER + jnp.log2(total)
        for h in range(HEADS):
            out_t[h * HD : (h + 1) * HD, here] = found[h] * scale[:, h * BQ : (h + 1) * BQ]
            logsum[h : h + 1, here] = base[:, h * BQ : (h + 1) * BQ]
    attended[...] = out_t[...].T.astype(BF)


def forward_call(heads):
    return call(
        forward_kernel,
        [shape(LEN, HC), shape(8, LEN, F32), shape(HC, LEN, F32)],
        LIMITS["forward"],
        scratch_shapes=[pltpu.VMEM((HC, LEN), BF)],
        us=TIMES["forward"],
    )(heads)


def backward_kernel(
    heads, grads, logsum, out_t, tables, out, sums, keys_t, query_grads, key_grads, value_grads
):
    queries, keys, values = (heads.at[:, j * HC : (j + 1) * HC] for j in range(3))
    keys_t[...] = keys[...].T
    turned = grads[...].astype(F32).T * out_t[...]
    lane = lax.broadcasted_iota(jnp.int32, (BQ, HC), 1) // HD
    seen = seen_mask()
    for q in reversed(range(LEN // BQ)):
        here = slice(q * BQ, (q + 1) * BQ)
        query = by_head(queries[here, :], lane)
        grad = by_head(grads[here, :], lane)
        base = jnp.concatenate([logsum[h : h + 1, here] for h in range(HEADS)], 1)
        dots = jnp.concatenate(
            [jnp.sum(turned[h * HD : (h + 1) * HD, here], 0, keepdims=True) for h in range(HEADS)], 1
        )
        found = [jnp.zeros((HD, BQ), F32)] * HEADS
        for k in range(q + 1):
            there = slice(k * BQ, (k + 1) * BQ)
            probs = jnp.exp2(nt(keys[there, :], query) * POWER - base)
            if k == q:
                probs = jnp.where(seen, probs, 0.0)
            score = (probs * (nt(values[there, :], grad) - dots)).astype(BF)
            value_grad, key_grad = nn(probs.astype(BF), grad), nn(score, query)
            if q == LEN // BQ - 1:
                value_grads[there, :] = value_grad
                key_grads[there, :] = key_grad
            else:
                value_grads[there, :] += value_grad
                key_grads[there, :] += key_grad
            for h in range(HEADS):
                found[h] = found[h] + nn(
                    keys_t[h * HD : (h + 1) * HD, there], score[:, h * BQ : (h + 1) * BQ]
                )
        for h in range(HEADS):
            query_grads[h * HD : (h + 1) * HD, here] = found[h]
    parts = (
        rotated(query_grads[...].T * SCALE, tables, -1.0),
        rotated(key_grads[...] * SCALE, tables, -1.0),
        value_grads[...],
    )
    for j, part in enumerate(parts):
        low = part.astype(BF)
        out[:, j * HC : (j + 1) * HC] = low
        sums[:, j * HC : (j + 1) * HC] = jnp.sum(low.astype(F32), 0, keepdims=True)


def backward_call(heads, grads, logsum, out_t, tables):
    return call(
        backward_kernel,
        [shape(LEN, 3 * HC), shape(1, 3 * HC, F32)],
        LIMITS["backward"],
        scratch_shapes=[pltpu.VMEM((HC, LEN), BF), pltpu.VMEM((HC, LEN), F32)] + [pltpu.VMEM((LEN, HC), F32)] * 2,
        us=TIMES["backward"],
    )(heads, grads, logsum, out_t, tables)


def adamw(param, grad, first, second, rate, decay):
    first_new = BETA_ONE * first + (1.0 - BETA_ONE) * grad
    second_new = BETA_TWO * second + (1.0 - BETA_TWO) * grad * grad
    ratio = (
        first_new
        / (1.0 - BETA_ONE**STEP)
        / (jnp.sqrt(second_new / (1.0 - BETA_TWO**STEP)) + ADAM_EPSILON)
    )
    return (grad, first_new, second_new, param - rate * (ratio + decay * param))


def side_by_side(stack):
    return jnp.concatenate([stack[j] for j in range(stack.shape[0])], 1)


def per_device(
    tokens,
    cotangent,
    attn_weight,
    mlp_weight,
    qkv_bias,
    fc1_bias,
    vectors,
    attn_first,
    mlp_first,
    qkv_first,
    fc1_first,
    vector_first,
    attn_second,
    mlp_second,
    qkv_second,
    fc1_second,
    vector_second,
):
    dp = lax.axis_index("dp")
    tensor = lax.axis_index("tensor")
    x, y, core = dp // 8, lax.rem(dp // 2, 4), lax.rem(dp, 2)
    z, h = tensor // 2, lax.rem(tensor, 2)
    places = weight_places(x, y, core)
    groups = jnp.stack([lax.rem(z + step, 4) for step in (2, 1, 3, 0)]).astype(jnp.int32)
    grad_places = [
        jnp.stack(
            [(xx * 4 + lax.rem(y + step, 4)) * 2 + c for step in (2, 1, 3, 0) for xx in (0, 1)]
        ).astype(jnp.int32)
        for c in (1 - core, core)
    ]

    half = ROWS // 2
    at_z = [place_of(z, h, step) for step in range(4)]
    tables = rotary_tables()

    qkv_own = side_by_side(attn_weight[:3].astype(BF))
    rest_own = jnp.concatenate([mlp_weight[0], attn_weight[3], mlp_weight[1]], 1).astype(BF)

    swapped = swap_h(tokens)
    below_own, above_own = up_z(tokens), down_z(tokens)
    qkv_swapped = swap_x(qkv_own)
    swapped, below_own, above_own, qkv_swapped = together(swapped, below_own, above_own, qkv_swapped)
    below_mid = up_z(jnp.concatenate([swapped, below_own[:half]], 0))
    above_mid = down_z(jnp.concatenate([swapped, above_own[half:]], 0))
    qkv_pair = jnp.concatenate([qkv_own, qkv_swapped], 0)
    qkv_below, qkv_above = up_y(qkv_pair), down_y(qkv_pair)
    rest_swapped = swap_x(after(rest_own, qkv_swapped))
    normed_a = call(norm_first_kernel, [shape(512, D), shape(512, 128, F32)], 8)(
        tokens, swapped, below_own, above_own, vectors
    )
    below_mid, above_mid, qkv_below, qkv_above, rest_swapped, normed_a = together(
        below_mid, above_mid, qkv_below, qkv_above, rest_swapped, normed_a
    )
    first, second = up_z(below_mid[:half]), down_z(above_mid[half:ROWS])
    fc1_pair = jnp.concatenate([rest_own[:, :FC], rest_swapped[:, :FC]], 0)
    below_message = up_y(beside(fc1_pair, qkv_below[:ROWS]))
    above_message = down_y(beside(fc1_pair, qkv_above[ROWS:]))
    backs_swapped = swap_h(after(cotangent, below_mid))
    normed_b = call(norm_second_kernel, [shape(384, D), shape(384, 128, F32)], 8)(below_mid, above_mid, vectors)
    back_pair = jnp.concatenate([rest_own[:, FC:], rest_swapped[:, FC:]], 0)
    first, second, below_message, above_message, backs_swapped, normed_b, back_pair = together(
        first, second, below_message, above_message, backs_swapped, normed_b, back_pair
    )
    backs_pair = jnp.concatenate([cotangent, backs_swapped], 0)
    below_backs, above_backs = up_z(backs_pair), down_z(backs_pair)
    fc1_below, fc1_above = below_message[:, :FC], above_message[:, :FC]
    qkv_mine = whole_ring(qkv_pair, qkv_above, apart(below_message, FC), apart(above_message, FC), qkv_below)
    qkv_full = assembled(places, qkv_mine, swap_core(qkv_mine))
    below_message = up_y(beside(back_pair, fc1_below[:ROWS]))
    above_message = down_y(beside(back_pair, fc1_above[ROWS:]))
    row_places = jnp.stack([*at_z[0], at_z[3][0], at_z[1][0], at_z[3][1], at_z[1][1], *at_z[2]]).astype(jnp.int32)
    normed, stats = call(norm_last_kernel, [shape(LEN, D), shape(LEN, 128, F32)], 12, [SMEM] + [VMEM] * 7)(
        row_places, first, second, vectors, *normed_a, *normed_b
    )
    heads = qkv_call(normed, qkv_full, qkv_bias, tables)
    attended, logsum, attended_t = forward_call(heads)
    below_backs, above_backs, below_message, above_message, attended = together(
        below_backs, above_backs, below_message, above_message, attended
    )
    far_backs, far_backs_swapped = up_z(below_backs[:ROWS]), down_z(above_backs[ROWS:])
    back_columns = HC + FC
    back_below, back_above = below_message[:, :back_columns], above_message[:, :back_columns]
    fc1_mine = whole_ring(
        fc1_pair, fc1_above, apart(below_message, back_columns), apart(above_message, back_columns), fc1_below
    )
    fc1_full = assembled(places, fc1_mine, swap_core(fc1_mine))
    rows = call(rows_kernel, shape(LEN, D), 12, [SMEM] + [VMEM] * 8)(
        row_places, after(tokens, attended), swapped, below_own, above_own, below_mid, above_mid, first, second
    )
    back_far, back_far_swapped = up_y(back_below[:ROWS]), down_y(back_above[ROWS:])
    activated, slope = hidden_call(normed, fc1_full, fc1_bias)
    far_backs, far_backs_swapped, back_far, back_far_swapped, activated, rows = together(
        far_backs, far_backs_swapped, back_far, back_far_swapped, activated, rows
    )
    back_mine = whole_ring(back_pair, back_above, back_far, back_far_swapped, back_below)
    back_full = assembled(places, back_mine, swap_core(back_mine))
    back_places = jnp.stack([*at_z[0], *at_z[3], *at_z[1], *at_z[2]]).astype(jnp.int32)
    backs = call(backs_kernel, shape(LEN, D), 10, [SMEM] + [VMEM] * 5)(
        back_places, backs_pair, below_backs, above_backs, far_backs, far_backs_swapped
    )
    out_parts = out_call(groups, attended, activated, back_full)
    out_parts, backs = together(out_parts, backs)
    from_below, from_above = up_z(out_parts[0]), down_z(out_parts[1])
    grad_attended, grad_hidden, hidden_sums = grad_call(backs, slope, back_full)
    early = ((backs, attended, activated), (normed, grad_hidden))
    early_other = weight_call(grad_places[0], *early)
    from_below, from_above, early_other = together(from_below, from_above, early_other)
    got_up, got_down = (
        send(part) for send, part in zip((up_z, down_z), near(out_parts[2], out_parts[3], from_below, from_above))
    )
    early_got = swap_core(early_other)
    projected, projected_sums = backward_call(heads, grad_attended, logsum, attended_t, tables)
    early_mine = weight_call(grad_places[1], *early)
    *normed_parts, normed_sums = normed_call(
        groups, projected, grad_hidden, rows, stats, qkv_full, fc1_full
    )
    late_other = weight_call(grad_places[0], (normed, projected))
    got_up, got_down, early_got, early_mine, normed_parts, normed_sums, late_other = together(
        got_up, got_down, early_got, early_mine, normed_parts, normed_sums, late_other
    )
    from_below, from_above = up_z(normed_parts[0]), down_z(normed_parts[1])
    early_far = summed_part(early_mine, early_got, 0)
    early_below, early_above = up_y(early_far[:ROWS]), down_y(early_far[ROWS:])
    late_got = swap_core(late_other)
    late_mine = weight_call(grad_places[1], (normed, projected))
    out_own, out_sent = last(h, out_parts[4], got_up, got_down)
    small = jnp.concatenate(
        [normed_sums.reshape(-1), jnp.sum(cotangent.astype(F32), 0), projected_sums.reshape(-1), hidden_sums.reshape(-1)]
    ).reshape(-1, 128)
    small = small + lax.ppermute(small, "dp", CORE_SWAP)
    from_below, from_above, early_below, early_above, early_mine, early_got, late_got, late_mine, out_sent, small = (
        together(
            from_below, from_above, early_below, early_above, early_mine, early_got, late_got, late_mine, out_sent, small
        )
    )
    got_up, got_down = (
        send(part)
        for send, part in zip((up_z, down_z), near(normed_parts[2], normed_parts[3], from_below, from_above))
    )
    late_far = summed_part(late_mine, late_got, 0)
    early_near = near(
        summed_part(early_mine, early_got, 1), summed_part(early_mine, early_got, 2), early_below, early_above
    )
    early_up = up_y(beside(early_near[0], late_far[:ROWS]))
    early_down = down_y(beside(early_near[1], late_far[ROWS:]))
    out_got = swap_h(out_sent)
    small = small + lax.ppermute(small, "dp", X_SWAP)
    got_up, got_down, early_up, early_down, early_mine, early_got, late_mine, late_got, out_got, small = together(
        got_up, got_down, early_up, early_down, early_mine, early_got, late_mine, late_got, out_got, small
    )
    grad_own, grad_sent = last(h, normed_parts[4], got_up, got_down)
    grad_got = swap_h(grad_sent)
    early_columns = HC + 2 * FC
    early_own, early_sent = last(
        x, summed_part(early_mine, early_got, 3), early_up[:, :early_columns], early_down[:, :early_columns]
    )
    early_last = swap_x(early_sent)
    late_below, late_above = apart(early_up, early_columns), apart(early_down, early_columns)
    late_near = near(summed_part(late_mine, late_got, 1), summed_part(late_mine, late_got, 2), late_below, late_above)
    late_up, late_down = up_y(late_near[0]), down_y(late_near[1])
    local = tokens.astype(F32)
    out = (local + (out_own + out_got.astype(F32)) + vectors[2] + vectors[3]).astype(BF)
    small = sum(lax.ppermute(small, "dp", p) for p in (Y_UP, Y_DOWN, Y_FAR)) + small
    grad_got, early_last, late_up, late_down, out, small = together(
        grad_got, early_last, late_up, late_down, out, small
    )
    late_own, late_sent = last(x, summed_part(late_mine, late_got, 3), late_up, late_down)
    late_last = swap_x(late_sent)
    bias_sum = small[3 * D // 128 :].reshape(-1)
    small = small[: 3 * D // 128]
    small = sum(lax.ppermute(small, "tensor", p) for p in (Z_UP, Z_DOWN, Z_FAR)) + small
    grad_normed = grad_own + grad_got.astype(F32)
    early_grad = early_own + early_last.astype(F32)

    local_centred = local - jnp.mean(local, -1, keepdims=True)
    local_inverse = lax.rsqrt(jnp.mean(local_centred * local_centred, -1, keepdims=True) + EPSILON)
    local_standard = local_centred * local_inverse
    back_local = cotangent.astype(F32)
    grad_standard = grad_normed * vectors[0]
    input_grad = back_local + local_inverse * (
        grad_standard
        - jnp.mean(grad_standard, -1, keepdims=True)
        - local_standard * jnp.mean(grad_standard * local_standard, -1, keepdims=True)
    )

    late_last, small, input_grad, early_grad = together(late_last, small, input_grad, early_grad)
    vector_sum = (small + lax.ppermute(small, "tensor", H_SWAP)).reshape(3, D)
    qkv_grad_w = late_own + late_last.astype(F32)
    vector_grad = jnp.concatenate([vector_sum, vector_sum[2:3]], 0)

    attn_grad = jnp.stack(
        [qkv_grad_w[:, :HC], qkv_grad_w[:, HC : 2 * HC], qkv_grad_w[:, 2 * HC :], early_grad[:, :HC]]
    )
    mlp_grad = jnp.stack([early_grad[:, back_columns:], early_grad[:, HC:back_columns]])
    qkv_grad = bias_sum[: 3 * HC].reshape(3, HC)
    fc1_grad = bias_sum[3 * HC :]
    attn_out = adamw(attn_weight, attn_grad, attn_first, attn_second, 0.04, 0.1)
    mlp_out = adamw(mlp_weight, mlp_grad, mlp_first, mlp_second, 0.04, 0.1)
    qkv_out = adamw(qkv_bias, qkv_grad, qkv_first, qkv_second, 0.3, 0.0)
    fc1_out = adamw(fc1_bias, fc1_grad, fc1_first, fc1_second, 0.3, 0.0)
    vector_out = adamw(vectors, vector_grad, vector_first, vector_second, 0.2, 0.0)
    return (out, input_grad, *attn_out, *mlp_out, *qkv_out, *fc1_out, *vector_out)


def solution(mesh):
    rows = P(("dp", "tensor"), None)
    weight = P(None, "dp", "tensor")
    qkv = P(None, "tensor")
    fc1 = P("tensor")
    return jax.shard_map(
        per_device,
        mesh=mesh,
        in_specs=(rows, rows, weight, weight, qkv, fc1, P()) + (weight, weight, qkv, fc1, P()) * 2,
        out_specs=(rows, rows) + (weight,) * 8 + (qkv,) * 4 + (fc1,) * 4 + (P(),) * 4,
        check_vma=False,
    )
```

```python
import functools

import jax
import jax.numpy as jnp
import numpy as np
from jax import lax
from jax.experimental import pallas as pl
from jax.experimental.pallas import tpu as pltpu
from jax.sharding import PartitionSpec as P

D = 2048
HD = 64
ROT = 32
LEN = 1024
STEP = 10
HEADS = 4
HC = HEADS * HD
FC = 1024
ROWS = 128
HALF = ROWS // 2
BQ = 256

EPSILON = 1e-05
SCALE = 0.125
BETA_ONE = 0.9
BETA_TWO = 0.999
ADAM_EPSILON = 1e-08
BF = jnp.bfloat16
LIMITS = dict(send=8, assemble=5, qkv=7, hidden=9, out=9, grad=8, normed=12, weight=8, forward=11, backward=13)
TIMES = dict(qkv=4.0, hidden=6.0, out=6.0, grad=5.5, normed=9.0, weight=5.0, forward=5.0, backward=8.0)
DECLARED = 0.3
F32 = jnp.float32


def dp_perm(move):
    pairs = []
    for x in range(2):
        for y in range(4):
            for c in range(2):
                nx, ny, nc = move(x, y, c)
                pairs.append(((x * 4 + y) * 2 + c, (nx * 4 + ny % 4) * 2 + nc))
    return pairs


def tensor_perm(move):
    pairs = []
    for z in range(4):
        for h in range(2):
            nz, nh = move(z, h)
            pairs.append((z * 2 + h, (nz % 4) * 2 + nh))
    return pairs


Y_UP = dp_perm(lambda x, y, c: (x, y + 1, c))
Y_DOWN = dp_perm(lambda x, y, c: (x, y - 1, c))
X_SWAP = dp_perm(lambda x, y, c: (1 - x, y, c))
CORE_SWAP = dp_perm(lambda x, y, c: (x, y, 1 - c))
Z_UP = tensor_perm(lambda z, h: (z + 1, h))
Z_DOWN = tensor_perm(lambda z, h: (z - 1, h))
Y_FAR = dp_perm(lambda x, y, c: (x, y + 2, c))
H_SWAP = tensor_perm(lambda z, h: (z, 1 - h))


def at(array, index, axis):
    return lax.dynamic_index_in_dim(array, index, axis, keepdims=False)


def up_z(v):
    return lax.ppermute(v, "tensor", Z_UP)


def down_z(v):
    return lax.ppermute(v, "tensor", Z_DOWN)


def swap_h(v):
    return lax.ppermute(v, "tensor", H_SWAP)


def up_y(v):
    return lax.ppermute(v, "dp", Y_UP)


def down_y(v):
    return lax.ppermute(v, "dp", Y_DOWN)


def swap_x(v):
    return lax.ppermute(v, "dp", X_SWAP)


def swap_core(v):
    return lax.ppermute(v, "dp", CORE_SWAP)


SMEM = pl.BlockSpec(memory_space=pltpu.SMEM)
VMEM = pl.BlockSpec(memory_space=pltpu.VMEM)


ANY = pl.BlockSpec(memory_space=pl.ANY)


def part(arrays, k):
    held = arrays[k * len(arrays) // 4]
    k = k % held.shape[0]
    return pl.BlockSpec((1, *held.shape[1:]), lambda i: (k, 0, 0)), held


def call(kernel, out_shape, mebibytes, in_specs=None, scratch_shapes=(), us=1.0, deps=()):
    def run(*args):
        specs = list(in_specs or [VMEM] * len(args))
        gridded = any(spec.index_map is not None for spec in specs)

        def fit(spec, array):
            if gridded and spec is VMEM:
                return pl.BlockSpec(array.shape, lambda i: (0,) * len(array.shape))
            return spec

        def body(*refs):
            kernel(*refs[: len(args)], *refs[len(args) + len(deps) :])

        return pl.pallas_call(
            body,
            out_shape=out_shape,
            grid=(1,) if gridded else (),
            out_specs=jax.tree.map(lambda out: fit(VMEM, out), out_shape),
            in_specs=[fit(spec, arg) for spec, arg in zip(specs, args)] + [ANY] * len(deps),
            scratch_shapes=scratch_shapes,
            compiler_params=pltpu.CompilerParams(vmem_limit_bytes=mebibytes * 1024 * 1024),
            cost_estimate=pl.CostEstimate(
                flops=int(us * DECLARED * 1.1e9), bytes_accessed=1000, transcendentals=0
            ),
        )(*args, *deps)

    return run


def nothing_kernel(*refs):
    pass


def tied(value, *deps):
    return pl.pallas_call(
        nothing_kernel,
        out_shape=jax.ShapeDtypeStruct(value.shape, value.dtype),
        in_specs=[ANY] * (1 + len(deps)),
        out_specs=ANY,
        input_output_aliases={0: 0},
        cost_estimate=pl.CostEstimate(flops=1000, bytes_accessed=1000, transcendentals=0),
    )(value, *deps)


def shape(rows, columns, dtype=BF):
    return jax.ShapeDtypeStruct((rows, columns), dtype)


def normalized(block, vectors, normed, stats, at):
    inputs = block.astype(F32)
    mean = jnp.mean(inputs, -1, keepdims=True)
    centred = inputs - mean
    inverse = lax.rsqrt(jnp.mean(centred * centred, -1, keepdims=True) + EPSILON)
    normed[at, :] = (centred * inverse * vectors[0:1, :] + vectors[1:2, :]).astype(BF)
    lane = lax.broadcasted_iota(jnp.int32, (ROWS, 128), 1)
    stats[at, :] = jnp.where(lane < 64, mean, inverse)


def norm_first_kernel(own, swapped, below, above, vectors, normed, stats):
    for i, block in enumerate((own, swapped, below, above)):
        normalized(block[...], vectors, normed, stats, slice(i * ROWS, (i + 1) * ROWS))


def norm_second_kernel(below, above, vectors, normed, stats):
    far = jnp.concatenate([below[ROWS:, :], above[ROWS:, :]], 0)
    for i, block in enumerate((below[:ROWS, :], above[:ROWS, :], far)):
        normalized(block, vectors, normed, stats, slice(i * ROWS, (i + 1) * ROWS))


def norm_last_kernel(places, below, above, vectors, normed_a, stats_a, normed_b, stats_b, normed, stats):
    at = [pl.ds(pl.multiple_of(places[i] * ROWS, ROWS), ROWS) for i in range(8)]
    normalized(jnp.concatenate([below[:HALF, :], above[:HALF, :]], 0), vectors, normed, stats, at[7])
    for i in range(7):
        held, held_stats, k = (normed_a, stats_a, i) if i < 4 else (normed_b, stats_b, i - 4)
        normed[at[i], :] = held[k * ROWS : (k + 1) * ROWS, :]
        stats[at[i], :] = held_stats[k * ROWS : (k + 1) * ROWS, :]


def rows_kernel(skipped, places, own, swapped, below, above, below_mid, above_mid, first, second, rows):
    far = jnp.concatenate([below_mid[ROWS:, :], above_mid[ROWS:, :]], 0)
    last = jnp.concatenate([first[:HALF, :], second[:HALF, :]], 0)
    near = [ref[skipped : skipped + ROWS, :] for ref in (below, above)]
    blocks = (own[...], swapped[...], *near, below_mid[:ROWS, :], above_mid[:ROWS, :], far, last)
    for i, block in enumerate(blocks):
        rows[pl.ds(pl.multiple_of(places[i] * ROWS, ROWS), ROWS), :] = block


def rows_call(skipped, places, *blocks, deps=()):
    return call(
        functools.partial(rows_kernel, skipped), shape(LEN, D), 12, [SMEM] + [VMEM] * 8, deps=deps
    )(places, *blocks)


def beside(message, wide, rows):
    done = 0
    for piece in wide:
        message[done : done + piece.shape[0], : piece.shape[1]] = piece
        done += piece.shape[0]
    columns, middle = wide[0].shape[1], rows.shape[1] // 2
    message[:ROWS, columns:] = rows[:, :middle]
    message[ROWS:, columns:] = rows[:, middle:]


def apart(message, columns):
    return jnp.concatenate([message[:ROWS, columns:], message[ROWS:, columns:]], 1)


def stack(out, *pieces):
    done = 0
    for piece in pieces:
        out[done : done + piece.shape[0], :] = piece
        done += piece.shape[0]


def send_second_kernel(swapped, below, above, qkv_own, qkv_swapped, rest_own, up, down, pair, rest):
    stack(up, swapped[...], below[:HALF, :])
    stack(down, swapped[...], above[HALF:, :])
    stack(pair, qkv_own[...], qkv_swapped[...])
    rest[...] = rest_own[...]


def send_third_kernel(
    below_mid, above_mid, qkv_below, qkv_above, rest_own, rest_swapped, backs, up, down, message_up, message_down, backs_out
):
    stack(up, below_mid[:HALF, :], backs[...])
    stack(down, above_mid[HALF:ROWS, :], backs[...])
    pair = rest_own[:, :FC], rest_swapped[:, :FC]
    beside(message_up, pair, qkv_below[:ROWS, :])
    beside(message_down, pair, qkv_above[ROWS:, :])
    backs_out[...] = backs[...]


def send_fourth_kernel(
    below_last,
    above_last,
    message_below,
    message_above,
    backs_swapped,
    rest_own,
    rest_swapped,
    qkv_pair,
    qkv_below,
    qkv_above,
    up,
    down,
    message_up,
    message_down,
    qkv_mine,
):
    stack(up, backs_swapped[...], below_last[HALF:ROWS, :])
    stack(down, backs_swapped[...], above_last[ROWS:, :])
    pair = rest_own[:, FC:], rest_swapped[:, FC:]
    beside(message_up, pair, message_below[:ROWS, :FC])
    beside(message_down, pair, message_above[ROWS:, :FC])
    stack(qkv_mine, qkv_pair[...], qkv_above[...], apart(message_below, FC), apart(message_above, FC), qkv_below[...])


def send_fifth_kernel(
    below_backs,
    above_backs,
    own_first,
    below_first,
    above_first,
    own_second,
    below_second,
    above_second,
    up,
    down,
    far_up,
    far_down,
    fc1_mine,
    back_mine,
):
    up[...] = below_backs[:HALF, :]
    down[...] = above_backs[HALF:ROWS, :]
    columns = HC + FC
    far_up[...] = below_second[:ROWS, :columns]
    far_down[...] = above_second[ROWS:, :columns]
    stack(
        fc1_mine,
        own_first[:, :FC],
        above_first[:, :FC],
        apart(below_second, columns),
        apart(above_second, columns),
        below_first[:, :FC],
    )
    stack(back_mine, own_second[:, :columns], above_second[:, :columns], below_second[:, :columns])


def send_sixth_kernel(far, far_swapped, mine):
    stack(mine, far[...], far_swapped[...])


def place_of(z, h, step):
    base = lax.rem(z + step, 4) * 2
    return base + h, base + 1 - h


def weight_places(x, y, core, steps):
    places = []
    for c in (core, 1 - core):
        for step in steps:
            yy = lax.rem(y + step, 4)
            places += [(x * 4 + yy) * 2 + c, ((1 - x) * 4 + yy) * 2 + c]
    return jnp.stack(places).astype(jnp.int32)


EXTRA = 16


def coded(sums):
    high = sums.astype(BF)
    low = (sums - high.astype(F32)).astype(BF)
    rest = jnp.zeros((EXTRA - 2 * sums.shape[0], sums.shape[1]), F32)
    return jnp.concatenate([high.astype(F32), low.astype(F32), rest], 0).astype(BF)


def decoded(block):
    block = block.astype(F32)
    return block[:3] + block[3:6]


def near_kernel(above, below, from_below, from_above, up, down):
    up[:ROWS, :] = (above[:ROWS, :].astype(F32) + from_below[:ROWS, :].astype(F32)).astype(BF)
    up[ROWS:256, :] = above[ROWS:, :]
    down[:ROWS, :] = below[:ROWS, :]
    down[ROWS:, :] = (below[ROWS:, :].astype(F32) + from_above[:ROWS, :].astype(F32)).astype(BF)
    if up.shape[0] > 256:
        up[256:, :] = from_below[ROWS:, :]


def near(above, below, from_below, from_above, deps=()):
    columns, more = above.shape[1], from_below.shape[0] - ROWS
    return call(near_kernel, [shape(256 + more, columns), shape(256, columns)], 10, deps=deps)(
        above, below, from_below, from_above
    )


def last_kernel(own, here, got_up, got_down, kept, sent):
    for out, which in ((kept, own[0]), (sent, 1 - own[0])):
        at = pl.ds(pl.multiple_of(which * ROWS, ROWS), ROWS)
        total = here[at, :].astype(F32) + got_up[at, :].astype(F32) + got_down[at, :].astype(F32)
        out[...] = total.astype(out.dtype)


def last(own, here, got_up, got_down, deps=()):
    columns = here.shape[1]
    return call(
        last_kernel, [shape(ROWS, columns, F32), shape(ROWS, columns)], 10, [SMEM] + [VMEM] * 3, deps=deps
    )(own, here, got_up, got_down)


def grad_last_kernel(own, here, got_up, got_down, sums, from_below, from_above, kept, sent, total_sums):
    last_kernel(own, here, got_up, got_down, kept, sent.at[:ROWS])
    total = sums[...] + decoded(from_below[ROWS:, :]) + decoded(from_above[ROWS:, :]) + decoded(got_up[256:, :])
    total_sums[...] = total
    sent[ROWS:, :] = coded(total)


def grad_last(own, here, got_up, got_down, sums, from_below, from_above, deps=()):
    outs = [shape(ROWS, D, F32), shape(ROWS + EXTRA, D), shape(3, D, F32)]
    return call(grad_last_kernel, outs, 12, [SMEM] + [VMEM] * 6, deps=deps)(
        own, here, got_up, got_down, sums, from_below, from_above
    )


def small_kernel(sums, got, projected, hidden, out):
    out[:3, :] = sums[...] + decoded(got[ROWS:, :])
    rest = jnp.zeros((1, D - 3 * HC - FC), F32)
    out[3:, :] = jnp.concatenate([projected[...], hidden[...], rest], 1)


def plus(mine, got):
    return mine.astype(F32) + got.astype(F32)


def weight_far_kernel(mine, got, first, second):
    total = plus(mine[...], got[0]).astype(BF)
    first[...] = total[:ROWS]
    second[...] = total[ROWS:]


def weight_far(mine, got, deps=()):
    columns = mine[0].shape[1]
    spec, held = part(got, 0)
    return call(weight_far_kernel, [shape(ROWS, columns)] * 2, 14, [VMEM, spec], deps=deps)(mine[0], held)


def weight_near_kernel(above, below, got_above, got_below, from_below, from_above, up, down):
    columns = above.shape[1]
    up[:ROWS, :columns] = (plus(above[:ROWS, :], got_above[0, :ROWS]) + from_below[...].astype(F32)).astype(BF)
    up[ROWS:, :columns] = plus(above[ROWS:, :], got_above[0, ROWS:]).astype(BF)
    down[:ROWS, :columns] = plus(below[:ROWS, :], got_below[0, :ROWS]).astype(BF)
    down[ROWS:, :columns] = (plus(below[ROWS:, :], got_below[0, ROWS:]) + from_above[...].astype(F32)).astype(BF)


def first_near_kernel(above, below, got_above, got_below, from_below, from_above, front, front_got, up, down):
    weight_near_kernel(above, below, got_above, got_below, from_below, from_above, up, down)
    columns = above.shape[1]
    far = plus(front[...], front_got[0]).astype(BF)
    middle = far.shape[1] // 2
    for message, rows in ((up, far[:ROWS]), (down, far[ROWS:])):
        message[:ROWS, columns:] = rows[:, :middle]
        message[ROWS:, columns:] = rows[:, middle:]


def first_near(mine, got, from_below, from_above, front, front_got, deps=()):
    columns, more = mine[0].shape[1], front[0].shape[1]
    (spec, above), (spec2, below), (spec3, far) = part(got, 1), part(got, 2), part(front_got, 0)
    specs = [VMEM, VMEM, spec, spec2, VMEM, VMEM, VMEM, spec3]
    return call(first_near_kernel, [shape(256, columns + more // 2)] * 2, 22, specs, deps=deps)(
        mine[1], mine[2], above, below, from_below, from_above, front[0], far
    )


def second_near_kernel(above, below, got_above, got_below, message_below, message_above, up, down):
    columns = message_below.shape[1] - above.shape[1] // 2
    far = apart(message_below, columns), apart(message_above, columns)
    weight_near_kernel(above, below, got_above, got_below, *far, up, down)


def second_near(mine, got, message_below, message_above, deps=()):
    (spec, above), (spec2, below) = part(got, 1), part(got, 2)
    specs = [VMEM, VMEM, spec, spec2, VMEM, VMEM]
    return call(second_near_kernel, [shape(256, mine[0].shape[1])] * 2, 22, specs, deps=deps)(
        mine[1], mine[2], above, below, message_below, message_above
    )


def weight_last_kernel(own, mine, got, got_up, got_down, kept, sent):
    columns = mine.shape[1]
    for out, which in ((kept, own[0]), (sent, 1 - own[0])):
        at = pl.ds(pl.multiple_of(which * ROWS, ROWS), ROWS)
        total = plus(mine[at, :], got[0, at, :]) + plus(got_up[at, :columns], got_down[at, :columns])
        out[...] = total.astype(out.dtype)


def weight_last(own, mine, got, got_up, got_down, deps=()):
    columns = mine[0].shape[1]
    spec, here = part(got, 3)
    specs = [SMEM, VMEM, spec, VMEM, VMEM]
    return call(weight_last_kernel, [shape(ROWS, columns, F32), shape(ROWS, columns)], 16, specs, deps=deps)(
        own, mine[3], here, got_up, got_down
    )


def add_kernel(first, *refs):
    total = first[...]
    for ref in refs[:-1]:
        total = total + ref[...]
    refs[-1][...] = total


def added(*values, deps=()):
    return call(add_kernel, jax.ShapeDtypeStruct(values[0].shape, F32), 4, deps=deps)(*values)


def send(v, axes, perm):
    return lax.ppermute(v, axes, perm)


def rotary_tables():
    half = ROT // 2
    position = np.arange(LEN, dtype=np.float32)
    frequency = np.float32(10000.0) ** (-np.arange(half, dtype=np.float32) * np.float32(2.0 / ROT))
    angle = (position[:, None] * frequency[None, :].astype(np.float32)).astype(np.float32)
    cosine, sine = np.cos(angle), np.sin(angle)
    rest = np.ones((LEN, HD - ROT), np.float32)
    none = np.zeros((LEN, half), np.float32)
    same = np.concatenate([cosine, cosine, rest] * 2, 1)
    ahead = np.concatenate([-sine, none, 0 * rest] * 2, 1)
    behind = np.concatenate([none, sine, 0 * rest] * 2, 1)
    return jnp.asarray(np.concatenate([same, ahead, behind], 1).astype(np.float32))


def rotated(values, tables, sign):
    wide = [jnp.concatenate([tables[:, j * 128 : (j + 1) * 128]] * 2, 1) for j in range(3)]
    half = ROT // 2
    return values * wide[0] + sign * (
        pltpu.roll(values, HC - half, 1) * wide[1] + pltpu.roll(values, half, 1) * wide[2]
    )


WIDE = 256
SPLIT = 2


def assemble_kernel(places, *refs):
    out = refs[-1]
    done = 0
    for source in refs[:-1]:
        for i in range(source.shape[0] // ROWS):
            start = pl.multiple_of(places[done] * ROWS, ROWS)
            out[pl.ds(start, ROWS), :] = source[i * ROWS : (i + 1) * ROWS, :]
            done += 1


def assembled(places, *sources, deps=()):
    specs = [SMEM] + [VMEM] * len(sources)
    return call(
        assemble_kernel, shape(D, sources[0].shape[1]), LIMITS["assemble"], specs, us=2.0, deps=deps
    )(places, *sources)


def qkv_kernel(rows, weights, bias, tables, heads):
    for j in range(3):
        part = slice(j * HC, (j + 1) * HC)
        pre = nn(rows[...], weights[:, part]) + bias[j : j + 1]
        heads[:, part] = (rotated(pre, tables, 1.0) if j < 2 else pre).astype(BF)


def qkv_call(normed, weights, bias, tables, deps=()):
    return call(qkv_kernel, shape(LEN, 3 * HC), LIMITS["qkv"], us=TIMES["qkv"], deps=deps)(normed, weights, bias, tables)


ROOT = 0.7978845608028654
CUBIC = 0.044715


def hidden_kernel(rows, weights, bias, activated, slope):
    for j in range(FC // WIDE):
        part = slice(j * WIDE, (j + 1) * WIDE)
        hidden = nn(rows[...], weights[:, part]) + bias[:, part]
        square = hidden * hidden
        bent = jnp.tanh(ROOT * (hidden + CUBIC * (square * hidden)))
        half = 0.5 * (1.0 + bent)
        activated[:, part] = (hidden * half).astype(BF)
        slope[:, part] = (
            half + (0.5 * ROOT) * hidden * (1.0 - bent * bent) * (1.0 + (3.0 * CUBIC) * square)
        ).astype(BF)


def hidden_call(normed, weights, bias, deps=()):
    return call(hidden_kernel, [shape(LEN, FC)] * 2, LIMITS["hidden"], us=TIMES["hidden"], deps=deps)(
        normed, weights, bias.reshape(1, FC)
    )


PART_SHAPES = [shape(ROWS, D)] * 2 + [shape(256, D)] * 3


def store_part(refs, r, columns, part):
    if r == 0:
        refs[0][:ROWS, columns] = part[:ROWS]
        refs[1][:ROWS, columns] = part[ROWS:]
    else:
        refs[r + 1][:, columns] = part


def out_kernel(groups, attended, activated, weights, *parts):
    for r in range(4):
        here = pl.ds(pl.multiple_of(groups[r] * 256, 256), 256)
        rows = jnp.concatenate([attended[here, :], activated[here, :]], 1)
        store_part(parts, r, slice(0, D), nt(rows, weights[...]).astype(BF))


def out_call(groups, attended, activated, weights, deps=()):
    return call(out_kernel, PART_SHAPES, LIMITS["out"], [SMEM] + [VMEM] * 3, us=TIMES["out"], deps=deps)(
        groups, attended, activated, weights
    )


def grad_kernel(backs, slope, weights, grad_attended, grad_hidden, sums):
    for j in range((HC + FC) // WIDE):
        grad = nn(backs[...], weights[:, j * WIDE : (j + 1) * WIDE])
        if j == 0:
            grad_attended[...] = grad.astype(BF)
        else:
            part = slice((j - 1) * WIDE, j * WIDE)
            low = (grad * slope[:, part].astype(F32)).astype(BF)
            grad_hidden[:, part] = low
            sums[:, part] = jnp.sum(low.astype(F32), 0, keepdims=True)


def grad_call(backs, slope, weights, deps=()):
    return call(
        grad_kernel, [shape(LEN, HC), shape(LEN, FC), shape(1, FC, F32)], LIMITS["grad"], us=TIMES["grad"], deps=deps
    )(backs, slope, weights)


def normed_kernel(groups, projected, hidden, rows, stats, weights, weights2, back_sums, *refs):
    parts, sums = refs[:5], refs[5]
    for n in range(2):
        part = slice(n * D // 2, (n + 1) * D // 2)
        first = second = None
        for r in range(4):
            here = pl.ds(pl.multiple_of(groups[r] * 256, 256), 256)
            grad = nt(projected[here, :], weights[part, :]) + nt(hidden[here, :], weights2[part, :])
            store_part(parts, r, part, grad.astype(BF))
            standard = (rows[here, part].astype(F32) - stats[here, 0:1]) * stats[here, 64:65]
            term, plain = jnp.sum(grad * standard, 0, keepdims=True), jnp.sum(grad, 0, keepdims=True)
            first, second = (term, plain) if r == 0 else (first + term, second + plain)
        sums[0:1, part] = first
        sums[1:2, part] = second
    sums[2:3, :] = back_sums[...]
    block = coded(sums[...])
    for ref in parts[:2]:
        ref[ROWS:, :] = block


def normed_call(groups, projected, hidden, rows, stats, weights, weights2, back_sums, deps=()):
    return call(
        normed_kernel,
        [shape(ROWS + EXTRA, D)] * 2 + PART_SHAPES[2:] + [shape(3, D, F32)],
        LIMITS["normed"],
        [SMEM] + [VMEM] * 7,
        us=TIMES["normed"],
        deps=deps,
    )(groups, projected, hidden, rows, stats, weights, weights2, back_sums)


def weight_kernel(counts, parts, places, *refs):
    outs, refs = refs[-parts:], list(refs[:-parts])
    outs = [outs[k * parts // 4].at[k % (4 // parts)] for k in range(4)] if parts < 4 else outs
    done = 0
    for count in counts:
        left, rights, refs = refs[0], refs[1 : 1 + count], refs[1 + count :]
        for step in range(2):
            turned = jnp.concatenate(
                [left[:, pl.ds(pl.multiple_of(places[4 * step + j] * ROWS, ROWS), ROWS)] for j in range(4)], 1
            ).T
            column = done
            for right in rights:
                for j in range(right.shape[1] // WIDE):
                    term = nn(turned, right[:, j * WIDE : (j + 1) * WIDE]).astype(BF)
                    outs[2 * step][:, column : column + WIDE] = term[:256]
                    outs[2 * step + 1][:, column : column + WIDE] = term[256:]
                    column += WIDE
        done = column


def weight_call(parts, places, *terms, deps=()):
    columns = sum(r.shape[1] for term in terms for r in term[1:])
    flat = [r for term in terms for r in term]
    outs = [jax.ShapeDtypeStruct((4 // parts, 256, columns), BF)] * parts if parts < 4 else [shape(256, columns)] * 4
    return call(
        functools.partial(weight_kernel, [len(term) - 1 for term in terms], parts),
        outs,
        LIMITS["weight"],
        [SMEM] + [VMEM] * len(flat),
        us=TIMES["weight"] * columns / 2304,
        deps=deps,
    )(places, *flat)


def nt(left, right):
    return lax.dot_general(left, right, (((1,), (1,)), ((), ())), preferred_element_type=F32)


def nn(left, right):
    return lax.dot_general(left, right, (((1,), (0,)), ((), ())), preferred_element_type=F32)


POWER = SCALE * 1.4426950408889634


def by_head(block, lane):
    return jnp.concatenate([jnp.where(lane == h, block, jnp.zeros((), BF)) for h in range(HEADS)], 0)


def seen_mask():
    key = lax.broadcasted_iota(jnp.int32, (BQ, BQ), 0)
    query = lax.broadcasted_iota(jnp.int32, (BQ, BQ), 1)
    return jnp.concatenate([key <= query] * HEADS, 1)


def forward_kernel(heads, attended, logsum, out_t, values_t):
    queries, keys, values = (heads.at[:, j * HC : (j + 1) * HC] for j in range(3))
    values_t[...] = values[...].T
    lane = lax.broadcasted_iota(jnp.int32, (BQ, HC), 1) // HD
    seen = seen_mask()
    for q in range(LEN // BQ):
        here = slice(q * BQ, (q + 1) * BQ)
        query = by_head(queries[here, :], lane)
        blocks = []
        largest = None
        for k in range(q + 1):
            block = nt(keys[k * BQ : (k + 1) * BQ, :], query)
            if k == q:
                block = jnp.where(seen, block, -1e30)
            blocks.append(block)
            top = jnp.max(block, 0, keepdims=True)
            largest = top if largest is None else jnp.maximum(largest, top)
        total = jnp.zeros((1, HEADS * BQ), F32)
        found = [jnp.zeros((HD, BQ), F32)] * HEADS
        for k in range(q + 1):
            powers = jnp.exp2((blocks[k] - largest) * POWER)
            total = total + jnp.sum(powers, 0, keepdims=True)
            low = powers.astype(BF)
            for h in range(HEADS):
                found[h] = found[h] + nn(
                    values_t[h * HD : (h + 1) * HD, k * BQ : (k + 1) * BQ], low[:, h * BQ : (h + 1) * BQ]
                )
        scale = 1.0 / total
        base = largest * POWER + jnp.log2(total)
        for h in range(HEADS):
            out_t[h * HD : (h + 1) * HD, here] = found[h] * scale[:, h * BQ : (h + 1) * BQ]
            logsum[h : h + 1, here] = base[:, h * BQ : (h + 1) * BQ]
    attended[...] = out_t[...].T.astype(BF)


def forward_call(heads, deps=()):
    return call(
        forward_kernel,
        [shape(LEN, HC), shape(8, LEN, F32), shape(HC, LEN, F32)],
        LIMITS["forward"],
        scratch_shapes=[pltpu.VMEM((HC, LEN), BF)],
        us=TIMES["forward"],
        deps=deps,
    )(heads)


def backward_kernel(
    heads, grads, logsum, out_t, tables, out, sums, keys_t, query_grads, key_grads, value_grads
):
    queries, keys, values = (heads.at[:, j * HC : (j + 1) * HC] for j in range(3))
    keys_t[...] = keys[...].T
    turned = grads[...].astype(F32).T * out_t[...]
    lane = lax.broadcasted_iota(jnp.int32, (BQ, HC), 1) // HD
    seen = seen_mask()
    for q in reversed(range(LEN // BQ)):
        here = slice(q * BQ, (q + 1) * BQ)
        query = by_head(queries[here, :], lane)
        grad = by_head(grads[here, :], lane)
        base = jnp.concatenate([logsum[h : h + 1, here] for h in range(HEADS)], 1)
        dots = jnp.concatenate(
            [jnp.sum(turned[h * HD : (h + 1) * HD, here], 0, keepdims=True) for h in range(HEADS)], 1
        )
        found = [jnp.zeros((HD, BQ), F32)] * HEADS
        for k in range(q + 1):
            there = slice(k * BQ, (k + 1) * BQ)
            probs = jnp.exp2(nt(keys[there, :], query) * POWER - base)
            if k == q:
                probs = jnp.where(seen, probs, 0.0)
            score = (probs * (nt(values[there, :], grad) - dots)).astype(BF)
            value_grad, key_grad = nn(probs.astype(BF), grad), nn(score, query)
            if q == LEN // BQ - 1:
                value_grads[there, :] = value_grad
                key_grads[there, :] = key_grad
            else:
                value_grads[there, :] += value_grad
                key_grads[there, :] += key_grad
            for h in range(HEADS):
                found[h] = found[h] + nn(
                    keys_t[h * HD : (h + 1) * HD, there], score[:, h * BQ : (h + 1) * BQ]
                )
        for h in range(HEADS):
            query_grads[h * HD : (h + 1) * HD, here] = found[h]
    parts = (
        rotated(query_grads[...].T * SCALE, tables, -1.0),
        rotated(key_grads[...] * SCALE, tables, -1.0),
        value_grads[...],
    )
    for j, part in enumerate(parts):
        low = part.astype(BF)
        out[:, j * HC : (j + 1) * HC] = low
        sums[:, j * HC : (j + 1) * HC] = jnp.sum(low.astype(F32), 0, keepdims=True)


def backward_call(heads, grads, logsum, out_t, tables, deps=()):
    return call(
        backward_kernel,
        [shape(LEN, 3 * HC), shape(1, 3 * HC, F32)],
        LIMITS["backward"],
        scratch_shapes=[pltpu.VMEM((HC, LEN), BF), pltpu.VMEM((HC, LEN), F32)] + [pltpu.VMEM((LEN, HC), F32)] * 2,
        us=TIMES["backward"],
        deps=deps,
    )(heads, grads, logsum, out_t, tables)


def adamw(param, grad, first, second, rate, decay):
    first_new = BETA_ONE * first + (1.0 - BETA_ONE) * grad
    second_new = BETA_TWO * second + (1.0 - BETA_TWO) * grad * grad
    ratio = (
        first_new
        / (1.0 - BETA_ONE**STEP)
        / (jnp.sqrt(second_new / (1.0 - BETA_TWO**STEP)) + ADAM_EPSILON)
    )
    return (grad, first_new, second_new, param - rate * (ratio + decay * param))


def side_by_side(stack):
    return jnp.concatenate([stack[j] for j in range(stack.shape[0])], 1)


def per_device(
    tokens,
    cotangent,
    attn_weight,
    mlp_weight,
    qkv_bias,
    fc1_bias,
    vectors,
    attn_first,
    mlp_first,
    qkv_first,
    fc1_first,
    vector_first,
    attn_second,
    mlp_second,
    qkv_second,
    fc1_second,
    vector_second,
):
    dp = lax.axis_index("dp")
    tensor = lax.axis_index("tensor")
    x, y, core = dp // 8, lax.rem(dp // 2, 4), lax.rem(dp, 2)
    z, h = tensor // 2, lax.rem(tensor, 2)
    places = weight_places(x, y, core, (0, 1, 2, 3))
    back_places = weight_places(x, y, core, (0, 1, 3, 2))
    groups = jnp.stack([lax.rem(z + step, 4) for step in (2, 1, 3, 0)]).astype(jnp.int32)
    grad_places = [
        jnp.stack(
            [(xx * 4 + lax.rem(y + step, 4)) * 2 + c for step in (2, 1, 3, 0) for xx in (0, 1)]
        ).astype(jnp.int32)
        for c in (1 - core, core)
    ]

    at_z = [place_of(z, h, step) for step in range(4)]
    row_places = jnp.stack([*at_z[0], at_z[3][0], at_z[1][0], at_z[3][1], at_z[1][1], *at_z[2]]).astype(jnp.int32)
    tables = rotary_tables()
    qkv_own = side_by_side(attn_weight[:3].astype(BF))
    rest_own = jnp.concatenate([mlp_weight[0], attn_weight[3], mlp_weight[1]], 1).astype(BF)

    own_x, own_h = (v.reshape(1).astype(jnp.int32) for v in (x, h))
    columns = HC + FC

    swapped = swap_h(tokens)
    below_own, above_own = up_z(tokens), down_z(tokens)
    qkv_swapped = swap_x(qkv_own)
    sent = call(
        send_second_kernel, [shape(192, D)] * 2 + [shape(256, 3 * HC), shape(ROWS, HC + 2 * FC)], LIMITS["send"]
    )(swapped, below_own, above_own, qkv_own, qkv_swapped, rest_own)
    below_mid, above_mid = up_z(sent[0]), down_z(sent[1])
    qkv_pair = sent[2]
    qkv_below, qkv_above = up_y(qkv_pair), down_y(qkv_pair)
    rest_swapped = swap_x(sent[3])
    normed_a = call(norm_first_kernel, [shape(512, D), shape(512, 128, F32)], 8, deps=(qkv_pair,))(
        tokens, swapped, below_own, above_own, vectors
    )
    back_sum = jnp.sum(cotangent.astype(F32), 0, keepdims=True)
    sent = call(
        send_third_kernel,
        [shape(192, D)] * 2 + [shape(256, FC + 3 * HC // 2)] * 2 + [shape(ROWS, D)],
        LIMITS["send"],
        deps=(normed_a[1],),
    )(below_mid, above_mid, qkv_below, qkv_above, rest_own, rest_swapped, cotangent)
    below_last, above_last = up_z(sent[0]), down_z(sent[1])
    own_first = sent[2]
    below_first, above_first = up_y(sent[2]), down_y(sent[3])
    backs_swapped = swap_h(sent[4])
    normed_b = call(norm_second_kernel, [shape(384, D), shape(384, 128, F32)], 8, deps=(own_first,))(
        below_mid, above_mid, vectors
    )
    sent = call(
        send_fourth_kernel,
        [shape(192, D)] * 2 + [shape(256, columns + FC // 2)] * 2 + [shape(8 * ROWS, 3 * HC)],
        LIMITS["send"],
        deps=(normed_b[1],),
    )(
        below_last,
        above_last,
        below_first,
        above_first,
        backs_swapped,
        rest_own,
        rest_swapped,
        qkv_pair,
        qkv_below,
        qkv_above,
    )
    below_backs, above_backs = up_z(sent[0]), down_z(sent[1])
    own_second = sent[2]
    below_second, above_second = up_y(sent[2]), down_y(sent[3])
    qkv_mine = sent[4]
    qkv_other = swap_core(qkv_mine)
    normed, stats = call(
        norm_last_kernel, [shape(LEN, D), shape(LEN, 128, F32)], 12, [SMEM] + [VMEM] * 7, deps=(qkv_mine,)
    )(row_places, below_last, above_last, vectors, *normed_a, *normed_b)
    qkv_full = assembled(places, qkv_mine, qkv_other, deps=(stats,))
    heads = qkv_call(normed, qkv_full, qkv_bias, tables)
    attended, logsum, attended_t = forward_call(heads)
    sent = call(
        send_fifth_kernel,
        [shape(HALF, D)] * 2 + [shape(ROWS, columns)] * 2 + [shape(8 * ROWS, FC), shape(6 * ROWS, columns)],
        LIMITS["send"],
        deps=(logsum,),
    )(below_backs, above_backs, own_first, below_first, above_first, own_second, below_second, above_second)
    first_backs, second_backs = up_z(sent[0]), down_z(sent[1])
    back_far, back_far_swapped = up_y(sent[2]), down_y(sent[3])
    fc1_mine, back_mine = sent[4:]
    fc1_other = swap_core(fc1_mine)
    back_other = swap_core(back_mine)
    rows = rows_call(
        0,
        row_places,
        tokens,
        swapped,
        below_own,
        above_own,
        below_mid,
        above_mid,
        below_last,
        above_last,
        deps=(fc1_mine,),
    )
    fc1_full = assembled(places, fc1_mine, fc1_other, deps=(rows,))
    activated, slope = hidden_call(normed, fc1_full, fc1_bias)
    far_mine = call(
        send_sixth_kernel, shape(256, columns), LIMITS["send"], deps=(slope, first_backs, second_backs, back_other)
    )(back_far, back_far_swapped)
    far_other = swap_core(far_mine)
    backs = rows_call(
        HALF,
        row_places,
        cotangent,
        backs_swapped,
        below_last,
        above_last,
        below_backs,
        above_backs,
        first_backs,
        second_backs,
        deps=(far_mine,),
    )
    back_full = assembled(back_places, back_mine, far_mine, back_other, far_other, deps=(backs,))
    out_parts = out_call(groups, attended, activated, back_full)
    from_below, from_above = up_z(out_parts[0]), down_z(out_parts[1])
    grad_attended, grad_hidden, hidden_sums = grad_call(backs, slope, back_full, deps=(out_parts[0],))
    back = (backs, attended, activated)
    (back_other,) = weight_call(1, grad_places[0], back, deps=(hidden_sums,))
    up, down = near(out_parts[2], out_parts[3], from_below, from_above, deps=(back_other,))
    got_up, got_down = up_z(up), down_z(down)
    back_got = (swap_core(tied(back_other, up)),)
    projected, projected_sums = backward_call(heads, grad_attended, logsum, attended_t, tables, deps=(up,))
    back_mine = weight_call(4, grad_places[1], back, deps=(projected_sums,))
    front = (normed, projected, grad_hidden)
    front_other = weight_call(SPLIT, grad_places[0], front, deps=(back_mine[0],))
    back_far = weight_far(back_mine, back_got, deps=(front_other[0],))
    back_below, back_above = up_y(back_far[0]), down_y(back_far[1])
    *normed_parts, normed_sums = normed_call(
        groups, projected, grad_hidden, rows, stats, qkv_full, fc1_full, back_sum, deps=(back_far[0], got_up, got_down)
    )
    from_below, from_above = up_z(normed_parts[0]), down_z(normed_parts[1])
    front_got = [swap_core(v) for v in front_other]
    front_mine = weight_call(4, grad_places[1], front, deps=(normed_parts[0],))
    out_own, out_sent = last(own_h, out_parts[4], got_up, got_down, deps=(front_mine[0],))
    out_got = swap_h(out_sent)
    far_below, far_above = from_below, from_above
    up, down = near(normed_parts[2], normed_parts[3], from_below, from_above, deps=(out_sent, back_below, back_above))
    got_up, got_down = up_z(up), down_z(down)
    sent = first_near(back_mine, back_got, back_below, back_above, front_mine, front_got, deps=(up, front_got[1]))
    back_up, back_down = up_y(sent[0]), down_y(sent[1])
    local = tokens.astype(F32)
    out = (local + (out_own + out_got.astype(F32)) + vectors[2] + vectors[3]).astype(BF)
    grad_own, grad_sent, sums = grad_last(
        own_h, normed_parts[4], got_up, got_down, normed_sums, far_below, far_above, deps=(out_got,)
    )
    grad_got = swap_h(grad_sent)
    sent = second_near(front_mine, front_got, back_up, back_down, deps=(grad_sent,))
    front_up, front_down = up_y(sent[0]), down_y(sent[1])
    back_own, back_sent = weight_last(own_x, back_mine, back_got, back_up, back_down, deps=(sent[0],))
    back_last = swap_x(back_sent)
    small = call(small_kernel, shape(4, D, F32), 4, deps=(back_last,))(sums, grad_got, projected_sums, hidden_sums)
    small = added(small, send(small, "dp", CORE_SWAP))
    front_own, front_sent = weight_last(
        own_x, front_mine, front_got, front_up, front_down, deps=(grad_got, back_last, small)
    )
    front_last = swap_x(front_sent)
    small = added(
        small, *(send(tied(small, front_sent), "dp", perm) for perm in (Y_UP, Y_DOWN, Y_FAR)), deps=(front_last,)
    )
    small = added(small, send(small, "dp", X_SWAP))
    vector_sum, bias_sum = small[:3], small[3]
    grad_normed = grad_own + grad_got[:ROWS].astype(F32)
    back_grad = back_own + back_last.astype(F32)
    front_grad = front_own + front_last.astype(F32)

    local_centred = local - jnp.mean(local, -1, keepdims=True)
    local_inverse = lax.rsqrt(jnp.mean(local_centred * local_centred, -1, keepdims=True) + EPSILON)
    local_standard = local_centred * local_inverse
    back_local = cotangent.astype(F32)
    grad_standard = grad_normed * vectors[0]
    input_grad = back_local + local_inverse * (
        grad_standard
        - jnp.mean(grad_standard, -1, keepdims=True)
        - local_standard * jnp.mean(grad_standard * local_standard, -1, keepdims=True)
    )

    vector_grad = jnp.concatenate([vector_sum, vector_sum[2:3]], 0)

    attn_grad = jnp.stack(
        [front_grad[:, :HC], front_grad[:, HC : 2 * HC], front_grad[:, 2 * HC : 3 * HC], back_grad[:, :HC]]
    )
    mlp_grad = jnp.stack([front_grad[:, 3 * HC :], back_grad[:, HC:]])
    qkv_grad = bias_sum[: 3 * HC].reshape(3, HC)
    fc1_grad = bias_sum[3 * HC : 3 * HC + FC]
    attn_out = adamw(attn_weight, attn_grad, attn_first, attn_second, 0.04, 0.1)
    mlp_out = adamw(mlp_weight, mlp_grad, mlp_first, mlp_second, 0.04, 0.1)
    qkv_out = adamw(qkv_bias, qkv_grad, qkv_first, qkv_second, 0.3, 0.0)
    fc1_out = adamw(fc1_bias, fc1_grad, fc1_first, fc1_second, 0.3, 0.0)
    vector_out = adamw(vectors, vector_grad, vector_first, vector_second, 0.2, 0.0)
    return (out, input_grad, *attn_out, *mlp_out, *qkv_out, *fc1_out, *vector_out)


def solution(mesh):
    rows = P(("dp", "tensor"), None)
    weight = P(None, "dp", "tensor")
    qkv = P(None, "tensor")
    fc1 = P("tensor")
    return jax.shard_map(
        per_device,
        mesh=mesh,
        in_specs=(rows, rows, weight, weight, qkv, fc1, P()) + (weight, weight, qkv, fc1, P()) * 2,
        out_specs=(rows, rows) + (weight,) * 8 + (qkv,) * 4 + (fc1,) * 4 + (P(),) * 4,
        check_vma=False,
    )
```

```python
import functools

import jax
import jax.numpy as jnp
import numpy as np
from jax import lax
from jax.experimental import pallas as pl
from jax.experimental.pallas import tpu as pltpu
from jax.sharding import PartitionSpec as P

D = 2048
HD = 64
ROT = 32
LEN = 1024
STEP = 10
HEADS = 4
HC = HEADS * HD
FC = 1024
ROWS = 128
HALF = ROWS // 2
BQ = 256

EPSILON = 1e-05
SCALE = 0.125
BETA_ONE = 0.9
BETA_TWO = 0.999
ADAM_EPSILON = 1e-08
BF = jnp.bfloat16
LIMITS = dict(send=8, assemble=5, qkv=7, hidden=9, out=9, grad=8, normed=12, weight=8, forward=11, backward=13)
TIMES = dict(qkv=4.0, hidden=6.0, out=6.0, grad=5.5, normed=9.0, weight=5.0, forward=5.0, backward=8.0)
DECLARED = 0.3
F32 = jnp.float32


def dp_perm(move):
    pairs = []
    for x in range(2):
        for y in range(4):
            for c in range(2):
                nx, ny, nc = move(x, y, c)
                pairs.append(((x * 4 + y) * 2 + c, (nx * 4 + ny % 4) * 2 + nc))
    return pairs


def tensor_perm(move):
    pairs = []
    for z in range(4):
        for h in range(2):
            nz, nh = move(z, h)
            pairs.append((z * 2 + h, (nz % 4) * 2 + nh))
    return pairs


Y_UP = dp_perm(lambda x, y, c: (x, y + 1, c))
Y_DOWN = dp_perm(lambda x, y, c: (x, y - 1, c))
X_SWAP = dp_perm(lambda x, y, c: (1 - x, y, c))
CORE_SWAP = dp_perm(lambda x, y, c: (x, y, 1 - c))
Z_UP = tensor_perm(lambda z, h: (z + 1, h))
Z_DOWN = tensor_perm(lambda z, h: (z - 1, h))
Y_FAR = dp_perm(lambda x, y, c: (x, y + 2, c))
H_SWAP = tensor_perm(lambda z, h: (z, 1 - h))


def at(array, index, axis):
    return lax.dynamic_index_in_dim(array, index, axis, keepdims=False)


def up_z(v):
    return lax.ppermute(v, "tensor", Z_UP)


def down_z(v):
    return lax.ppermute(v, "tensor", Z_DOWN)


def swap_h(v):
    return lax.ppermute(v, "tensor", H_SWAP)


def up_y(v):
    return lax.ppermute(v, "dp", Y_UP)


def down_y(v):
    return lax.ppermute(v, "dp", Y_DOWN)


def swap_x(v):
    return lax.ppermute(v, "dp", X_SWAP)


def swap_core(v):
    return lax.ppermute(v, "dp", CORE_SWAP)


SMEM = pl.BlockSpec(memory_space=pltpu.SMEM)
VMEM = pl.BlockSpec(memory_space=pltpu.VMEM)


ANY = pl.BlockSpec(memory_space=pl.ANY)


def part(arrays, k):
    held = arrays[k * len(arrays) // 4]
    k = k % held.shape[0]
    return pl.BlockSpec((1, *held.shape[1:]), lambda i: (k, 0, 0)), held


def call(kernel, out_shape, mebibytes, in_specs=None, scratch_shapes=(), us=1.0, deps=()):
    def run(*args):
        specs = list(in_specs or [VMEM] * len(args))
        gridded = any(spec.index_map is not None for spec in specs)

        def fit(spec, array):
            if gridded and spec is VMEM:
                return pl.BlockSpec(array.shape, lambda i: (0,) * len(array.shape))
            return spec

        def body(*refs):
            kernel(*refs[: len(args)], *refs[len(args) + len(deps) :])

        return pl.pallas_call(
            body,
            out_shape=out_shape,
            grid=(1,) if gridded else (),
            out_specs=jax.tree.map(lambda out: fit(VMEM, out), out_shape),
            in_specs=[fit(spec, arg) for spec, arg in zip(specs, args)] + [ANY] * len(deps),
            scratch_shapes=scratch_shapes,
            compiler_params=pltpu.CompilerParams(vmem_limit_bytes=mebibytes * 1024 * 1024),
            cost_estimate=pl.CostEstimate(
                flops=int(us * DECLARED * 1.1e9), bytes_accessed=1000, transcendentals=0
            ),
        )(*args, *deps)

    return run


def nothing_kernel(*refs):
    pass


def tied(value, *deps):
    return pl.pallas_call(
        nothing_kernel,
        out_shape=jax.ShapeDtypeStruct(value.shape, value.dtype),
        in_specs=[ANY] * (1 + len(deps)),
        out_specs=ANY,
        input_output_aliases={0: 0},
        compiler_params=pltpu.CompilerParams(vmem_limit_bytes=1024 * 1024),
        cost_estimate=pl.CostEstimate(flops=1000, bytes_accessed=1000, transcendentals=0),
    )(value, *deps)


def shape(rows, columns, dtype=BF):
    return jax.ShapeDtypeStruct((rows, columns), dtype)


def normalized(block, vectors, normed, stats, at):
    inputs = block.astype(F32)
    mean = jnp.mean(inputs, -1, keepdims=True)
    centred = inputs - mean
    inverse = lax.rsqrt(jnp.mean(centred * centred, -1, keepdims=True) + EPSILON)
    normed[at, :] = (centred * inverse * vectors[0:1, :] + vectors[1:2, :]).astype(BF)
    lane = lax.broadcasted_iota(jnp.int32, (ROWS, 128), 1)
    stats[at, :] = jnp.where(lane < 64, mean, inverse)


def norm_first_kernel(own, swapped, below, above, vectors, normed, stats):
    for i, block in enumerate((own, swapped, below, above)):
        normalized(block[...], vectors, normed, stats, slice(i * ROWS, (i + 1) * ROWS))


def norm_second_kernel(below, above, vectors, normed, stats):
    far = jnp.concatenate([below[ROWS:, :], above[ROWS:, :]], 0)
    for i, block in enumerate((below[:ROWS, :], above[:ROWS, :], far)):
        normalized(block, vectors, normed, stats, slice(i * ROWS, (i + 1) * ROWS))


def norm_last_kernel(info, below, above, vectors, normed_a, stats_a, normed_b, stats_b, normed, stats):
    places = At(info, ROW_PLACES)
    at = [pl.ds(pl.multiple_of(places[i] * ROWS, ROWS), ROWS) for i in range(8)]
    normalized(jnp.concatenate([below[:HALF, :], above[:HALF, :]], 0), vectors, normed, stats, at[7])
    for i in range(7):
        held, held_stats, k = (normed_a, stats_a, i) if i < 4 else (normed_b, stats_b, i - 4)
        normed[at[i], :] = held[k * ROWS : (k + 1) * ROWS, :]
        stats[at[i], :] = held_stats[k * ROWS : (k + 1) * ROWS, :]


def rows_kernel(skipped, info, own, swapped, below, above, below_mid, above_mid, first, second, rows):
    places = At(info, ROW_PLACES)
    far = jnp.concatenate([below_mid[ROWS:, :], above_mid[ROWS:, :]], 0)
    last = jnp.concatenate([first[:HALF, :], second[:HALF, :]], 0)
    near = [ref[skipped : skipped + ROWS, :] for ref in (below, above)]
    blocks = (own[...], swapped[...], *near, below_mid[:ROWS, :], above_mid[:ROWS, :], far, last)
    for i, block in enumerate(blocks):
        rows[pl.ds(pl.multiple_of(places[i] * ROWS, ROWS), ROWS), :] = block


def rows_call(skipped, info, *blocks, deps=()):
    return call(
        functools.partial(rows_kernel, skipped), shape(LEN, D), 12, [SMEM] + [VMEM] * 8, deps=deps
    )(info, *blocks)


def beside(message, wide, rows):
    done = 0
    for piece in wide:
        message[done : done + piece.shape[0], : piece.shape[1]] = piece
        done += piece.shape[0]
    columns, middle = wide[0].shape[1], rows.shape[1] // 2
    message[:ROWS, columns:] = rows[:, :middle]
    message[ROWS:, columns:] = rows[:, middle:]


def apart(message, columns):
    return jnp.concatenate([message[:ROWS, columns:], message[ROWS:, columns:]], 1)


def stack(out, *pieces):
    done = 0
    for piece in pieces:
        out[done : done + piece.shape[0], :] = piece
        done += piece.shape[0]


def send_second_kernel(swapped, below, above, qkv_own, qkv_swapped, rest_own, up, down, pair, rest):
    stack(up, swapped[...], below[:HALF, :])
    stack(down, swapped[...], above[HALF:, :])
    stack(pair, qkv_own[...], qkv_swapped[...])
    rest[...] = rest_own[...]


def send_third_kernel(
    below_mid, above_mid, qkv_below, qkv_above, rest_own, rest_swapped, backs, up, down, message_up, message_down, backs_out
):
    stack(up, below_mid[:HALF, :], backs[...])
    stack(down, above_mid[HALF:ROWS, :], backs[...])
    pair = rest_own[:, :FC], rest_swapped[:, :FC]
    beside(message_up, pair, qkv_below[:ROWS, :])
    beside(message_down, pair, qkv_above[ROWS:, :])
    backs_out[...] = backs[...]


def send_fourth_kernel(
    below_last,
    above_last,
    message_below,
    message_above,
    backs_swapped,
    rest_own,
    rest_swapped,
    qkv_pair,
    qkv_below,
    qkv_above,
    up,
    down,
    message_up,
    message_down,
    qkv_mine,
):
    stack(up, backs_swapped[...], below_last[HALF:ROWS, :])
    stack(down, backs_swapped[...], above_last[ROWS:, :])
    pair = rest_own[:, FC:], rest_swapped[:, FC:]
    beside(message_up, pair, message_below[:ROWS, :FC])
    beside(message_down, pair, message_above[ROWS:, :FC])
    stack(qkv_mine, qkv_pair[...], qkv_above[...], apart(message_below, FC), apart(message_above, FC), qkv_below[...])


def send_fifth_kernel(
    below_backs,
    above_backs,
    own_first,
    below_first,
    above_first,
    own_second,
    below_second,
    above_second,
    up,
    down,
    far_up,
    far_down,
    fc1_mine,
    back_mine,
):
    up[...] = below_backs[:HALF, :]
    down[...] = above_backs[HALF:ROWS, :]
    columns = HC + FC
    far_up[...] = below_second[:ROWS, :columns]
    far_down[...] = above_second[ROWS:, :columns]
    stack(
        fc1_mine,
        own_first[:, :FC],
        above_first[:, :FC],
        apart(below_second, columns),
        apart(above_second, columns),
        below_first[:, :FC],
    )
    stack(back_mine, own_second[:, :columns], above_second[:, :columns], below_second[:, :columns])


def send_sixth_kernel(far, far_swapped, mine):
    stack(mine, far[...], far_swapped[...])


PLACES, BACK_PLACES, FIRST_PLACES, SECOND_PLACES, ROW_PLACES, GROUPS, OWN_X, OWN_H = (0, 16, 32, 40, 48, 56, 60, 61)


def position_table():
    table = np.zeros((128, 64), np.int32)
    for dp in range(16):
        x, y, core = dp // 8, dp // 2 % 4, dp % 2

        def block(step, other_x, c):
            return ((x ^ other_x) * 4 + (y + step) % 4) * 2 + c

        def gathered(steps):
            return [block(step, o, c) for c in (core, 1 - core) for step in steps for o in (0, 1)]

        def grads(c):
            return [(xx * 4 + (y + step) % 4) * 2 + c for step in (2, 1, 3, 0) for xx in (0, 1)]

        for tensor in range(8):
            z, h = tensor // 2, tensor % 2

            def row(step, other):
                return (z + step) % 4 * 2 + (h ^ other)

            rows = [row(0, 0), row(0, 1), row(3, 0), row(1, 0), row(3, 1), row(1, 1), row(2, 0), row(2, 1)]
            groups = [(z + step) % 4 for step in (2, 1, 3, 0)]
            table[dp * 8 + tensor] = [
                *gathered((0, 1, 2, 3)),
                *gathered((0, 1, 3, 2)),
                *grads(1 - core),
                *grads(core),
                *rows,
                *groups,
                x,
                h,
                0,
                0,
            ]
    return table


class At:
    def __init__(self, info, first):
        self.info, self.first = info, first

    def __getitem__(self, i):
        return self.info[self.first + i]


EXTRA = 16


def coded(sums):
    high = sums.astype(BF)
    low = (sums - high.astype(F32)).astype(BF)
    rest = jnp.zeros((EXTRA - 2 * sums.shape[0], sums.shape[1]), F32)
    return jnp.concatenate([high.astype(F32), low.astype(F32), rest], 0).astype(BF)


def decoded(block):
    block = block.astype(F32)
    return block[:3] + block[3:6]


def near_kernel(above, below, from_below, from_above, up, down):
    up[:ROWS, :] = (above[:ROWS, :].astype(F32) + from_below[:ROWS, :].astype(F32)).astype(BF)
    up[ROWS:256, :] = above[ROWS:, :]
    down[:ROWS, :] = below[:ROWS, :]
    down[ROWS:, :] = (below[ROWS:, :].astype(F32) + from_above[:ROWS, :].astype(F32)).astype(BF)
    if up.shape[0] > 256:
        up[256:, :] = from_below[ROWS:, :]


def near(above, below, from_below, from_above, deps=()):
    columns, more = above.shape[1], from_below.shape[0] - ROWS
    return call(near_kernel, [shape(256 + more, columns), shape(256, columns)], 10, deps=deps)(
        above, below, from_below, from_above
    )


def last_kernel(info, here, got_up, got_down, kept, sent):
    own = At(info, OWN_H)[0]
    for out, which in ((kept, own), (sent, 1 - own)):
        at = pl.ds(pl.multiple_of(which * ROWS, ROWS), ROWS)
        total = here[at, :].astype(F32) + got_up[at, :].astype(F32) + got_down[at, :].astype(F32)
        out[...] = total.astype(out.dtype)


def last(info, here, got_up, got_down, deps=()):
    columns = here.shape[1]
    return call(
        last_kernel, [shape(ROWS, columns, F32), shape(ROWS, columns)], 10, [SMEM] + [VMEM] * 3, deps=deps
    )(info, here, got_up, got_down)


def grad_last_kernel(info, here, got_up, got_down, sums, from_below, from_above, kept, sent, total_sums):
    last_kernel(info, here, got_up, got_down, kept, sent.at[:ROWS])
    total = sums[...] + decoded(from_below[ROWS:, :]) + decoded(from_above[ROWS:, :]) + decoded(got_up[256:, :])
    total_sums[...] = total
    sent[ROWS:, :] = coded(total)


def grad_last(info, here, got_up, got_down, sums, from_below, from_above, deps=()):
    outs = [shape(ROWS, D, F32), shape(ROWS + EXTRA, D), shape(3, D, F32)]
    return call(grad_last_kernel, outs, 12, [SMEM] + [VMEM] * 6, deps=deps)(
        info, here, got_up, got_down, sums, from_below, from_above
    )


def small_kernel(sums, got, projected, hidden, out):
    out[:3, :] = sums[...] + decoded(got[ROWS:, :])
    rest = jnp.zeros((1, D - 3 * HC - FC), F32)
    out[3:, :] = jnp.concatenate([projected[...], hidden[...], rest], 1)


def plus(mine, got):
    return mine.astype(F32) + got.astype(F32)


def weight_far_kernel(mine, got, first, second):
    total = plus(mine[...], got[0]).astype(BF)
    first[...] = total[:ROWS]
    second[...] = total[ROWS:]


def weight_far(mine, got, deps=()):
    columns = mine[0].shape[1]
    spec, held = part(got, 0)
    return call(weight_far_kernel, [shape(ROWS, columns)] * 2, 14, [VMEM, spec], deps=deps)(mine[0], held)


def weight_near_kernel(above, below, got_above, got_below, from_below, from_above, up, down):
    columns = above.shape[1]
    up[:ROWS, :columns] = (plus(above[:ROWS, :], got_above[0, :ROWS]) + from_below[...].astype(F32)).astype(BF)
    up[ROWS:, :columns] = plus(above[ROWS:, :], got_above[0, ROWS:]).astype(BF)
    down[:ROWS, :columns] = plus(below[:ROWS, :], got_below[0, :ROWS]).astype(BF)
    down[ROWS:, :columns] = (plus(below[ROWS:, :], got_below[0, ROWS:]) + from_above[...].astype(F32)).astype(BF)


def first_near_kernel(above, below, got_above, got_below, from_below, from_above, front, front_got, up, down):
    weight_near_kernel(above, below, got_above, got_below, from_below, from_above, up, down)
    columns = above.shape[1]
    far = plus(front[...], front_got[0]).astype(BF)
    middle = far.shape[1] // 2
    for message, rows in ((up, far[:ROWS]), (down, far[ROWS:])):
        message[:ROWS, columns:] = rows[:, :middle]
        message[ROWS:, columns:] = rows[:, middle:]


def first_near(mine, got, from_below, from_above, front, front_got, deps=()):
    columns, more = mine[0].shape[1], front[0].shape[1]
    (spec, above), (spec2, below), (spec3, far) = part(got, 1), part(got, 2), part(front_got, 0)
    specs = [VMEM, VMEM, spec, spec2, VMEM, VMEM, VMEM, spec3]
    return call(first_near_kernel, [shape(256, columns + more // 2)] * 2, 22, specs, deps=deps)(
        mine[1], mine[2], above, below, from_below, from_above, front[0], far
    )


def second_near_kernel(above, below, got_above, got_below, message_below, message_above, up, down):
    columns = message_below.shape[1] - above.shape[1] // 2
    far = apart(message_below, columns), apart(message_above, columns)
    weight_near_kernel(above, below, got_above, got_below, *far, up, down)


def second_near(mine, got, message_below, message_above, deps=()):
    (spec, above), (spec2, below) = part(got, 1), part(got, 2)
    specs = [VMEM, VMEM, spec, spec2, VMEM, VMEM]
    return call(second_near_kernel, [shape(256, mine[0].shape[1])] * 2, 22, specs, deps=deps)(
        mine[1], mine[2], above, below, message_below, message_above
    )


def weight_last_kernel(info, mine, got, got_up, got_down, kept, sent):
    columns, own = mine.shape[1], At(info, OWN_X)[0]
    for out, which in ((kept, own), (sent, 1 - own)):
        at = pl.ds(pl.multiple_of(which * ROWS, ROWS), ROWS)
        total = plus(mine[at, :], got[0, at, :]) + plus(got_up[at, :columns], got_down[at, :columns])
        out[...] = total.astype(out.dtype)


def weight_last(info, mine, got, got_up, got_down, deps=()):
    columns = mine[0].shape[1]
    spec, here = part(got, 3)
    specs = [SMEM, VMEM, spec, VMEM, VMEM]
    return call(weight_last_kernel, [shape(ROWS, columns, F32), shape(ROWS, columns)], 16, specs, deps=deps)(
        info, mine[3], here, got_up, got_down
    )


def add_kernel(first, *refs):
    total = first[...]
    for ref in refs[:-1]:
        total = total + ref[...]
    refs[-1][...] = total


def added(*values, deps=()):
    return call(add_kernel, jax.ShapeDtypeStruct(values[0].shape, F32), 4, deps=deps)(*values)


def send(v, axes, perm):
    return lax.ppermute(v, axes, perm)


def rotary_tables():
    half = ROT // 2
    position = np.arange(LEN, dtype=np.float32)
    frequency = np.float32(10000.0) ** (-np.arange(half, dtype=np.float32) * np.float32(2.0 / ROT))
    angle = (position[:, None] * frequency[None, :].astype(np.float32)).astype(np.float32)
    cosine, sine = np.cos(angle), np.sin(angle)
    rest = np.ones((LEN, HD - ROT), np.float32)
    none = np.zeros((LEN, half), np.float32)
    same = np.concatenate([cosine, cosine, rest] * 2, 1)
    ahead = np.concatenate([-sine, none, 0 * rest] * 2, 1)
    behind = np.concatenate([none, sine, 0 * rest] * 2, 1)
    return jnp.asarray(np.concatenate([same, ahead, behind], 1).astype(np.float32))


def rotated(values, tables, sign):
    wide = [jnp.concatenate([tables[:, j * 128 : (j + 1) * 128]] * 2, 1) for j in range(3)]
    half = ROT // 2
    return values * wide[0] + sign * (
        pltpu.roll(values, HC - half, 1) * wide[1] + pltpu.roll(values, half, 1) * wide[2]
    )


WIDE = 256
SPLIT = 2


def assemble_kernel(first, info, *refs):
    places, out = At(info, first), refs[-1]
    done = 0
    for source in refs[:-1]:
        for i in range(source.shape[0] // ROWS):
            start = pl.multiple_of(places[done] * ROWS, ROWS)
            out[pl.ds(start, ROWS), :] = source[i * ROWS : (i + 1) * ROWS, :]
            done += 1


def assembled(first, info, *sources, deps=()):
    specs = [SMEM] + [VMEM] * len(sources)
    return call(
        functools.partial(assemble_kernel, first),
        shape(D, sources[0].shape[1]),
        LIMITS["assemble"],
        specs,
        us=2.0,
        deps=deps,
    )(info, *sources)


def qkv_kernel(rows, weights, bias, tables, heads):
    for j in range(3):
        part = slice(j * HC, (j + 1) * HC)
        pre = nn(rows[...], weights[:, part]) + bias[j : j + 1]
        heads[:, part] = (rotated(pre, tables, 1.0) if j < 2 else pre).astype(BF)


def qkv_call(normed, weights, bias, tables, deps=()):
    return call(qkv_kernel, shape(LEN, 3 * HC), LIMITS["qkv"], us=TIMES["qkv"], deps=deps)(normed, weights, bias, tables)


ROOT = 0.7978845608028654
CUBIC = 0.044715


def hidden_kernel(rows, weights, bias, activated, slope):
    for j in range(FC // WIDE):
        part = slice(j * WIDE, (j + 1) * WIDE)
        hidden = nn(rows[...], weights[:, part]) + bias[:, part]
        square = hidden * hidden
        bent = jnp.tanh(ROOT * (hidden + CUBIC * (square * hidden)))
        half = 0.5 * (1.0 + bent)
        activated[:, part] = (hidden * half).astype(BF)
        slope[:, part] = (
            half + (0.5 * ROOT) * hidden * (1.0 - bent * bent) * (1.0 + (3.0 * CUBIC) * square)
        ).astype(BF)


def hidden_call(normed, weights, bias, deps=()):
    return call(hidden_kernel, [shape(LEN, FC)] * 2, LIMITS["hidden"], us=TIMES["hidden"], deps=deps)(
        normed, weights, bias.reshape(1, FC)
    )


PART_SHAPES = [shape(ROWS, D)] * 2 + [shape(256, D)] * 3


def store_part(refs, r, columns, part):
    if r == 0:
        refs[0][:ROWS, columns] = part[:ROWS]
        refs[1][:ROWS, columns] = part[ROWS:]
    else:
        refs[r + 1][:, columns] = part


def out_kernel(info, attended, activated, weights, *parts):
    groups = At(info, GROUPS)
    for r in range(4):
        here = pl.ds(pl.multiple_of(groups[r] * 256, 256), 256)
        rows = jnp.concatenate([attended[here, :], activated[here, :]], 1)
        store_part(parts, r, slice(0, D), nt(rows, weights[...]).astype(BF))


def out_call(info, attended, activated, weights, deps=()):
    return call(out_kernel, PART_SHAPES, LIMITS["out"], [SMEM] + [VMEM] * 3, us=TIMES["out"], deps=deps)(
        info, attended, activated, weights
    )


def grad_kernel(backs, slope, weights, grad_attended, grad_hidden, sums):
    for j in range((HC + FC) // WIDE):
        grad = nn(backs[...], weights[:, j * WIDE : (j + 1) * WIDE])
        if j == 0:
            grad_attended[...] = grad.astype(BF)
        else:
            part = slice((j - 1) * WIDE, j * WIDE)
            low = (grad * slope[:, part].astype(F32)).astype(BF)
            grad_hidden[:, part] = low
            sums[:, part] = jnp.sum(low.astype(F32), 0, keepdims=True)


def grad_call(backs, slope, weights, deps=()):
    return call(
        grad_kernel, [shape(LEN, HC), shape(LEN, FC), shape(1, FC, F32)], LIMITS["grad"], us=TIMES["grad"], deps=deps
    )(backs, slope, weights)


def normed_kernel(info, projected, hidden, rows, stats, weights, weights2, back_sums, *refs):
    parts, sums = refs[:5], refs[5]
    groups = At(info, GROUPS)
    for n in range(2):
        part = slice(n * D // 2, (n + 1) * D // 2)
        first = second = None
        for r in range(4):
            here = pl.ds(pl.multiple_of(groups[r] * 256, 256), 256)
            grad = nt(projected[here, :], weights[part, :]) + nt(hidden[here, :], weights2[part, :])
            store_part(parts, r, part, grad.astype(BF))
            standard = (rows[here, part].astype(F32) - stats[here, 0:1]) * stats[here, 64:65]
            term, plain = jnp.sum(grad * standard, 0, keepdims=True), jnp.sum(grad, 0, keepdims=True)
            first, second = (term, plain) if r == 0 else (first + term, second + plain)
        sums[0:1, part] = first
        sums[1:2, part] = second
    sums[2:3, :] = back_sums[...]
    block = coded(sums[...])
    for ref in parts[:2]:
        ref[ROWS:, :] = block


def normed_call(info, projected, hidden, rows, stats, weights, weights2, back_sums, deps=()):
    return call(
        normed_kernel,
        [shape(ROWS + EXTRA, D)] * 2 + PART_SHAPES[2:] + [shape(3, D, F32)],
        LIMITS["normed"],
        [SMEM] + [VMEM] * 7,
        us=TIMES["normed"],
        deps=deps,
    )(info, projected, hidden, rows, stats, weights, weights2, back_sums)


def weight_kernel(counts, parts, first, info, *refs):
    places, outs, refs = At(info, first), refs[-parts:], list(refs[:-parts])
    outs = [outs[k * parts // 4].at[k % (4 // parts)] for k in range(4)] if parts < 4 else outs
    done = 0
    for count in counts:
        left, rights, refs = refs[0], refs[1 : 1 + count], refs[1 + count :]
        for step in range(2):
            turned = jnp.concatenate(
                [left[:, pl.ds(pl.multiple_of(places[4 * step + j] * ROWS, ROWS), ROWS)] for j in range(4)], 1
            ).T
            column = done
            for right in rights:
                for j in range(right.shape[1] // WIDE):
                    term = nn(turned, right[:, j * WIDE : (j + 1) * WIDE]).astype(BF)
                    outs[2 * step][:, column : column + WIDE] = term[:256]
                    outs[2 * step + 1][:, column : column + WIDE] = term[256:]
                    column += WIDE
        done = column


def weight_call(parts, first, info, *terms, deps=()):
    columns = sum(r.shape[1] for term in terms for r in term[1:])
    flat = [r for term in terms for r in term]
    outs = [jax.ShapeDtypeStruct((4 // parts, 256, columns), BF)] * parts if parts < 4 else [shape(256, columns)] * 4
    return call(
        functools.partial(weight_kernel, [len(term) - 1 for term in terms], parts, first),
        outs,
        LIMITS["weight"],
        [SMEM] + [VMEM] * len(flat),
        us=TIMES["weight"] * columns / 2304,
        deps=deps,
    )(info, *flat)


def nt(left, right):
    return lax.dot_general(left, right, (((1,), (1,)), ((), ())), preferred_element_type=F32)


def nn(left, right):
    return lax.dot_general(left, right, (((1,), (0,)), ((), ())), preferred_element_type=F32)


POWER = SCALE * 1.4426950408889634


def by_head(block, lane):
    return jnp.concatenate([jnp.where(lane == h, block, jnp.zeros((), BF)) for h in range(HEADS)], 0)


def seen_mask():
    key = lax.broadcasted_iota(jnp.int32, (BQ, BQ), 0)
    query = lax.broadcasted_iota(jnp.int32, (BQ, BQ), 1)
    return jnp.concatenate([key <= query] * HEADS, 1)


def forward_kernel(heads, attended, logsum, out_t, values_t):
    queries, keys, values = (heads.at[:, j * HC : (j + 1) * HC] for j in range(3))
    values_t[...] = values[...].T
    lane = lax.broadcasted_iota(jnp.int32, (BQ, HC), 1) // HD
    seen = seen_mask()
    for q in range(LEN // BQ):
        here = slice(q * BQ, (q + 1) * BQ)
        query = by_head(queries[here, :], lane)
        blocks = []
        largest = None
        for k in range(q + 1):
            block = nt(keys[k * BQ : (k + 1) * BQ, :], query)
            if k == q:
                block = jnp.where(seen, block, -1e30)
            blocks.append(block)
            top = jnp.max(block, 0, keepdims=True)
            largest = top if largest is None else jnp.maximum(largest, top)
        total = jnp.zeros((1, HEADS * BQ), F32)
        found = [jnp.zeros((HD, BQ), F32)] * HEADS
        for k in range(q + 1):
            powers = jnp.exp2((blocks[k] - largest) * POWER)
            total = total + jnp.sum(powers, 0, keepdims=True)
            low = powers.astype(BF)
            for h in range(HEADS):
                found[h] = found[h] + nn(
                    values_t[h * HD : (h + 1) * HD, k * BQ : (k + 1) * BQ], low[:, h * BQ : (h + 1) * BQ]
                )
        scale = 1.0 / total
        base = largest * POWER + jnp.log2(total)
        for h in range(HEADS):
            out_t[h * HD : (h + 1) * HD, here] = found[h] * scale[:, h * BQ : (h + 1) * BQ]
            logsum[h : h + 1, here] = base[:, h * BQ : (h + 1) * BQ]
    attended[...] = out_t[...].T.astype(BF)


def forward_call(heads, deps=()):
    return call(
        forward_kernel,
        [shape(LEN, HC), shape(8, LEN, F32), shape(HC, LEN, F32)],
        LIMITS["forward"],
        scratch_shapes=[pltpu.VMEM((HC, LEN), BF)],
        us=TIMES["forward"],
        deps=deps,
    )(heads)


def backward_kernel(
    heads, grads, logsum, out_t, tables, out, sums, keys_t, query_grads, key_grads, value_grads
):
    queries, keys, values = (heads.at[:, j * HC : (j + 1) * HC] for j in range(3))
    keys_t[...] = keys[...].T
    turned = grads[...].astype(F32).T * out_t[...]
    lane = lax.broadcasted_iota(jnp.int32, (BQ, HC), 1) // HD
    seen = seen_mask()
    for q in reversed(range(LEN // BQ)):
        here = slice(q * BQ, (q + 1) * BQ)
        query = by_head(queries[here, :], lane)
        grad = by_head(grads[here, :], lane)
        base = jnp.concatenate([logsum[h : h + 1, here] for h in range(HEADS)], 1)
        dots = jnp.concatenate(
            [jnp.sum(turned[h * HD : (h + 1) * HD, here], 0, keepdims=True) for h in range(HEADS)], 1
        )
        found = [jnp.zeros((HD, BQ), F32)] * HEADS
        for k in range(q + 1):
            there = slice(k * BQ, (k + 1) * BQ)
            probs = jnp.exp2(nt(keys[there, :], query) * POWER - base)
            if k == q:
                probs = jnp.where(seen, probs, 0.0)
            score = (probs * (nt(values[there, :], grad) - dots)).astype(BF)
            value_grad, key_grad = nn(probs.astype(BF), grad), nn(score, query)
            if q == LEN // BQ - 1:
                value_grads[there, :] = value_grad
                key_grads[there, :] = key_grad
            else:
                value_grads[there, :] += value_grad
                key_grads[there, :] += key_grad
            for h in range(HEADS):
                found[h] = found[h] + nn(
                    keys_t[h * HD : (h + 1) * HD, there], score[:, h * BQ : (h + 1) * BQ]
                )
        for h in range(HEADS):
            query_grads[h * HD : (h + 1) * HD, here] = found[h]
    parts = (
        rotated(query_grads[...].T * SCALE, tables, -1.0),
        rotated(key_grads[...] * SCALE, tables, -1.0),
        value_grads[...],
    )
    for j, part in enumerate(parts):
        low = part.astype(BF)
        out[:, j * HC : (j + 1) * HC] = low
        sums[:, j * HC : (j + 1) * HC] = jnp.sum(low.astype(F32), 0, keepdims=True)


def backward_call(heads, grads, logsum, out_t, tables, deps=()):
    return call(
        backward_kernel,
        [shape(LEN, 3 * HC), shape(1, 3 * HC, F32)],
        LIMITS["backward"],
        scratch_shapes=[pltpu.VMEM((HC, LEN), BF), pltpu.VMEM((HC, LEN), F32)] + [pltpu.VMEM((LEN, HC), F32)] * 2,
        us=TIMES["backward"],
        deps=deps,
    )(heads, grads, logsum, out_t, tables)


def adamw(param, grad, first, second, rate, decay):
    first_new = BETA_ONE * first + (1.0 - BETA_ONE) * grad
    second_new = BETA_TWO * second + (1.0 - BETA_TWO) * grad * grad
    ratio = (
        first_new
        / (1.0 - BETA_ONE**STEP)
        / (jnp.sqrt(second_new / (1.0 - BETA_TWO**STEP)) + ADAM_EPSILON)
    )
    return (grad, first_new, second_new, param - rate * (ratio + decay * param))


def side_by_side(stack):
    return jnp.concatenate([stack[j] for j in range(stack.shape[0])], 1)


def per_device(
    tokens,
    cotangent,
    attn_weight,
    mlp_weight,
    qkv_bias,
    fc1_bias,
    vectors,
    attn_first,
    mlp_first,
    qkv_first,
    fc1_first,
    vector_first,
    attn_second,
    mlp_second,
    qkv_second,
    fc1_second,
    vector_second,
):
    dp = lax.axis_index("dp")
    tensor = lax.axis_index("tensor")
    info = lax.dynamic_index_in_dim(jnp.asarray(position_table()), dp * 8 + tensor, 0, keepdims=False)
    tables = rotary_tables()
    qkv_own = side_by_side(attn_weight[:3].astype(BF))
    rest_own = jnp.concatenate([mlp_weight[0], attn_weight[3], mlp_weight[1]], 1).astype(BF)

    columns = HC + FC

    back_sum = jnp.sum(cotangent.astype(F32), 0, keepdims=True)

    swapped = swap_h(tokens)
    below_own, above_own = up_z(tokens), down_z(tokens)
    qkv_swapped = swap_x(qkv_own)
    sent = call(
        send_second_kernel, [shape(192, D)] * 2 + [shape(256, 3 * HC), shape(ROWS, HC + 2 * FC)], LIMITS["send"], deps=(info, back_sum)
    )(swapped, below_own, above_own, qkv_own, qkv_swapped, rest_own)
    below_mid, above_mid = up_z(sent[0]), down_z(sent[1])
    qkv_pair = sent[2]
    qkv_below, qkv_above = up_y(qkv_pair), down_y(qkv_pair)
    rest_swapped = swap_x(sent[3])
    normed_a = call(norm_first_kernel, [shape(512, D), shape(512, 128, F32)], 8, deps=(qkv_pair,))(
        tokens, swapped, below_own, above_own, vectors
    )
    sent = call(
        send_third_kernel,
        [shape(192, D)] * 2 + [shape(256, FC + 3 * HC // 2)] * 2 + [shape(ROWS, D)],
        LIMITS["send"],
        deps=(normed_a[1],),
    )(below_mid, above_mid, qkv_below, qkv_above, rest_own, rest_swapped, cotangent)
    below_last, above_last = up_z(sent[0]), down_z(sent[1])
    own_first = sent[2]
    below_first, above_first = up_y(sent[2]), down_y(sent[3])
    backs_swapped = swap_h(sent[4])
    normed_b = call(norm_second_kernel, [shape(384, D), shape(384, 128, F32)], 8, deps=(own_first,))(
        below_mid, above_mid, vectors
    )
    sent = call(
        send_fourth_kernel,
        [shape(192, D)] * 2 + [shape(256, columns + FC // 2)] * 2 + [shape(8 * ROWS, 3 * HC)],
        LIMITS["send"],
        deps=(normed_b[1],),
    )(
        below_last,
        above_last,
        below_first,
        above_first,
        backs_swapped,
        rest_own,
        rest_swapped,
        qkv_pair,
        qkv_below,
        qkv_above,
    )
    below_backs, above_backs = up_z(sent[0]), down_z(sent[1])
    own_second = sent[2]
    below_second, above_second = up_y(sent[2]), down_y(sent[3])
    qkv_mine = sent[4]
    qkv_other = swap_core(qkv_mine)
    normed, stats = call(
        norm_last_kernel, [shape(LEN, D), shape(LEN, 128, F32)], 12, [SMEM] + [VMEM] * 7, deps=(qkv_mine,)
    )(info, below_last, above_last, vectors, *normed_a, *normed_b)
    qkv_full = assembled(PLACES, info, qkv_mine, qkv_other, deps=(stats,))
    heads = qkv_call(normed, qkv_full, qkv_bias, tables)
    attended, logsum, attended_t = forward_call(heads)
    sent = call(
        send_fifth_kernel,
        [shape(HALF, D)] * 2 + [shape(ROWS, columns)] * 2 + [shape(8 * ROWS, FC), shape(6 * ROWS, columns)],
        LIMITS["send"],
        deps=(logsum,),
    )(below_backs, above_backs, own_first, below_first, above_first, own_second, below_second, above_second)
    first_backs, second_backs = up_z(sent[0]), down_z(sent[1])
    back_far, back_far_swapped = up_y(sent[2]), down_y(sent[3])
    fc1_mine, back_mine = sent[4:]
    fc1_other = swap_core(fc1_mine)
    back_other = swap_core(back_mine)
    rows = rows_call(
        0,
        info,
        tokens,
        swapped,
        below_own,
        above_own,
        below_mid,
        above_mid,
        below_last,
        above_last,
        deps=(fc1_mine,),
    )
    fc1_full = assembled(PLACES, info, fc1_mine, fc1_other, deps=(rows,))
    activated, slope = hidden_call(normed, fc1_full, fc1_bias)
    far_mine = call(
        send_sixth_kernel, shape(256, columns), LIMITS["send"], deps=(slope, first_backs, second_backs, back_other)
    )(back_far, back_far_swapped)
    far_other = swap_core(far_mine)
    backs = rows_call(
        HALF,
        info,
        cotangent,
        backs_swapped,
        below_last,
        above_last,
        below_backs,
        above_backs,
        first_backs,
        second_backs,
        deps=(far_mine,),
    )
    back_full = assembled(BACK_PLACES, info, back_mine, far_mine, back_other, far_other, deps=(backs,))
    out_parts = out_call(info, attended, activated, back_full)
    from_below, from_above = up_z(out_parts[0]), down_z(out_parts[1])
    grad_attended, grad_hidden, hidden_sums = grad_call(backs, slope, back_full, deps=(out_parts[0],))
    back = (backs, attended, activated)
    (back_other,) = weight_call(1, FIRST_PLACES, info, back, deps=(hidden_sums,))
    up, down = near(out_parts[2], out_parts[3], from_below, from_above, deps=(back_other,))
    got_up, got_down = up_z(up), down_z(down)
    back_got = (swap_core(tied(back_other, up)),)
    projected, projected_sums = backward_call(heads, grad_attended, logsum, attended_t, tables, deps=(up,))
    back_mine = weight_call(4, SECOND_PLACES, info, back, deps=(projected_sums,))
    front = (normed, projected, grad_hidden)
    front_other = weight_call(SPLIT, FIRST_PLACES, info, front, deps=(back_mine[0],))
    back_far = weight_far(back_mine, back_got, deps=(front_other[0],))
    back_below, back_above = up_y(back_far[0]), down_y(back_far[1])
    *normed_parts, normed_sums = normed_call(
        info, projected, grad_hidden, rows, stats, qkv_full, fc1_full, back_sum, deps=(back_far[0], got_up, got_down)
    )
    from_below, from_above = up_z(normed_parts[0]), down_z(normed_parts[1])
    front_got = [swap_core(v) for v in front_other]
    front_mine = weight_call(4, SECOND_PLACES, info, front, deps=(normed_parts[0],))
    out_own, out_sent = last(info, out_parts[4], got_up, got_down, deps=(front_mine[0],))
    out_got = swap_h(out_sent)
    far_below, far_above = from_below, from_above
    up, down = near(normed_parts[2], normed_parts[3], from_below, from_above, deps=(out_sent, back_below, back_above))
    got_up, got_down = up_z(up), down_z(down)
    sent = first_near(back_mine, back_got, back_below, back_above, front_mine, front_got, deps=(up, front_got[1]))
    back_up, back_down = up_y(sent[0]), down_y(sent[1])
    local = tokens.astype(F32)
    out = (local + (out_own + out_got.astype(F32)) + vectors[2] + vectors[3]).astype(BF)
    grad_own, grad_sent, sums = grad_last(
        info, normed_parts[4], got_up, got_down, normed_sums, far_below, far_above, deps=(out_got,)
    )
    grad_got = swap_h(grad_sent)
    sent = second_near(front_mine, front_got, back_up, back_down, deps=(grad_sent,))
    front_up, front_down = up_y(sent[0]), down_y(sent[1])
    back_own, back_sent = weight_last(info, back_mine, back_got, back_up, back_down, deps=(sent[0],))
    back_last = swap_x(back_sent)
    small = call(small_kernel, shape(4, D, F32), 4, deps=(back_last,))(sums, grad_got, projected_sums, hidden_sums)
    small = added(small, send(small, "dp", CORE_SWAP))
    front_own, front_sent = weight_last(
        info, front_mine, front_got, front_up, front_down, deps=(grad_got, back_last, small)
    )
    front_last = swap_x(front_sent)
    small = added(
        small, *(send(tied(small, front_sent), "dp", perm) for perm in (Y_UP, Y_DOWN, Y_FAR)), deps=(front_last,)
    )
    small = added(small, send(small, "dp", X_SWAP))
    vector_sum, bias_sum = small[:3], small[3]
    grad_normed = grad_own + grad_got[:ROWS].astype(F32)
    back_grad = back_own + back_last.astype(F32)
    front_grad = front_own + front_last.astype(F32)

    local_centred = local - jnp.mean(local, -1, keepdims=True)
    local_inverse = lax.rsqrt(jnp.mean(local_centred * local_centred, -1, keepdims=True) + EPSILON)
    local_standard = local_centred * local_inverse
    back_local = cotangent.astype(F32)
    grad_standard = grad_normed * vectors[0]
    input_grad = back_local + local_inverse * (
        grad_standard
        - jnp.mean(grad_standard, -1, keepdims=True)
        - local_standard * jnp.mean(grad_standard * local_standard, -1, keepdims=True)
    )

    vector_grad = jnp.concatenate([vector_sum, vector_sum[2:3]], 0)

    attn_grad = jnp.stack(
        [front_grad[:, :HC], front_grad[:, HC : 2 * HC], front_grad[:, 2 * HC : 3 * HC], back_grad[:, :HC]]
    )
    mlp_grad = jnp.stack([front_grad[:, 3 * HC :], back_grad[:, HC:]])
    qkv_grad = bias_sum[: 3 * HC].reshape(3, HC)
    fc1_grad = bias_sum[3 * HC : 3 * HC + FC]
    attn_out = adamw(attn_weight, attn_grad, attn_first, attn_second, 0.04, 0.1)
    mlp_out = adamw(mlp_weight, mlp_grad, mlp_first, mlp_second, 0.04, 0.1)
    qkv_out = adamw(qkv_bias, qkv_grad, qkv_first, qkv_second, 0.3, 0.0)
    fc1_out = adamw(fc1_bias, fc1_grad, fc1_first, fc1_second, 0.3, 0.0)
    vector_out = adamw(vectors, vector_grad, vector_first, vector_second, 0.2, 0.0)
    return (out, input_grad, *attn_out, *mlp_out, *qkv_out, *fc1_out, *vector_out)


def solution(mesh):
    rows = P(("dp", "tensor"), None)
    weight = P(None, "dp", "tensor")
    qkv = P(None, "tensor")
    fc1 = P("tensor")
    return jax.shard_map(
        per_device,
        mesh=mesh,
        in_specs=(rows, rows, weight, weight, qkv, fc1, P()) + (weight, weight, qkv, fc1, P()) * 2,
        out_specs=(rows, rows) + (weight,) * 8 + (qkv,) * 4 + (fc1,) * 4 + (P(),) * 4,
        check_vma=False,
    )
```

```python
import functools

import jax
import jax.numpy as jnp
import numpy as np
from jax import lax
from jax.experimental import pallas as pl
from jax.experimental.pallas import tpu as pltpu
from jax.sharding import PartitionSpec as P

D = 2048
HD = 64
ROT = 32
LEN = 1024
STEP = 10
HEADS = 4
HC = HEADS * HD
FC = 1024
ROWS = 128
HALF = ROWS // 2
BQ = 256

EPSILON = 1e-05
SCALE = 0.125
BETA_ONE = 0.9
BETA_TWO = 0.999
ADAM_EPSILON = 1e-08
BF = jnp.bfloat16
LIMITS = dict(send=8, assemble=5, qkv=7, hidden=9, out=9, grad=8, normed=11, weight=6, forward=11, backward=12)
TIMES = dict(qkv=4.0, hidden=6.0, out=6.0, grad=5.5, normed=9.0, weight=5.0, forward=5.0, backward=8.0)
DECLARED = 0.3
F32 = jnp.float32


def dp_perm(move):
    pairs = []
    for x in range(2):
        for y in range(4):
            for c in range(2):
                nx, ny, nc = move(x, y, c)
                pairs.append(((x * 4 + y) * 2 + c, (nx * 4 + ny % 4) * 2 + nc))
    return pairs


def tensor_perm(move):
    pairs = []
    for z in range(4):
        for h in range(2):
            nz, nh = move(z, h)
            pairs.append((z * 2 + h, (nz % 4) * 2 + nh))
    return pairs


Y_UP = dp_perm(lambda x, y, c: (x, y + 1, c))
Y_DOWN = dp_perm(lambda x, y, c: (x, y - 1, c))
X_SWAP = dp_perm(lambda x, y, c: (1 - x, y, c))
CORE_SWAP = dp_perm(lambda x, y, c: (x, y, 1 - c))
Z_UP = tensor_perm(lambda z, h: (z + 1, h))
Z_DOWN = tensor_perm(lambda z, h: (z - 1, h))
Y_FAR = dp_perm(lambda x, y, c: (x, y + 2, c))
Z_FAR = tensor_perm(lambda z, h: (z + 2, h))
H_SWAP = tensor_perm(lambda z, h: (z, 1 - h))


def at(array, index, axis):
    return lax.dynamic_index_in_dim(array, index, axis, keepdims=False)


def up_z(v):
    return lax.ppermute(v, "tensor", Z_UP)


def down_z(v):
    return lax.ppermute(v, "tensor", Z_DOWN)


def swap_h(v):
    return lax.ppermute(v, "tensor", H_SWAP)


def up_y(v):
    return lax.ppermute(v, "dp", Y_UP)


def down_y(v):
    return lax.ppermute(v, "dp", Y_DOWN)


def swap_x(v):
    return lax.ppermute(v, "dp", X_SWAP)


def swap_core(v):
    return lax.ppermute(v, "dp", CORE_SWAP)


SMEM = pl.BlockSpec(memory_space=pltpu.SMEM)
VMEM = pl.BlockSpec(memory_space=pltpu.VMEM)


ANY = pl.BlockSpec(memory_space=pl.ANY)


def part(arrays, k):
    for held in arrays:
        if k < held.shape[0]:
            return pl.BlockSpec((1, *held.shape[1:]), lambda i: (k, 0, 0)), held
        k -= held.shape[0]


def call(kernel, out_shape, mebibytes, in_specs=None, scratch_shapes=(), us=1.0, deps=()):
    def run(*args):
        specs = list(in_specs or [VMEM] * len(args))
        gridded = any(spec.index_map is not None for spec in specs)

        def fit(spec, array):
            if gridded and spec is VMEM:
                return pl.BlockSpec(array.shape, lambda i: (0,) * len(array.shape))
            return spec

        def body(*refs):
            kernel(*refs[: len(args)], *refs[len(args) + len(deps) :])

        return pl.pallas_call(
            body,
            out_shape=out_shape,
            grid=(1,) if gridded else (),
            out_specs=jax.tree.map(lambda out: fit(VMEM, out), out_shape),
            in_specs=[fit(spec, arg) for spec, arg in zip(specs, args)] + [ANY] * len(deps),
            scratch_shapes=scratch_shapes,
            compiler_params=pltpu.CompilerParams(vmem_limit_bytes=mebibytes * 1024 * 1024),
            cost_estimate=pl.CostEstimate(
                flops=int(us * DECLARED * 1.1e9), bytes_accessed=1000, transcendentals=0
            ),
        )(*args, *deps)

    return run


def nothing_kernel(*refs):
    pass


def tied(value, *deps):
    return pl.pallas_call(
        nothing_kernel,
        out_shape=jax.ShapeDtypeStruct(value.shape, value.dtype),
        in_specs=[ANY] * (1 + len(deps)),
        out_specs=ANY,
        input_output_aliases={0: 0},
        compiler_params=pltpu.CompilerParams(vmem_limit_bytes=1024 * 1024),
        cost_estimate=pl.CostEstimate(flops=1000, bytes_accessed=1000, transcendentals=0),
    )(value, *deps)


def shape(rows, columns, dtype=BF):
    return jax.ShapeDtypeStruct((rows, columns), dtype)


def normalized(block, vectors, normed, stats, at):
    inputs = block.astype(F32)
    mean = jnp.mean(inputs, -1, keepdims=True)
    centred = inputs - mean
    inverse = lax.rsqrt(jnp.mean(centred * centred, -1, keepdims=True) + EPSILON)
    normed[at, :] = (centred * inverse * vectors[0:1, :] + vectors[1:2, :]).astype(BF)
    lane = lax.broadcasted_iota(jnp.int32, (ROWS, 128), 1)
    stats[at, :] = jnp.where(lane < 64, mean, inverse)


def norm_first_kernel(own, swapped, below, above, vectors, normed, stats):
    for i, block in enumerate((own, swapped, below, above)):
        normalized(block[...], vectors, normed, stats, slice(i * ROWS, (i + 1) * ROWS))


def norm_second_kernel(below, above, vectors, normed, stats):
    far = jnp.concatenate([below[ROWS:, :], above[ROWS:, :]], 0)
    for i, block in enumerate((below[:ROWS, :], above[:ROWS, :], far)):
        normalized(block, vectors, normed, stats, slice(i * ROWS, (i + 1) * ROWS))


def norm_last_kernel(info, below, above, vectors, normed_a, stats_a, normed_b, stats_b, normed, stats):
    places = At(info, ROW_PLACES)
    at = [pl.ds(pl.multiple_of(places[i] * ROWS, ROWS), ROWS) for i in range(8)]
    normalized(jnp.concatenate([below[:HALF, :], above[:HALF, :]], 0), vectors, normed, stats, at[7])
    for i in range(7):
        held, held_stats, k = (normed_a, stats_a, i) if i < 4 else (normed_b, stats_b, i - 4)
        normed[at[i], :] = held[k * ROWS : (k + 1) * ROWS, :]
        stats[at[i], :] = held_stats[k * ROWS : (k + 1) * ROWS, :]


def rows_kernel(skipped, info, own, swapped, below, above, below_mid, above_mid, first, second, rows):
    places = At(info, ROW_PLACES)
    far = jnp.concatenate([below_mid[ROWS:, :], above_mid[ROWS:, :]], 0)
    last = jnp.concatenate([first[:HALF, :], second[:HALF, :]], 0)
    near = [ref[skipped : skipped + ROWS, :] for ref in (below, above)]
    blocks = (own[...], swapped[...], *near, below_mid[:ROWS, :], above_mid[:ROWS, :], far, last)
    for i, block in enumerate(blocks):
        rows[pl.ds(pl.multiple_of(places[i] * ROWS, ROWS), ROWS), :] = block


def rows_call(skipped, info, *blocks, deps=()):
    return call(
        functools.partial(rows_kernel, skipped), shape(LEN, D), 12, [SMEM] + [VMEM] * 8, deps=deps
    )(info, *blocks)


def beside(message, wide, rows):
    done = 0
    for piece in wide:
        message[done : done + piece.shape[0], : piece.shape[1]] = piece
        done += piece.shape[0]
    columns, middle = wide[0].shape[1], rows.shape[1] // 2
    message[:ROWS, columns:] = rows[:, :middle]
    message[ROWS:, columns:] = rows[:, middle:]


def apart(message, columns):
    return jnp.concatenate([message[:ROWS, columns:], message[ROWS:, columns:]], 1)


def stack(out, *pieces):
    done = 0
    for piece in pieces:
        out[done : done + piece.shape[0], :] = piece
        done += piece.shape[0]


def send_second_kernel(swapped, below, above, qkv_own, qkv_swapped, rest_own, up, down, pair, rest):
    stack(up, swapped[...], below[:HALF, :])
    stack(down, swapped[...], above[HALF:, :])
    stack(pair, qkv_own[...], qkv_swapped[...])
    rest[...] = rest_own[...]


def send_third_kernel(
    below_mid, above_mid, qkv_below, qkv_above, rest_own, rest_swapped, backs, up, down, message_up, message_down, backs_out
):
    stack(up, below_mid[:HALF, :], backs[...])
    stack(down, above_mid[HALF:ROWS, :], backs[...])
    pair = rest_own[:, :FC], rest_swapped[:, :FC]
    beside(message_up, pair, qkv_below[:ROWS, :])
    beside(message_down, pair, qkv_above[ROWS:, :])
    backs_out[...] = backs[...]


def send_fourth_kernel(
    below_last,
    above_last,
    message_below,
    message_above,
    backs_swapped,
    rest_own,
    rest_swapped,
    qkv_pair,
    qkv_below,
    qkv_above,
    up,
    down,
    message_up,
    message_down,
    qkv_mine,
):
    stack(up, backs_swapped[...], below_last[HALF:ROWS, :])
    stack(down, backs_swapped[...], above_last[ROWS:, :])
    pair = rest_own[:, FC:], rest_swapped[:, FC:]
    beside(message_up, pair, message_below[:ROWS, :FC])
    beside(message_down, pair, message_above[ROWS:, :FC])
    stack(qkv_mine, qkv_pair[...], qkv_above[...], apart(message_below, FC), apart(message_above, FC), qkv_below[...])


def send_fifth_kernel(
    below_backs,
    above_backs,
    own_first,
    below_first,
    above_first,
    own_second,
    below_second,
    above_second,
    up,
    down,
    far_up,
    far_down,
    fc1_mine,
    back_mine,
):
    up[...] = below_backs[:HALF, :]
    down[...] = above_backs[HALF:ROWS, :]
    columns = HC + FC
    far_up[...] = below_second[:ROWS, :columns]
    far_down[...] = above_second[ROWS:, :columns]
    stack(
        fc1_mine,
        own_first[:, :FC],
        above_first[:, :FC],
        apart(below_second, columns),
        apart(above_second, columns),
        below_first[:, :FC],
    )
    stack(back_mine, own_second[:, :columns], above_second[:, :columns], below_second[:, :columns])


def send_sixth_kernel(far, far_swapped, mine):
    stack(mine, far[...], far_swapped[...])


PLACES, BACK_PLACES, FIRST_PLACES, SECOND_PLACES, ROW_PLACES, GROUPS, OWN_X, OWN_H = (0, 16, 32, 40, 48, 56, 60, 61)


def position_table():
    table = np.zeros((128, 64), np.int32)
    for dp in range(16):
        x, y, core = dp // 8, dp // 2 % 4, dp % 2

        def block(step, other_x, c):
            return ((x ^ other_x) * 4 + (y + step) % 4) * 2 + c

        def gathered(steps):
            return [block(step, o, c) for c in (core, 1 - core) for step in steps for o in (0, 1)]

        def grads(c):
            return [(xx * 4 + (y + step) % 4) * 2 + c for step in (2, 1, 3, 0) for xx in (0, 1)]

        for tensor in range(8):
            z, h = tensor // 2, tensor % 2

            def row(step, other):
                return (z + step) % 4 * 2 + (h ^ other)

            rows = [row(0, 0), row(0, 1), row(3, 0), row(1, 0), row(3, 1), row(1, 1), row(2, 0), row(2, 1)]
            groups = [(z + step) % 4 for step in (2, 1, 3, 0)]
            table[dp * 8 + tensor] = [
                *gathered((0, 1, 2, 3)),
                *gathered((0, 1, 3, 2)),
                *grads(1 - core),
                *grads(core),
                *rows,
                *groups,
                x,
                h,
                0,
                0,
            ]
    return table


class At:
    def __init__(self, info, first):
        self.info, self.first = info, first

    def __getitem__(self, i):
        return self.info[self.first + i]


EXTRA = 16


def coded(sums):
    high = sums.astype(BF)
    low = (sums - high.astype(F32)).astype(BF)
    rest = jnp.zeros((EXTRA - 2 * sums.shape[0], sums.shape[1]), F32)
    return jnp.concatenate([high.astype(F32), low.astype(F32), rest], 0).astype(BF)


def decoded(block):
    block = block.astype(F32)
    return block[:3] + block[3:6]


def near_kernel(above, below, from_below, from_above, *refs):
    up, down = refs[-2:]
    up[:ROWS, :] = (above[:ROWS, :].astype(F32) + from_below[...].astype(F32)).astype(BF)
    up[ROWS:256, :] = above[ROWS:, :]
    down[:ROWS, :] = below[:ROWS, :]
    down[ROWS:256, :] = (below[ROWS:, :].astype(F32) + from_above[...].astype(F32)).astype(BF)
    if len(refs) > 2:
        block = coded(refs[0][:3, :])
        up[256:, :] = block
        down[256:, :] = block


def near(above, below, from_below, from_above, *sums, deps=()):
    rows = 256 + EXTRA * len(sums)
    return call(near_kernel, [shape(rows, above.shape[1])] * 2, 12, deps=deps)(
        above, below, from_below, from_above, *sums
    )


def last_kernel(info, here, got_up, got_down, kept, sent):
    own = At(info, OWN_H)[0]
    for out, which in ((kept, own), (sent, 1 - own)):
        at = pl.ds(pl.multiple_of(which * ROWS, ROWS), ROWS)
        total = here[at, :].astype(F32) + got_up[at, :].astype(F32) + got_down[at, :].astype(F32)
        out[...] = total.astype(out.dtype)


def last(info, here, got_up, got_down, deps=()):
    columns = here.shape[1]
    return call(
        last_kernel, [shape(ROWS, columns, F32), shape(ROWS, columns)], 10, [SMEM] + [VMEM] * 3, deps=deps
    )(info, here, got_up, got_down)


def grad_last_kernel(info, here, got_up, got_down, sums, far_sums, kept, sent, total_sums):
    last_kernel(info, here, got_up, got_down, kept, sent.at[:ROWS])
    total = sums[:3, :] + far_sums[:3, :] + decoded(got_up[256:, :]) + decoded(got_down[256:, :])
    total_sums[...] = total
    sent[ROWS:, :] = coded(total)


def grad_last(info, here, got_up, got_down, sums, far_sums, deps=()):
    outs = [shape(ROWS, D, F32), shape(ROWS + EXTRA, D), shape(3, D, F32)]
    return call(grad_last_kernel, outs, 12, [SMEM] + [VMEM] * 5, deps=deps)(
        info, here, got_up, got_down, sums, far_sums
    )


def small_kernel(sums, got, projected, hidden, out):
    out[:3, :] = sums[...] + decoded(got[ROWS:, :])
    rest = jnp.zeros((1, D - 3 * HC - FC), F32)
    out[3:, :] = jnp.concatenate([projected[...], hidden[...], rest], 1)


def plus(mine, got):
    return mine.astype(F32) + got.astype(F32)


def weight_far_kernel(mine, got, first, second):
    total = plus(mine[0], got[0]).astype(BF)
    first[...] = total[:ROWS]
    second[...] = total[ROWS:]


def weight_far(mine, got, deps=()):
    columns = mine[0].shape[2]
    spec, held = part(got, 0)
    return call(weight_far_kernel, [shape(ROWS, columns)] * 2, 14, [VMEM, spec], deps=deps)(mine[0], held)


def weight_near_kernel(above, below, got_above, got_below, from_below, from_above, up, down):
    columns = above.shape[2]
    up[:ROWS, :columns] = (plus(above[0, :ROWS], got_above[0, :ROWS]) + from_below[...].astype(F32)).astype(BF)
    up[ROWS:, :columns] = plus(above[0, ROWS:], got_above[0, ROWS:]).astype(BF)
    down[:ROWS, :columns] = plus(below[0, :ROWS], got_below[0, :ROWS]).astype(BF)
    down[ROWS:, :columns] = (plus(below[0, ROWS:], got_below[0, ROWS:]) + from_above[...].astype(F32)).astype(BF)


def first_near_kernel(above, below, got_above, got_below, from_below, from_above, front, front_got, up, down):
    weight_near_kernel(above, below, got_above, got_below, from_below, from_above, up, down)
    columns = above.shape[2]
    far = plus(front[0], front_got[0]).astype(BF)
    middle = far.shape[1] // 2
    for message, rows in ((up, far[:ROWS]), (down, far[ROWS:])):
        message[:ROWS, columns:] = rows[:, :middle]
        message[ROWS:, columns:] = rows[:, middle:]


def first_near(mine, got, from_below, from_above, front, front_got, deps=()):
    columns, more = mine[0].shape[2], front[0].shape[2]
    (spec, above), (spec2, below), (spec3, far) = part(got, 1), part(got, 2), part(front_got, 0)
    specs = [VMEM, VMEM, spec, spec2, VMEM, VMEM, VMEM, spec3]
    return call(first_near_kernel, [shape(256, columns + more // 2)] * 2, 22, specs, deps=deps)(
        mine[1], mine[2], above, below, from_below, from_above, front[0], far
    )


def second_near_kernel(above, below, got_above, got_below, message_below, message_above, up, down):
    columns = message_below.shape[1] - above.shape[2] // 2
    far = apart(message_below, columns), apart(message_above, columns)
    weight_near_kernel(above, below, got_above, got_below, *far, up, down)


def second_near(mine, got, message_below, message_above, deps=()):
    (spec, above), (spec2, below) = part(got, 1), part(got, 2)
    specs = [VMEM, VMEM, spec, spec2, VMEM, VMEM]
    return call(second_near_kernel, [shape(256, mine[0].shape[2])] * 2, 22, specs, deps=deps)(
        mine[1], mine[2], above, below, message_below, message_above
    )


def weight_last_kernel(info, mine, got, got_up, got_down, kept, sent):
    columns, own = mine.shape[2], At(info, OWN_X)[0]
    for out, which in ((kept, own), (sent, 1 - own)):
        at = pl.ds(pl.multiple_of(which * ROWS, ROWS), ROWS)
        total = plus(mine[0, at, :], got[0, at, :]) + plus(got_up[at, :columns], got_down[at, :columns])
        out[...] = total.astype(out.dtype)


def weight_last(info, mine, got, got_up, got_down, deps=()):
    columns = mine[0].shape[2]
    spec, here = part(got, 3)
    specs = [SMEM, VMEM, spec, VMEM, VMEM]
    return call(weight_last_kernel, [shape(ROWS, columns, F32), shape(ROWS, columns)], 16, specs, deps=deps)(
        info, mine[3], here, got_up, got_down
    )


def add_kernel(first, *refs):
    total = first[...]
    for ref in refs[:-1]:
        total = total + ref[...]
    refs[-1][...] = total


def added(*values, deps=()):
    return call(add_kernel, jax.ShapeDtypeStruct(values[0].shape, F32), 4, deps=deps)(*values)


def send(v, axes, perm):
    return lax.ppermute(v, axes, perm)


def rotary_tables():
    half = ROT // 2
    position = np.arange(LEN, dtype=np.float32)
    frequency = np.float32(10000.0) ** (-np.arange(half, dtype=np.float32) * np.float32(2.0 / ROT))
    angle = (position[:, None] * frequency[None, :].astype(np.float32)).astype(np.float32)
    cosine, sine = np.cos(angle), np.sin(angle)
    rest = np.ones((LEN, HD - ROT), np.float32)
    none = np.zeros((LEN, half), np.float32)
    same = np.concatenate([cosine, cosine, rest] * 2, 1)
    ahead = np.concatenate([-sine, none, 0 * rest] * 2, 1)
    behind = np.concatenate([none, sine, 0 * rest] * 2, 1)
    return jnp.asarray(np.concatenate([same, ahead, behind], 1).astype(np.float32))


def rotated(values, tables, sign):
    wide = [jnp.concatenate([tables[:, j * 128 : (j + 1) * 128]] * 2, 1) for j in range(3)]
    half = ROT // 2
    return values * wide[0] + sign * (
        pltpu.roll(values, HC - half, 1) * wide[1] + pltpu.roll(values, half, 1) * wide[2]
    )


WIDE = 256


def assemble_kernel(first, info, *refs):
    places, out = At(info, first), refs[-1]
    done = 0
    for source in refs[:-1]:
        for i in range(source.shape[0] // ROWS):
            start = pl.multiple_of(places[done] * ROWS, ROWS)
            out[pl.ds(start, ROWS), :] = source[i * ROWS : (i + 1) * ROWS, :]
            done += 1


def assembled(first, info, *sources, deps=()):
    specs = [SMEM] + [VMEM] * len(sources)
    return call(
        functools.partial(assemble_kernel, first),
        shape(D, sources[0].shape[1]),
        LIMITS["assemble"],
        specs,
        us=2.0,
        deps=deps,
    )(info, *sources)


def qkv_kernel(rows, weights, bias, tables, heads):
    for j in range(3):
        part = slice(j * HC, (j + 1) * HC)
        pre = nn(rows[...], weights[:, part]) + bias[j : j + 1]
        heads[:, part] = (rotated(pre, tables, 1.0) if j < 2 else pre).astype(BF)


def qkv_call(normed, weights, bias, tables, deps=()):
    return call(qkv_kernel, shape(LEN, 3 * HC), LIMITS["qkv"], us=TIMES["qkv"], deps=deps)(normed, weights, bias, tables)


ROOT = 0.7978845608028654
CUBIC = 0.044715


def hidden_kernel(rows, weights, bias, activated, slope):
    for j in range(FC // WIDE):
        part = slice(j * WIDE, (j + 1) * WIDE)
        hidden = nn(rows[...], weights[:, part]) + bias[:, part]
        square = hidden * hidden
        bent = jnp.tanh(ROOT * (hidden + CUBIC * (square * hidden)))
        half = 0.5 * (1.0 + bent)
        activated[:, part] = (hidden * half).astype(BF)
        slope[:, part] = (
            half + (0.5 * ROOT) * hidden * (1.0 - bent * bent) * (1.0 + (3.0 * CUBIC) * square)
        ).astype(BF)


def hidden_call(normed, weights, bias, deps=()):
    return call(hidden_kernel, [shape(LEN, FC)] * 2, LIMITS["hidden"], us=TIMES["hidden"], deps=deps)(
        normed, weights, bias.reshape(1, FC)
    )


PART_SHAPES = [shape(ROWS, D)] * 2 + [shape(256, D)] * 3


def store_part(refs, r, columns, part):
    if r == 0:
        refs[0][:ROWS, columns] = part[:ROWS]
        refs[1][:ROWS, columns] = part[ROWS:]
    else:
        refs[r + 1][:, columns] = part


def out_kernel(info, attended, activated, weights, *parts):
    groups = At(info, GROUPS)
    for r in range(4):
        here = pl.ds(pl.multiple_of(groups[r] * 256, 256), 256)
        rows = jnp.concatenate([attended[here, :], activated[here, :]], 1)
        store_part(parts, r, slice(0, D), nt(rows, weights[...]).astype(BF))


def out_call(info, attended, activated, weights, deps=()):
    return call(out_kernel, PART_SHAPES, LIMITS["out"], [SMEM] + [VMEM] * 3, us=TIMES["out"], deps=deps)(
        info, attended, activated, weights
    )


def grad_kernel(backs, slope, weights, grad_attended, grad_hidden, sums):
    for j in range((HC + FC) // WIDE):
        grad = nn(backs[...], weights[:, j * WIDE : (j + 1) * WIDE])
        if j == 0:
            grad_attended[...] = grad.astype(BF)
        else:
            part = slice((j - 1) * WIDE, j * WIDE)
            low = (grad * slope[:, part].astype(F32)).astype(BF)
            grad_hidden[:, part] = low
            sums[:, part] = jnp.sum(low.astype(F32), 0, keepdims=True)


def grad_call(backs, slope, weights, deps=()):
    return call(
        grad_kernel, [shape(LEN, HC), shape(LEN, FC), shape(1, FC, F32)], LIMITS["grad"], us=TIMES["grad"], deps=deps
    )(backs, slope, weights)


def normed_kernel(steps, info, projected, hidden, rows, stats, weights, weights2, before, *refs):
    parts, sums = refs[:-1], refs[-1]
    groups = At(info, GROUPS)
    for n in range(2):
        columns = slice(n * D // 2, (n + 1) * D // 2)
        first, second = before[0:1, columns], before[1:2, columns]
        for i, r in enumerate(steps):
            here = pl.ds(pl.multiple_of(groups[r] * 256, 256), 256)
            grad = nt(projected[here, :], weights[columns, :]) + nt(hidden[here, :], weights2[columns, :])
            low = grad.astype(BF)
            if r == 0:
                parts[0][:, columns] = low[:ROWS]
                parts[1][:, columns] = low[ROWS:]
            else:
                parts[i][:, columns] = low
            standard = (rows[here, columns].astype(F32) - stats[here, 0:1]) * stats[here, 64:65]
            first = first + jnp.sum(grad * standard, 0, keepdims=True)
            second = second + jnp.sum(grad, 0, keepdims=True)
        sums[0:1, columns] = first
        sums[1:2, columns] = second
    sums[2:, :] = before[2:, :]


def normed_call(steps, info, projected, hidden, rows, stats, weights, weights2, before, deps=()):
    parts = [shape(ROWS, D)] * 2 if steps == (0,) else [shape(256, D)] * len(steps)
    return call(
        functools.partial(normed_kernel, steps),
        parts + [shape(4, D, F32)],
        LIMITS["normed"],
        [SMEM] + [VMEM] * 7,
        us=TIMES["normed"] * len(steps) / 4,
        deps=deps,
    )(info, projected, hidden, rows, stats, weights, weights2, before)


def weight_kernel(counts, parts, first, info, *refs):
    places, outs, refs = At(info, first), refs[-len(parts) :], list(refs[: -len(parts)])
    outs = [ref.at[k] for ref, size in zip(outs, parts) for k in range(size)]
    done = 0
    for count in counts:
        left, rights, refs = refs[0], refs[1 : 1 + count], refs[1 + count :]
        for step in range(2):
            turned = jnp.concatenate(
                [left[:, pl.ds(pl.multiple_of(places[4 * step + j] * ROWS, ROWS), ROWS)] for j in range(4)], 1
            ).T
            column = done
            for right in rights:
                for j in range(right.shape[1] // WIDE):
                    term = nn(turned, right[:, j * WIDE : (j + 1) * WIDE]).astype(BF)
                    outs[2 * step][:, column : column + WIDE] = term[:256]
                    outs[2 * step + 1][:, column : column + WIDE] = term[256:]
                    column += WIDE
        done = column


def weight_call(parts, first, info, *terms, deps=()):
    columns = sum(r.shape[1] for term in terms for r in term[1:])
    flat = [r for term in terms for r in term]
    outs = [jax.ShapeDtypeStruct((size, 256, columns), BF) for size in parts]
    return call(
        functools.partial(weight_kernel, [len(term) - 1 for term in terms], parts, first),
        outs,
        LIMITS["weight"],
        [SMEM] + [VMEM] * len(flat),
        us=TIMES["weight"] * columns / 2304,
        deps=deps,
    )(info, *flat)


def nt(left, right):
    return lax.dot_general(left, right, (((1,), (1,)), ((), ())), preferred_element_type=F32)


def nn(left, right):
    return lax.dot_general(left, right, (((1,), (0,)), ((), ())), preferred_element_type=F32)


POWER = SCALE * 1.4426950408889634


def by_head(block, lane):
    return jnp.concatenate([jnp.where(lane == h, block, jnp.zeros((), BF)) for h in range(HEADS)], 0)


def seen_mask():
    key = lax.broadcasted_iota(jnp.int32, (BQ, BQ), 0)
    query = lax.broadcasted_iota(jnp.int32, (BQ, BQ), 1)
    return jnp.concatenate([key <= query] * HEADS, 1)


def forward_kernel(heads, attended, logsum, out_t, values_t):
    queries, keys, values = (heads.at[:, j * HC : (j + 1) * HC] for j in range(3))
    values_t[...] = values[...].T
    lane = lax.broadcasted_iota(jnp.int32, (BQ, HC), 1) // HD
    seen = seen_mask()
    for q in range(LEN // BQ):
        here = slice(q * BQ, (q + 1) * BQ)
        query = by_head(queries[here, :], lane)
        blocks = []
        largest = None
        for k in range(q + 1):
            block = nt(keys[k * BQ : (k + 1) * BQ, :], query)
            if k == q:
                block = jnp.where(seen, block, -1e30)
            blocks.append(block)
            top = jnp.max(block, 0, keepdims=True)
            largest = top if largest is None else jnp.maximum(largest, top)
        total = jnp.zeros((1, HEADS * BQ), F32)
        found = [jnp.zeros((HD, BQ), F32)] * HEADS
        for k in range(q + 1):
            powers = jnp.exp2((blocks[k] - largest) * POWER)
            total = total + jnp.sum(powers, 0, keepdims=True)
            low = powers.astype(BF)
            for h in range(HEADS):
                found[h] = found[h] + nn(
                    values_t[h * HD : (h + 1) * HD, k * BQ : (k + 1) * BQ], low[:, h * BQ : (h + 1) * BQ]
                )
        scale = 1.0 / total
        base = largest * POWER + jnp.log2(total)
        for h in range(HEADS):
            out_t[h * HD : (h + 1) * HD, here] = found[h] * scale[:, h * BQ : (h + 1) * BQ]
            logsum[h : h + 1, here] = base[:, h * BQ : (h + 1) * BQ]
    attended[...] = out_t[...].T.astype(BF)


def forward_call(heads, deps=()):
    return call(
        forward_kernel,
        [shape(LEN, HC), shape(8, LEN, F32), shape(HC, LEN, F32)],
        LIMITS["forward"],
        scratch_shapes=[pltpu.VMEM((HC, LEN), BF)],
        us=TIMES["forward"],
        deps=deps,
    )(heads)


def backward_kernel(
    heads, grads, logsum, out_t, tables, out, sums, keys_t, query_grads, key_grads, value_grads
):
    queries, keys, values = (heads.at[:, j * HC : (j + 1) * HC] for j in range(3))
    keys_t[...] = keys[...].T
    turned = grads[...].astype(F32).T * out_t[...]
    lane = lax.broadcasted_iota(jnp.int32, (BQ, HC), 1) // HD
    seen = seen_mask()
    for q in reversed(range(LEN // BQ)):
        here = slice(q * BQ, (q + 1) * BQ)
        query = by_head(queries[here, :], lane)
        grad = by_head(grads[here, :], lane)
        base = jnp.concatenate([logsum[h : h + 1, here] for h in range(HEADS)], 1)
        dots = jnp.concatenate(
            [jnp.sum(turned[h * HD : (h + 1) * HD, here], 0, keepdims=True) for h in range(HEADS)], 1
        )
        found = [jnp.zeros((HD, BQ), F32)] * HEADS
        for k in range(q + 1):
            there = slice(k * BQ, (k + 1) * BQ)
            probs = jnp.exp2(nt(keys[there, :], query) * POWER - base)
            if k == q:
                probs = jnp.where(seen, probs, 0.0)
            score = (probs * (nt(values[there, :], grad) - dots)).astype(BF)
            value_grad, key_grad = nn(probs.astype(BF), grad), nn(score, query)
            if q == LEN // BQ - 1:
                value_grads[there, :] = value_grad
                key_grads[there, :] = key_grad
            else:
                value_grads[there, :] += value_grad
                key_grads[there, :] += key_grad
            for h in range(HEADS):
                found[h] = found[h] + nn(
                    keys_t[h * HD : (h + 1) * HD, there], score[:, h * BQ : (h + 1) * BQ]
                )
        for h in range(HEADS):
            query_grads[h * HD : (h + 1) * HD, here] = found[h]
    parts = (
        rotated(query_grads[...].T * SCALE, tables, -1.0),
        rotated(key_grads[...] * SCALE, tables, -1.0),
        value_grads[...],
    )
    for j, part in enumerate(parts):
        low = part.astype(BF)
        out[:, j * HC : (j + 1) * HC] = low
        sums[:, j * HC : (j + 1) * HC] = jnp.sum(low.astype(F32), 0, keepdims=True)


def backward_call(heads, grads, logsum, out_t, tables, deps=()):
    return call(
        backward_kernel,
        [shape(LEN, 3 * HC), shape(1, 3 * HC, F32)],
        LIMITS["backward"],
        scratch_shapes=[pltpu.VMEM((HC, LEN), BF), pltpu.VMEM((HC, LEN), F32)] + [pltpu.VMEM((LEN, HC), F32)] * 2,
        us=TIMES["backward"],
        deps=deps,
    )(heads, grads, logsum, out_t, tables)


def adamw(param, grad, first, second, rate, decay):
    first_new = BETA_ONE * first + (1.0 - BETA_ONE) * grad
    second_new = BETA_TWO * second + (1.0 - BETA_TWO) * grad * grad
    ratio = (
        first_new
        / (1.0 - BETA_ONE**STEP)
        / (jnp.sqrt(second_new / (1.0 - BETA_TWO**STEP)) + ADAM_EPSILON)
    )
    return (grad, first_new, second_new, param - rate * (ratio + decay * param))


def side_by_side(stack):
    return jnp.concatenate([stack[j] for j in range(stack.shape[0])], 1)


def per_device(
    tokens,
    cotangent,
    attn_weight,
    mlp_weight,
    qkv_bias,
    fc1_bias,
    vectors,
    attn_first,
    mlp_first,
    qkv_first,
    fc1_first,
    vector_first,
    attn_second,
    mlp_second,
    qkv_second,
    fc1_second,
    vector_second,
):
    dp = lax.axis_index("dp")
    tensor = lax.axis_index("tensor")
    info = lax.dynamic_index_in_dim(jnp.asarray(position_table()), dp * 8 + tensor, 0, keepdims=False)
    tables = rotary_tables()
    qkv_own = side_by_side(attn_weight[:3].astype(BF))
    rest_own = jnp.concatenate([mlp_weight[0], attn_weight[3], mlp_weight[1]], 1).astype(BF)

    columns = HC + FC

    back_sum = jnp.pad(jnp.sum(cotangent.astype(F32), 0, keepdims=True), ((2, 1), (0, 0)))

    swapped = swap_h(tokens)
    below_own, above_own = up_z(tokens), down_z(tokens)
    qkv_swapped = swap_x(qkv_own)
    sent = call(
        send_second_kernel, [shape(192, D)] * 2 + [shape(256, 3 * HC), shape(ROWS, HC + 2 * FC)], LIMITS["send"], deps=(info, back_sum)
    )(swapped, below_own, above_own, qkv_own, qkv_swapped, rest_own)
    below_mid, above_mid = up_z(sent[0]), down_z(sent[1])
    qkv_pair = sent[2]
    qkv_below, qkv_above = up_y(qkv_pair), down_y(qkv_pair)
    rest_swapped = swap_x(sent[3])
    normed_a = call(norm_first_kernel, [shape(512, D), shape(512, 128, F32)], 8, deps=(qkv_pair,))(
        tokens, swapped, below_own, above_own, vectors
    )
    sent = call(
        send_third_kernel,
        [shape(192, D)] * 2 + [shape(256, FC + 3 * HC // 2)] * 2 + [shape(ROWS, D)],
        LIMITS["send"],
        deps=(normed_a[1],),
    )(below_mid, above_mid, qkv_below, qkv_above, rest_own, rest_swapped, cotangent)
    below_last, above_last = up_z(sent[0]), down_z(sent[1])
    own_first = sent[2]
    below_first, above_first = up_y(sent[2]), down_y(sent[3])
    backs_swapped = swap_h(sent[4])
    normed_b = call(norm_second_kernel, [shape(384, D), shape(384, 128, F32)], 8, deps=(own_first,))(
        below_mid, above_mid, vectors
    )
    sent = call(
        send_fourth_kernel,
        [shape(192, D)] * 2 + [shape(256, columns + FC // 2)] * 2 + [shape(8 * ROWS, 3 * HC)],
        LIMITS["send"],
        deps=(normed_b[1],),
    )(
        below_last,
        above_last,
        below_first,
        above_first,
        backs_swapped,
        rest_own,
        rest_swapped,
        qkv_pair,
        qkv_below,
        qkv_above,
    )
    below_backs, above_backs = up_z(sent[0]), down_z(sent[1])
    own_second = sent[2]
    below_second, above_second = up_y(sent[2]), down_y(sent[3])
    qkv_mine = sent[4]
    qkv_other = swap_core(qkv_mine)
    normed, stats = call(
        norm_last_kernel, [shape(LEN, D), shape(LEN, 128, F32)], 12, [SMEM] + [VMEM] * 7, deps=(qkv_mine,)
    )(info, below_last, above_last, vectors, *normed_a, *normed_b)
    qkv_full = assembled(PLACES, info, qkv_mine, qkv_other, deps=(stats,))
    heads = qkv_call(normed, qkv_full, qkv_bias, tables)
    attended, logsum, attended_t = forward_call(heads)
    sent = call(
        send_fifth_kernel,
        [shape(HALF, D)] * 2 + [shape(ROWS, columns)] * 2 + [shape(8 * ROWS, FC), shape(6 * ROWS, columns)],
        LIMITS["send"],
        deps=(logsum,),
    )(below_backs, above_backs, own_first, below_first, above_first, own_second, below_second, above_second)
    first_backs, second_backs = up_z(sent[0]), down_z(sent[1])
    back_far, back_far_swapped = up_y(sent[2]), down_y(sent[3])
    fc1_mine, back_mine = sent[4:]
    fc1_other = swap_core(fc1_mine)
    back_other = swap_core(back_mine)
    rows = rows_call(
        0,
        info,
        tokens,
        swapped,
        below_own,
        above_own,
        below_mid,
        above_mid,
        below_last,
        above_last,
        deps=(fc1_mine,),
    )
    fc1_full = assembled(PLACES, info, fc1_mine, fc1_other, deps=(rows,))
    activated, slope = hidden_call(normed, fc1_full, fc1_bias)
    far_mine = call(
        send_sixth_kernel, shape(256, columns), LIMITS["send"], deps=(slope, first_backs, second_backs, back_other)
    )(back_far, back_far_swapped)
    far_other = swap_core(far_mine)
    backs = rows_call(
        HALF,
        info,
        cotangent,
        backs_swapped,
        below_last,
        above_last,
        below_backs,
        above_backs,
        first_backs,
        second_backs,
        deps=(far_mine,),
    )
    back_full = assembled(BACK_PLACES, info, back_mine, far_mine, back_other, far_other, deps=(backs,))
    out_parts = out_call(info, attended, activated, back_full)
    from_below, from_above = up_z(out_parts[0]), down_z(out_parts[1])
    grad_attended, grad_hidden, hidden_sums = grad_call(backs, slope, back_full, deps=(out_parts[0],))
    back = (backs, attended, activated)
    (back_other,) = weight_call((4,), FIRST_PLACES, info, back, deps=(hidden_sums,))
    up, down = near(out_parts[2], out_parts[3], from_below, from_above, deps=(back_other,))
    got_up, got_down = up_z(up), down_z(down)
    back_got = (swap_core(tied(back_other, up)),)
    projected, projected_sums = backward_call(heads, grad_attended, logsum, attended_t, tables, deps=(up,))
    back_mine = weight_call((1, 1, 1, 1), SECOND_PLACES, info, back, deps=(projected_sums,))
    front = (normed, projected, grad_hidden)
    front_other = weight_call((1, 1, 1, 1), FIRST_PLACES, info, front, deps=(back_mine[0], *back_got))
    back_far = weight_far(back_mine, back_got, deps=(front_other[0],))
    back_below, back_above = up_y(back_far[0]), down_y(back_far[1])
    front_got = [swap_core(v) for v in front_other[:3]]
    front_mine = weight_call((1, 1, 1, 1), SECOND_PLACES, info, front, deps=(front_other[0],))
    terms = (info, projected, grad_hidden, rows, stats, qkv_full, fc1_full)
    *far_parts, far_sums = normed_call((0,), *terms, back_sum, deps=(back_far[0], front_mine[0], got_up, got_down))
    from_below, from_above = up_z(far_parts[0]), down_z(far_parts[1])
    *normed_parts, normed_sums = normed_call((1, 2, 3), *terms, far_sums, deps=front_got)
    out_own, out_sent = last(info, out_parts[4], got_up, got_down, deps=(normed_sums,))
    out_got = swap_h(out_sent)
    up, down = near(
        normed_parts[0], normed_parts[1], from_below, from_above, normed_sums, deps=(out_sent, back_below, back_above)
    )
    got_up, got_down = up_z(up), down_z(down)
    far_sums = send(tied(normed_sums, up, out_got), "tensor", Z_FAR)
    sent = first_near(back_mine, back_got, back_below, back_above, front_mine, front_got, deps=(up,))
    back_up, back_down = up_y(sent[0]), down_y(sent[1])
    local = tokens.astype(F32)
    out = (local + (out_own + out_got.astype(F32)) + vectors[2] + vectors[3]).astype(BF)
    grad_own, grad_sent, sums = grad_last(
        info, normed_parts[2], got_up, got_down, normed_sums, far_sums, deps=(out_got,)
    )
    grad_got = swap_h(grad_sent)
    sent = second_near(front_mine, front_got, back_up, back_down, deps=(grad_sent,))
    front_up, front_down = up_y(sent[0]), down_y(sent[1])
    back_own, back_sent = weight_last(info, back_mine, back_got, back_up, back_down, deps=(sent[0],))
    back_last = swap_x(back_sent)
    front_got.append(swap_core(tied(front_other[3], back_last)))
    small = call(small_kernel, shape(4, D, F32), 4, deps=(back_last,))(sums, grad_got, projected_sums, hidden_sums)
    small = added(small, send(small, "dp", CORE_SWAP))
    front_own, front_sent = weight_last(
        info, front_mine, front_got, front_up, front_down, deps=(grad_got, back_last, small)
    )
    front_last = swap_x(front_sent)
    small = added(
        small, *(send(tied(small, front_sent), "dp", perm) for perm in (Y_UP, Y_DOWN, Y_FAR)), deps=(front_last,)
    )
    small = added(small, send(small, "dp", X_SWAP))
    vector_sum, bias_sum = small[:3], small[3]
    grad_normed = grad_own + grad_got[:ROWS].astype(F32)
    back_grad = back_own + back_last.astype(F32)
    front_grad = front_own + front_last.astype(F32)

    local_centred = local - jnp.mean(local, -1, keepdims=True)
    local_inverse = lax.rsqrt(jnp.mean(local_centred * local_centred, -1, keepdims=True) + EPSILON)
    local_standard = local_centred * local_inverse
    back_local = cotangent.astype(F32)
    grad_standard = grad_normed * vectors[0]
    input_grad = back_local + local_inverse * (
        grad_standard
        - jnp.mean(grad_standard, -1, keepdims=True)
        - local_standard * jnp.mean(grad_standard * local_standard, -1, keepdims=True)
    )

    vector_grad = jnp.concatenate([vector_sum, vector_sum[2:3]], 0)

    attn_grad = jnp.stack(
        [front_grad[:, :HC], front_grad[:, HC : 2 * HC], front_grad[:, 2 * HC : 3 * HC], back_grad[:, :HC]]
    )
    mlp_grad = jnp.stack([front_grad[:, 3 * HC :], back_grad[:, HC:]])
    qkv_grad = bias_sum[: 3 * HC].reshape(3, HC)
    fc1_grad = bias_sum[3 * HC : 3 * HC + FC]
    attn_out = adamw(attn_weight, attn_grad, attn_first, attn_second, 0.04, 0.1)
    mlp_out = adamw(mlp_weight, mlp_grad, mlp_first, mlp_second, 0.04, 0.1)
    qkv_out = adamw(qkv_bias, qkv_grad, qkv_first, qkv_second, 0.3, 0.0)
    fc1_out = adamw(fc1_bias, fc1_grad, fc1_first, fc1_second, 0.3, 0.0)
    vector_out = adamw(vectors, vector_grad, vector_first, vector_second, 0.2, 0.0)
    return (out, input_grad, *attn_out, *mlp_out, *qkv_out, *fc1_out, *vector_out)


def solution(mesh):
    rows = P(("dp", "tensor"), None)
    weight = P(None, "dp", "tensor")
    qkv = P(None, "tensor")
    fc1 = P("tensor")
    return jax.shard_map(
        per_device,
        mesh=mesh,
        in_specs=(rows, rows, weight, weight, qkv, fc1, P()) + (weight, weight, qkv, fc1, P()) * 2,
        out_specs=(rows, rows) + (weight,) * 8 + (qkv,) * 4 + (fc1,) * 4 + (P(),) * 4,
        check_vma=False,
    )
```

```python
import functools

import jax
import jax.numpy as jnp
import numpy as np
from jax import lax
from jax.experimental import pallas as pl
from jax.experimental.pallas import tpu as pltpu
from jax.sharding import PartitionSpec as P

D = 2048
HD = 64
ROT = 32
LEN = 1024
STEP = 10
HEADS = 4
HC = HEADS * HD
FC = 1024
ROWS = 128
HALF = ROWS // 2
BQ = 256

EPSILON = 1e-05
SCALE = 0.125
BETA_ONE = 0.9
BETA_TWO = 0.999
ADAM_EPSILON = 1e-08
BF = jnp.bfloat16
LIMITS = dict(send=8, assemble=5, qkv=7, hidden=9, out=9, grad=8, normed=11, weight=6, forward=11, backward=12)
TIMES = dict(qkv=4.0, hidden=6.0, out=6.0, grad=5.5, normed=9.0, weight=5.0, forward=5.0, backward=8.0)
DECLARED = 0.3
F32 = jnp.float32


def dp_perm(move):
    pairs = []
    for x in range(2):
        for y in range(4):
            for c in range(2):
                nx, ny, nc = move(x, y, c)
                pairs.append(((x * 4 + y) * 2 + c, (nx * 4 + ny % 4) * 2 + nc))
    return pairs


def tensor_perm(move):
    pairs = []
    for z in range(4):
        for h in range(2):
            nz, nh = move(z, h)
            pairs.append((z * 2 + h, (nz % 4) * 2 + nh))
    return pairs


Y_UP = dp_perm(lambda x, y, c: (x, y + 1, c))
Y_DOWN = dp_perm(lambda x, y, c: (x, y - 1, c))
X_SWAP = dp_perm(lambda x, y, c: (1 - x, y, c))
CORE_SWAP = dp_perm(lambda x, y, c: (x, y, 1 - c))
Z_UP = tensor_perm(lambda z, h: (z + 1, h))
Z_DOWN = tensor_perm(lambda z, h: (z - 1, h))
Y_FAR = dp_perm(lambda x, y, c: (x, y + 2, c))
Z_FAR = tensor_perm(lambda z, h: (z + 2, h))
H_SWAP = tensor_perm(lambda z, h: (z, 1 - h))


def at(array, index, axis):
    return lax.dynamic_index_in_dim(array, index, axis, keepdims=False)


def up_z(v):
    return lax.ppermute(v, "tensor", Z_UP)


def down_z(v):
    return lax.ppermute(v, "tensor", Z_DOWN)


def swap_h(v):
    return lax.ppermute(v, "tensor", H_SWAP)


def up_y(v):
    return lax.ppermute(v, "dp", Y_UP)


def down_y(v):
    return lax.ppermute(v, "dp", Y_DOWN)


def swap_x(v):
    return lax.ppermute(v, "dp", X_SWAP)


def swap_core(v):
    return lax.ppermute(v, "dp", CORE_SWAP)


SMEM = pl.BlockSpec(memory_space=pltpu.SMEM)
VMEM = pl.BlockSpec(memory_space=pltpu.VMEM)


ANY = pl.BlockSpec(memory_space=pl.ANY)


def part(arrays, k):
    for held in arrays:
        if k < held.shape[0]:
            return pl.BlockSpec((1, *held.shape[1:]), lambda i: (k, 0, 0)), held
        k -= held.shape[0]


def call(kernel, out_shape, mebibytes, in_specs=None, scratch_shapes=(), us=1.0, deps=()):
    def run(*args):
        specs = list(in_specs or [VMEM] * len(args))
        gridded = any(spec.index_map is not None for spec in specs)

        def fit(spec, array):
            if gridded and spec is VMEM:
                return pl.BlockSpec(array.shape, lambda i: (0,) * len(array.shape))
            return spec

        def body(*refs):
            kernel(*refs[: len(args)], *refs[len(args) + len(deps) :])

        return pl.pallas_call(
            body,
            out_shape=out_shape,
            grid=(1,) if gridded else (),
            out_specs=jax.tree.map(lambda out: fit(VMEM, out), out_shape),
            in_specs=[fit(spec, arg) for spec, arg in zip(specs, args)] + [ANY] * len(deps),
            scratch_shapes=scratch_shapes,
            compiler_params=pltpu.CompilerParams(vmem_limit_bytes=mebibytes * 1024 * 1024),
            cost_estimate=pl.CostEstimate(
                flops=int(us * DECLARED * 1.1e9), bytes_accessed=1000, transcendentals=0
            ),
        )(*args, *deps)

    return run


def nothing_kernel(*refs):
    pass


def tied(value, *deps):
    return pl.pallas_call(
        nothing_kernel,
        out_shape=jax.ShapeDtypeStruct(value.shape, value.dtype),
        in_specs=[ANY] * (1 + len(deps)),
        out_specs=ANY,
        input_output_aliases={0: 0},
        compiler_params=pltpu.CompilerParams(vmem_limit_bytes=1024 * 1024),
        cost_estimate=pl.CostEstimate(flops=1000, bytes_accessed=1000, transcendentals=0),
    )(value, *deps)


def shape(rows, columns, dtype=BF):
    return jax.ShapeDtypeStruct((rows, columns), dtype)


def normalized(block, vectors, normed, stats, at):
    inputs = block.astype(F32)
    mean = jnp.mean(inputs, -1, keepdims=True)
    centred = inputs - mean
    inverse = lax.rsqrt(jnp.mean(centred * centred, -1, keepdims=True) + EPSILON)
    normed[at, :] = (centred * inverse * vectors[0:1, :] + vectors[1:2, :]).astype(BF)
    lane = lax.broadcasted_iota(jnp.int32, (ROWS, 128), 1)
    stats[at, :] = jnp.where(lane < 64, mean, inverse)


def norm_first_kernel(own, swapped, below, above, vectors, normed, stats):
    for i, block in enumerate((own, swapped, below, above)):
        normalized(block[...], vectors, normed, stats, slice(i * ROWS, (i + 1) * ROWS))


def norm_second_kernel(below, above, vectors, normed, stats):
    far = jnp.concatenate([below[ROWS:, :], above[ROWS:, :]], 0)
    for i, block in enumerate((below[:ROWS, :], above[:ROWS, :], far)):
        normalized(block, vectors, normed, stats, slice(i * ROWS, (i + 1) * ROWS))


def norm_last_kernel(info, below, above, vectors, normed_a, stats_a, normed_b, stats_b, normed, stats):
    places = At(info, ROW_PLACES)
    at = [pl.ds(pl.multiple_of(places[i] * ROWS, ROWS), ROWS) for i in range(8)]
    normalized(jnp.concatenate([below[:HALF, :], above[:HALF, :]], 0), vectors, normed, stats, at[7])
    for i in range(7):
        held, held_stats, k = (normed_a, stats_a, i) if i < 4 else (normed_b, stats_b, i - 4)
        normed[at[i], :] = held[k * ROWS : (k + 1) * ROWS, :]
        stats[at[i], :] = held_stats[k * ROWS : (k + 1) * ROWS, :]


def rows_kernel(skipped, info, own, swapped, below, above, below_mid, above_mid, first, second, rows):
    places = At(info, ROW_PLACES)
    far = jnp.concatenate([below_mid[ROWS:, :], above_mid[ROWS:, :]], 0)
    last = jnp.concatenate([first[:HALF, :], second[:HALF, :]], 0)
    near = [ref[skipped : skipped + ROWS, :] for ref in (below, above)]
    blocks = (own[...], swapped[...], *near, below_mid[:ROWS, :], above_mid[:ROWS, :], far, last)
    for i, block in enumerate(blocks):
        rows[pl.ds(pl.multiple_of(places[i] * ROWS, ROWS), ROWS), :] = block


def rows_call(skipped, info, *blocks, deps=()):
    return call(
        functools.partial(rows_kernel, skipped), shape(LEN, D), 12, [SMEM] + [VMEM] * 8, deps=deps
    )(info, *blocks)


def beside(message, wide, rows):
    done = 0
    for piece in wide:
        message[done : done + piece.shape[0], : piece.shape[1]] = piece
        done += piece.shape[0]
    columns, middle = wide[0].shape[1], rows.shape[1] // 2
    message[:ROWS, columns:] = rows[:, :middle]
    message[ROWS:, columns:] = rows[:, middle:]


def apart(message, columns):
    return jnp.concatenate([message[:ROWS, columns:], message[ROWS:, columns:]], 1)


def stack(out, *pieces):
    done = 0
    for piece in pieces:
        out[done : done + piece.shape[0], :] = piece
        done += piece.shape[0]


def send_second_kernel(swapped, below, above, qkv_own, qkv_swapped, rest_own, up, down, pair, rest):
    stack(up, swapped[...], below[:HALF, :])
    stack(down, swapped[...], above[HALF:, :])
    stack(pair, qkv_own[...], qkv_swapped[...])
    rest[...] = rest_own[...]


def send_third_kernel(
    below_mid, above_mid, qkv_below, qkv_above, rest_own, rest_swapped, backs, up, down, message_up, message_down, backs_out
):
    stack(up, below_mid[:HALF, :], backs[...])
    stack(down, above_mid[HALF:ROWS, :], backs[...])
    pair = rest_own[:, :FC], rest_swapped[:, :FC]
    beside(message_up, pair, qkv_below[:ROWS, :])
    beside(message_down, pair, qkv_above[ROWS:, :])
    backs_out[...] = backs[...]


def send_fourth_kernel(
    below_last,
    above_last,
    message_below,
    message_above,
    backs_swapped,
    rest_own,
    rest_swapped,
    qkv_pair,
    qkv_below,
    qkv_above,
    up,
    down,
    message_up,
    message_down,
    qkv_mine,
):
    stack(up, backs_swapped[...], below_last[HALF:ROWS, :])
    stack(down, backs_swapped[...], above_last[ROWS:, :])
    pair = rest_own[:, FC:], rest_swapped[:, FC:]
    beside(message_up, pair, message_below[:ROWS, :FC])
    beside(message_down, pair, message_above[ROWS:, :FC])
    stack(qkv_mine, qkv_pair[...], qkv_above[...], apart(message_below, FC), apart(message_above, FC), qkv_below[...])


def send_fifth_kernel(
    below_backs,
    above_backs,
    own_first,
    below_first,
    above_first,
    own_second,
    below_second,
    above_second,
    up,
    down,
    far_up,
    far_down,
    fc1_mine,
    back_mine,
):
    up[...] = below_backs[:HALF, :]
    down[...] = above_backs[HALF:ROWS, :]
    columns = HC + FC
    far_up[...] = below_second[:ROWS, :columns]
    far_down[...] = above_second[ROWS:, :columns]
    stack(
        fc1_mine,
        own_first[:, :FC],
        above_first[:, :FC],
        apart(below_second, columns),
        apart(above_second, columns),
        below_first[:, :FC],
    )
    stack(back_mine, own_second[:, :columns], above_second[:, :columns], below_second[:, :columns])


def send_sixth_kernel(far, far_swapped, mine):
    stack(mine, far[...], far_swapped[...])


PLACES, BACK_PLACES, FIRST_PLACES, SECOND_PLACES, ROW_PLACES, GROUPS, OWN_X, OWN_H = (0, 16, 32, 40, 48, 56, 60, 61)


def position_table():
    table = np.zeros((128, 64), np.int32)
    for dp in range(16):
        x, y, core = dp // 8, dp // 2 % 4, dp % 2

        def block(step, other_x, c):
            return ((x ^ other_x) * 4 + (y + step) % 4) * 2 + c

        def gathered(steps):
            return [block(step, o, c) for c in (core, 1 - core) for step in steps for o in (0, 1)]

        def grads(c):
            return [(xx * 4 + (y + step) % 4) * 2 + c for step in (2, 1, 3, 0) for xx in (0, 1)]

        for tensor in range(8):
            z, h = tensor // 2, tensor % 2

            def row(step, other):
                return (z + step) % 4 * 2 + (h ^ other)

            rows = [row(0, 0), row(0, 1), row(3, 0), row(1, 0), row(3, 1), row(1, 1), row(2, 0), row(2, 1)]
            groups = [(z + step) % 4 for step in (2, 1, 3, 0)]
            table[dp * 8 + tensor] = [
                *gathered((0, 1, 2, 3)),
                *gathered((0, 1, 3, 2)),
                *grads(1 - core),
                *grads(core),
                *rows,
                *groups,
                x,
                h,
                0,
                0,
            ]
    return table


class At:
    def __init__(self, info, first):
        self.info, self.first = info, first

    def __getitem__(self, i):
        return self.info[self.first + i]


EXTRA = 16


def coded(sums):
    high = sums.astype(BF)
    low = (sums - high.astype(F32)).astype(BF)
    rest = jnp.zeros((EXTRA - 2 * sums.shape[0], sums.shape[1]), F32)
    return jnp.concatenate([high.astype(F32), low.astype(F32), rest], 0).astype(BF)


def decoded(block):
    block = block.astype(F32)
    return block[:3] + block[3:6]


def near_kernel(above, below, from_below, from_above, *refs):
    up, down = refs[-2:]
    up[:ROWS, :] = (above[:ROWS, :].astype(F32) + from_below[...].astype(F32)).astype(BF)
    up[ROWS:256, :] = above[ROWS:, :]
    down[:ROWS, :] = below[:ROWS, :]
    down[ROWS:256, :] = (below[ROWS:, :].astype(F32) + from_above[...].astype(F32)).astype(BF)
    if len(refs) > 2:
        block = coded(refs[0][:3, :])
        up[256:, :] = block
        down[256:, :] = block


def near(above, below, from_below, from_above, *sums, deps=()):
    rows = 256 + EXTRA * len(sums)
    return call(near_kernel, [shape(rows, above.shape[1])] * 2, 12, deps=deps)(
        above, below, from_below, from_above, *sums
    )


def last_kernel(info, here, got_up, got_down, kept, sent):
    own = At(info, OWN_H)[0]
    for out, which in ((kept, own), (sent, 1 - own)):
        at = pl.ds(pl.multiple_of(which * ROWS, ROWS), ROWS)
        total = here[at, :].astype(F32) + got_up[at, :].astype(F32) + got_down[at, :].astype(F32)
        out[...] = total.astype(out.dtype)


def last(info, here, got_up, got_down, deps=()):
    columns = here.shape[1]
    return call(
        last_kernel, [shape(ROWS, columns, F32), shape(ROWS, columns)], 10, [SMEM] + [VMEM] * 3, deps=deps
    )(info, here, got_up, got_down)


def grad_last_kernel(info, here, got_up, got_down, sums, far_sums, kept, sent, total_sums):
    last_kernel(info, here, got_up, got_down, kept, sent.at[:ROWS])
    total = sums[:3, :] + far_sums[:3, :] + decoded(got_up[256:, :]) + decoded(got_down[256:, :])
    total_sums[...] = total
    sent[ROWS:, :] = coded(total)


def grad_last(info, here, got_up, got_down, sums, far_sums, deps=()):
    outs = [shape(ROWS, D, F32), shape(ROWS + EXTRA, D), shape(3, D, F32)]
    return call(grad_last_kernel, outs, 12, [SMEM] + [VMEM] * 5, deps=deps)(
        info, here, got_up, got_down, sums, far_sums
    )


def small_kernel(sums, got, projected, hidden, out):
    out[:3, :] = sums[...] + decoded(got[ROWS:, :])
    rest = jnp.zeros((1, D - 3 * HC - FC), F32)
    out[3:, :] = jnp.concatenate([projected[...], hidden[...], rest], 1)


def plus(mine, got):
    return mine.astype(F32) + got.astype(F32)


def weight_far_kernel(mine, got, first, second):
    total = plus(mine[0], got[0]).astype(BF)
    first[...] = total[:ROWS]
    second[...] = total[ROWS:]


def weight_far(mine, got, deps=()):
    columns = mine[0].shape[2]
    spec, held = part(got, 0)
    return call(weight_far_kernel, [shape(ROWS, columns)] * 2, 14, [VMEM, spec], deps=deps)(mine[0], held)


def weight_near_kernel(above, below, got_above, got_below, from_below, from_above, up, down):
    columns = above.shape[2]
    up[:ROWS, :columns] = (plus(above[0, :ROWS], got_above[0, :ROWS]) + from_below[...].astype(F32)).astype(BF)
    up[ROWS:, :columns] = plus(above[0, ROWS:], got_above[0, ROWS:]).astype(BF)
    down[:ROWS, :columns] = plus(below[0, :ROWS], got_below[0, :ROWS]).astype(BF)
    down[ROWS:, :columns] = (plus(below[0, ROWS:], got_below[0, ROWS:]) + from_above[...].astype(F32)).astype(BF)


def first_near_kernel(above, below, got_above, got_below, from_below, from_above, front, front_got, up, down):
    weight_near_kernel(above, below, got_above, got_below, from_below, from_above, up, down)
    columns = above.shape[2]
    far = plus(front[0], front_got[0]).astype(BF)
    middle = far.shape[1] // 2
    for message, rows in ((up, far[:ROWS]), (down, far[ROWS:])):
        message[:ROWS, columns:] = rows[:, :middle]
        message[ROWS:, columns:] = rows[:, middle:]


def first_near(mine, got, from_below, from_above, front, front_got, deps=()):
    columns, more = mine[0].shape[2], front[0].shape[2]
    (spec, above), (spec2, below), (spec3, far) = part(got, 1), part(got, 2), part(front_got, 0)
    specs = [VMEM, VMEM, spec, spec2, VMEM, VMEM, VMEM, spec3]
    return call(first_near_kernel, [shape(256, columns + more // 2)] * 2, 22, specs, deps=deps)(
        mine[1], mine[2], above, below, from_below, from_above, front[0], far
    )


def second_near_kernel(above, below, got_above, got_below, message_below, message_above, up, down):
    columns = message_below.shape[1] - above.shape[2] // 2
    far = apart(message_below, columns), apart(message_above, columns)
    weight_near_kernel(above, below, got_above, got_below, *far, up, down)


def second_near(mine, got, message_below, message_above, deps=()):
    (spec, above), (spec2, below) = part(got, 1), part(got, 2)
    specs = [VMEM, VMEM, spec, spec2, VMEM, VMEM]
    return call(second_near_kernel, [shape(256, mine[0].shape[2])] * 2, 22, specs, deps=deps)(
        mine[1], mine[2], above, below, message_below, message_above
    )


def weight_last_kernel(info, mine, got, got_up, got_down, kept, sent):
    columns, own = mine.shape[2], At(info, OWN_X)[0]
    for out, which in ((kept, own), (sent, 1 - own)):
        at = pl.ds(pl.multiple_of(which * ROWS, ROWS), ROWS)
        total = plus(mine[0, at, :], got[0, at, :]) + plus(got_up[at, :columns], got_down[at, :columns])
        out[...] = total.astype(out.dtype)


def weight_last(info, mine, got, got_up, got_down, deps=()):
    columns = mine[0].shape[2]
    spec, here = part(got, 3)
    specs = [SMEM, VMEM, spec, VMEM, VMEM]
    return call(weight_last_kernel, [shape(ROWS, columns, F32), shape(ROWS, columns)], 16, specs, deps=deps)(
        info, mine[3], here, got_up, got_down
    )


def add_kernel(first, *refs):
    total = first[...]
    for ref in refs[:-1]:
        total = total + ref[...]
    refs[-1][...] = total


def added(*values, deps=()):
    return call(add_kernel, jax.ShapeDtypeStruct(values[0].shape, F32), 4, deps=deps)(*values)


def send(v, axes, perm):
    return lax.ppermute(v, axes, perm)


def rotary_tables():
    half = ROT // 2
    position = np.arange(LEN, dtype=np.float32)
    frequency = np.float32(10000.0) ** (-np.arange(half, dtype=np.float32) * np.float32(2.0 / ROT))
    angle = (position[:, None] * frequency[None, :].astype(np.float32)).astype(np.float32)
    cosine, sine = np.cos(angle), np.sin(angle)
    rest = np.ones((LEN, HD - ROT), np.float32)
    none = np.zeros((LEN, half), np.float32)
    same = np.concatenate([cosine, cosine, rest] * 2, 1)
    ahead = np.concatenate([-sine, none, 0 * rest] * 2, 1)
    behind = np.concatenate([none, sine, 0 * rest] * 2, 1)
    return jnp.asarray(np.concatenate([same, ahead, behind], 1).astype(np.float32))


def rotated(values, tables, sign):
    wide = [jnp.concatenate([tables[:, j * 128 : (j + 1) * 128]] * 2, 1) for j in range(3)]
    half = ROT // 2
    return values * wide[0] + sign * (
        pltpu.roll(values, HC - half, 1) * wide[1] + pltpu.roll(values, half, 1) * wide[2]
    )


WIDE = 256


def assemble_kernel(first, info, *refs):
    places, out = At(info, first), refs[-1]
    done = 0
    for source in refs[:-1]:
        for i in range(source.shape[0] // ROWS):
            start = pl.multiple_of(places[done] * ROWS, ROWS)
            out[pl.ds(start, ROWS), :] = source[i * ROWS : (i + 1) * ROWS, :]
            done += 1


def assembled(first, info, *sources, deps=()):
    specs = [SMEM] + [VMEM] * len(sources)
    return call(
        functools.partial(assemble_kernel, first),
        shape(D, sources[0].shape[1]),
        LIMITS["assemble"],
        specs,
        us=2.0,
        deps=deps,
    )(info, *sources)


def qkv_kernel(rows, weights, bias, tables, heads):
    for j in range(3):
        part = slice(j * HC, (j + 1) * HC)
        pre = nn(rows[...], weights[:, part]) + bias[j : j + 1]
        heads[:, part] = (rotated(pre, tables, 1.0) if j < 2 else pre).astype(BF)


def qkv_call(normed, weights, bias, tables, deps=()):
    return call(qkv_kernel, shape(LEN, 3 * HC), LIMITS["qkv"], us=TIMES["qkv"], deps=deps)(normed, weights, bias, tables)


ROOT = 0.7978845608028654
CUBIC = 0.044715


def hidden_kernel(rows, weights, bias, activated, slope):
    for j in range(FC // WIDE):
        part = slice(j * WIDE, (j + 1) * WIDE)
        hidden = nn(rows[...], weights[:, part]) + bias[:, part]
        square = hidden * hidden
        bent = jnp.tanh(ROOT * (hidden + CUBIC * (square * hidden)))
        half = 0.5 * (1.0 + bent)
        activated[:, part] = (hidden * half).astype(BF)
        slope[:, part] = (
            half + (0.5 * ROOT) * hidden * (1.0 - bent * bent) * (1.0 + (3.0 * CUBIC) * square)
        ).astype(BF)


def hidden_call(normed, weights, bias, deps=()):
    return call(hidden_kernel, [shape(LEN, FC)] * 2, LIMITS["hidden"], us=TIMES["hidden"], deps=deps)(
        normed, weights, bias.reshape(1, FC)
    )


def out_kernel(steps, info, attended, activated, weights, *parts):
    groups = At(info, GROUPS)
    for i, r in enumerate(steps):
        here = pl.ds(pl.multiple_of(groups[r] * 256, 256), 256)
        rows = jnp.concatenate([attended[here, :], activated[here, :]], 1)
        low = nt(rows, weights[...]).astype(BF)
        if r == 0:
            parts[0][...] = low[:ROWS]
            parts[1][...] = low[ROWS:]
        else:
            parts[i][...] = low


def out_call(steps, info, attended, activated, weights, deps=()):
    return call(
        functools.partial(out_kernel, steps),
        [shape(ROWS, D)] * 2 if steps == (0,) else [shape(256, D)] * len(steps),
        LIMITS["out"],
        [SMEM] + [VMEM] * 3,
        us=TIMES["out"] * len(steps) / 4,
        deps=deps,
    )(info, attended, activated, weights)


def grad_kernel(backs, slope, weights, grad_attended, grad_hidden, sums):
    for j in range((HC + FC) // WIDE):
        grad = nn(backs[...], weights[:, j * WIDE : (j + 1) * WIDE])
        if j == 0:
            grad_attended[...] = grad.astype(BF)
        else:
            part = slice((j - 1) * WIDE, j * WIDE)
            low = (grad * slope[:, part].astype(F32)).astype(BF)
            grad_hidden[:, part] = low
            sums[:, part] = jnp.sum(low.astype(F32), 0, keepdims=True)


def grad_call(backs, slope, weights, deps=()):
    return call(
        grad_kernel, [shape(LEN, HC), shape(LEN, FC), shape(1, FC, F32)], LIMITS["grad"], us=TIMES["grad"], deps=deps
    )(backs, slope, weights)


def normed_kernel(steps, info, projected, hidden, rows, stats, weights, weights2, before, *refs):
    parts, sums = refs[:-1], refs[-1]
    groups = At(info, GROUPS)
    for n in range(2):
        columns = slice(n * D // 2, (n + 1) * D // 2)
        first, second = before[0:1, columns], before[1:2, columns]
        for i, r in enumerate(steps):
            here = pl.ds(pl.multiple_of(groups[r] * 256, 256), 256)
            grad = nt(projected[here, :], weights[columns, :]) + nt(hidden[here, :], weights2[columns, :])
            low = grad.astype(BF)
            if r == 0:
                parts[0][:, columns] = low[:ROWS]
                parts[1][:, columns] = low[ROWS:]
            else:
                parts[i][:, columns] = low
            standard = (rows[here, columns].astype(F32) - stats[here, 0:1]) * stats[here, 64:65]
            first = first + jnp.sum(grad * standard, 0, keepdims=True)
            second = second + jnp.sum(grad, 0, keepdims=True)
        sums[0:1, columns] = first
        sums[1:2, columns] = second
    sums[2:, :] = before[2:, :]


def normed_call(steps, info, projected, hidden, rows, stats, weights, weights2, before, deps=()):
    parts = [shape(ROWS, D)] * 2 if steps == (0,) else [shape(256, D)] * len(steps)
    return call(
        functools.partial(normed_kernel, steps),
        parts + [shape(4, D, F32)],
        LIMITS["normed"],
        [SMEM] + [VMEM] * 7,
        us=TIMES["normed"] * len(steps) / 4,
        deps=deps,
    )(info, projected, hidden, rows, stats, weights, weights2, before)


def weight_kernel(counts, parts, first, info, *refs):
    places, outs, refs = At(info, first), refs[-len(parts) :], list(refs[: -len(parts)])
    outs = [ref.at[k] for ref, size in zip(outs, parts) for k in range(size)]
    done = 0
    for count in counts:
        left, rights, refs = refs[0], refs[1 : 1 + count], refs[1 + count :]
        for step in range(2):
            turned = jnp.concatenate(
                [left[:, pl.ds(pl.multiple_of(places[4 * step + j] * ROWS, ROWS), ROWS)] for j in range(4)], 1
            ).T
            column = done
            for right in rights:
                for j in range(right.shape[1] // WIDE):
                    term = nn(turned, right[:, j * WIDE : (j + 1) * WIDE]).astype(BF)
                    outs[2 * step][:, column : column + WIDE] = term[:256]
                    outs[2 * step + 1][:, column : column + WIDE] = term[256:]
                    column += WIDE
        done = column


def weight_call(parts, first, info, *terms, deps=()):
    columns = sum(r.shape[1] for term in terms for r in term[1:])
    flat = [r for term in terms for r in term]
    outs = [jax.ShapeDtypeStruct((size, 256, columns), BF) for size in parts]
    return call(
        functools.partial(weight_kernel, [len(term) - 1 for term in terms], parts, first),
        outs,
        LIMITS["weight"],
        [SMEM] + [VMEM] * len(flat),
        us=TIMES["weight"] * columns / 2304,
        deps=deps,
    )(info, *flat)


def nt(left, right):
    return lax.dot_general(left, right, (((1,), (1,)), ((), ())), preferred_element_type=F32)


def nn(left, right):
    return lax.dot_general(left, right, (((1,), (0,)), ((), ())), preferred_element_type=F32)


POWER = SCALE * 1.4426950408889634


def by_head(block, lane):
    return jnp.concatenate([jnp.where(lane == h, block, jnp.zeros((), BF)) for h in range(HEADS)], 0)


def seen_mask():
    key = lax.broadcasted_iota(jnp.int32, (BQ, BQ), 0)
    query = lax.broadcasted_iota(jnp.int32, (BQ, BQ), 1)
    return jnp.concatenate([key <= query] * HEADS, 1)


def forward_kernel(heads, attended, logsum, out_t, values_t):
    queries, keys, values = (heads.at[:, j * HC : (j + 1) * HC] for j in range(3))
    values_t[...] = values[...].T
    lane = lax.broadcasted_iota(jnp.int32, (BQ, HC), 1) // HD
    seen = seen_mask()
    for q in range(LEN // BQ):
        here = slice(q * BQ, (q + 1) * BQ)
        query = by_head(queries[here, :], lane)
        blocks = []
        largest = None
        for k in range(q + 1):
            block = nt(keys[k * BQ : (k + 1) * BQ, :], query)
            if k == q:
                block = jnp.where(seen, block, -1e30)
            blocks.append(block)
            top = jnp.max(block, 0, keepdims=True)
            largest = top if largest is None else jnp.maximum(largest, top)
        total = jnp.zeros((1, HEADS * BQ), F32)
        found = [jnp.zeros((HD, BQ), F32)] * HEADS
        for k in range(q + 1):
            powers = jnp.exp2((blocks[k] - largest) * POWER)
            total = total + jnp.sum(powers, 0, keepdims=True)
            low = powers.astype(BF)
            for h in range(HEADS):
                found[h] = found[h] + nn(
                    values_t[h * HD : (h + 1) * HD, k * BQ : (k + 1) * BQ], low[:, h * BQ : (h + 1) * BQ]
                )
        scale = 1.0 / total
        base = largest * POWER + jnp.log2(total)
        for h in range(HEADS):
            out_t[h * HD : (h + 1) * HD, here] = found[h] * scale[:, h * BQ : (h + 1) * BQ]
            logsum[h : h + 1, here] = base[:, h * BQ : (h + 1) * BQ]
    attended[...] = out_t[...].T.astype(BF)


def forward_call(heads, deps=()):
    return call(
        forward_kernel,
        [shape(LEN, HC), shape(8, LEN, F32), shape(HC, LEN, F32)],
        LIMITS["forward"],
        scratch_shapes=[pltpu.VMEM((HC, LEN), BF)],
        us=TIMES["forward"],
        deps=deps,
    )(heads)


def backward_kernel(
    heads, grads, logsum, out_t, tables, out, sums, keys_t, query_grads, key_grads, value_grads
):
    queries, keys, values = (heads.at[:, j * HC : (j + 1) * HC] for j in range(3))
    keys_t[...] = keys[...].T
    turned = grads[...].astype(F32).T * out_t[...]
    lane = lax.broadcasted_iota(jnp.int32, (BQ, HC), 1) // HD
    seen = seen_mask()
    for q in reversed(range(LEN // BQ)):
        here = slice(q * BQ, (q + 1) * BQ)
        query = by_head(queries[here, :], lane)
        grad = by_head(grads[here, :], lane)
        base = jnp.concatenate([logsum[h : h + 1, here] for h in range(HEADS)], 1)
        dots = jnp.concatenate(
            [jnp.sum(turned[h * HD : (h + 1) * HD, here], 0, keepdims=True) for h in range(HEADS)], 1
        )
        found = [jnp.zeros((HD, BQ), F32)] * HEADS
        for k in range(q + 1):
            there = slice(k * BQ, (k + 1) * BQ)
            probs = jnp.exp2(nt(keys[there, :], query) * POWER - base)
            if k == q:
                probs = jnp.where(seen, probs, 0.0)
            score = (probs * (nt(values[there, :], grad) - dots)).astype(BF)
            value_grad, key_grad = nn(probs.astype(BF), grad), nn(score, query)
            if q == LEN // BQ - 1:
                value_grads[there, :] = value_grad
                key_grads[there, :] = key_grad
            else:
                value_grads[there, :] += value_grad
                key_grads[there, :] += key_grad
            for h in range(HEADS):
                found[h] = found[h] + nn(
                    keys_t[h * HD : (h + 1) * HD, there], score[:, h * BQ : (h + 1) * BQ]
                )
        for h in range(HEADS):
            query_grads[h * HD : (h + 1) * HD, here] = found[h]
    parts = (
        rotated(query_grads[...].T * SCALE, tables, -1.0),
        rotated(key_grads[...] * SCALE, tables, -1.0),
        value_grads[...],
    )
    for j, part in enumerate(parts):
        low = part.astype(BF)
        out[:, j * HC : (j + 1) * HC] = low
        sums[:, j * HC : (j + 1) * HC] = jnp.sum(low.astype(F32), 0, keepdims=True)


def backward_call(heads, grads, logsum, out_t, tables, deps=()):
    return call(
        backward_kernel,
        [shape(LEN, 3 * HC), shape(1, 3 * HC, F32)],
        LIMITS["backward"],
        scratch_shapes=[pltpu.VMEM((HC, LEN), BF), pltpu.VMEM((HC, LEN), F32)] + [pltpu.VMEM((LEN, HC), F32)] * 2,
        us=TIMES["backward"],
        deps=deps,
    )(heads, grads, logsum, out_t, tables)


def adamw(param, grad, first, second, rate, decay):
    first_new = BETA_ONE * first + (1.0 - BETA_ONE) * grad
    second_new = BETA_TWO * second + (1.0 - BETA_TWO) * grad * grad
    ratio = (
        first_new
        / (1.0 - BETA_ONE**STEP)
        / (jnp.sqrt(second_new / (1.0 - BETA_TWO**STEP)) + ADAM_EPSILON)
    )
    return (grad, first_new, second_new, param - rate * (ratio + decay * param))


def side_by_side(stack):
    return jnp.concatenate([stack[j] for j in range(stack.shape[0])], 1)


def per_device(
    tokens,
    cotangent,
    attn_weight,
    mlp_weight,
    qkv_bias,
    fc1_bias,
    vectors,
    attn_first,
    mlp_first,
    qkv_first,
    fc1_first,
    vector_first,
    attn_second,
    mlp_second,
    qkv_second,
    fc1_second,
    vector_second,
):
    dp = lax.axis_index("dp")
    tensor = lax.axis_index("tensor")
    info = lax.dynamic_index_in_dim(jnp.asarray(position_table()), dp * 8 + tensor, 0, keepdims=False)
    tables = rotary_tables()
    qkv_own = side_by_side(attn_weight[:3].astype(BF))
    rest_own = jnp.concatenate([mlp_weight[0], attn_weight[3], mlp_weight[1]], 1).astype(BF)

    columns = HC + FC

    back_sum = jnp.pad(jnp.sum(cotangent.astype(F32), 0, keepdims=True), ((2, 1), (0, 0)))

    swapped = swap_h(tokens)
    below_own, above_own = up_z(tokens), down_z(tokens)
    qkv_swapped = swap_x(qkv_own)
    sent = call(
        send_second_kernel, [shape(192, D)] * 2 + [shape(256, 3 * HC), shape(ROWS, HC + 2 * FC)], LIMITS["send"], deps=(info, back_sum)
    )(swapped, below_own, above_own, qkv_own, qkv_swapped, rest_own)
    below_mid, above_mid = up_z(sent[0]), down_z(sent[1])
    qkv_pair = sent[2]
    qkv_below, qkv_above = up_y(qkv_pair), down_y(qkv_pair)
    rest_swapped = swap_x(sent[3])
    normed_a = call(norm_first_kernel, [shape(512, D), shape(512, 128, F32)], 8, deps=(qkv_pair,))(
        tokens, swapped, below_own, above_own, vectors
    )
    sent = call(
        send_third_kernel,
        [shape(192, D)] * 2 + [shape(256, FC + 3 * HC // 2)] * 2 + [shape(ROWS, D)],
        LIMITS["send"],
        deps=(normed_a[1],),
    )(below_mid, above_mid, qkv_below, qkv_above, rest_own, rest_swapped, cotangent)
    below_last, above_last = up_z(sent[0]), down_z(sent[1])
    own_first = sent[2]
    below_first, above_first = up_y(sent[2]), down_y(sent[3])
    backs_swapped = swap_h(sent[4])
    normed_b = call(norm_second_kernel, [shape(384, D), shape(384, 128, F32)], 8, deps=(own_first,))(
        below_mid, above_mid, vectors
    )
    sent = call(
        send_fourth_kernel,
        [shape(192, D)] * 2 + [shape(256, columns + FC // 2)] * 2 + [shape(8 * ROWS, 3 * HC)],
        LIMITS["send"],
        deps=(normed_b[1],),
    )(
        below_last,
        above_last,
        below_first,
        above_first,
        backs_swapped,
        rest_own,
        rest_swapped,
        qkv_pair,
        qkv_below,
        qkv_above,
    )
    below_backs, above_backs = up_z(sent[0]), down_z(sent[1])
    own_second = sent[2]
    below_second, above_second = up_y(sent[2]), down_y(sent[3])
    qkv_mine = sent[4]
    qkv_other = swap_core(qkv_mine)
    normed, stats = call(
        norm_last_kernel, [shape(LEN, D), shape(LEN, 128, F32)], 12, [SMEM] + [VMEM] * 7, deps=(qkv_mine,)
    )(info, below_last, above_last, vectors, *normed_a, *normed_b)
    qkv_full = assembled(PLACES, info, qkv_mine, qkv_other, deps=(stats,))
    heads = qkv_call(normed, qkv_full, qkv_bias, tables)
    attended, logsum, attended_t = forward_call(heads)
    rows = rows_call(
        0,
        info,
        tokens,
        swapped,
        below_own,
        above_own,
        below_mid,
        above_mid,
        below_last,
        above_last,
        deps=(logsum,),
    )
    sent = call(
        send_fifth_kernel,
        [shape(HALF, D)] * 2 + [shape(ROWS, columns)] * 2 + [shape(8 * ROWS, FC), shape(6 * ROWS, columns)],
        LIMITS["send"],
        deps=(logsum, rows),
    )(below_backs, above_backs, own_first, below_first, above_first, own_second, below_second, above_second)
    first_backs, second_backs = up_z(sent[0]), down_z(sent[1])
    back_far, back_far_swapped = up_y(sent[2]), down_y(sent[3])
    fc1_mine, back_mine = sent[4:]
    fc1_other = swap_core(fc1_mine)
    back_other = swap_core(back_mine)
    fc1_full = assembled(PLACES, info, fc1_mine, fc1_other)
    activated, slope = hidden_call(normed, fc1_full, fc1_bias)
    far_mine = call(
        send_sixth_kernel, shape(256, columns), LIMITS["send"], deps=(slope, first_backs, second_backs, back_other)
    )(back_far, back_far_swapped)
    far_other = swap_core(far_mine)
    backs = rows_call(
        HALF,
        info,
        cotangent,
        backs_swapped,
        below_last,
        above_last,
        below_backs,
        above_backs,
        first_backs,
        second_backs,
        deps=(far_mine,),
    )
    back_full = assembled(BACK_PLACES, info, back_mine, far_mine, back_other, far_other, deps=(backs,))
    out_far = out_call((0,), info, attended, activated, back_full)
    from_below, from_above = up_z(out_far[0]), down_z(out_far[1])
    out_parts = out_call((1, 2, 3), info, attended, activated, back_full, deps=(out_far[0],))
    grad_attended, grad_hidden, hidden_sums = grad_call(backs, slope, back_full, deps=(out_parts[0],))
    back = (backs, attended, activated)
    (back_other,) = weight_call((4,), FIRST_PLACES, info, back, deps=(hidden_sums,))
    up, down = near(out_parts[0], out_parts[1], from_below, from_above, deps=(back_other,))
    got_up, got_down = up_z(up), down_z(down)
    back_got = (swap_core(tied(back_other, up)),)
    projected, projected_sums = backward_call(heads, grad_attended, logsum, attended_t, tables, deps=(up,))
    back_mine = weight_call((1, 1, 1, 1), SECOND_PLACES, info, back, deps=(projected_sums,))
    front = (normed, projected, grad_hidden)
    front_other = weight_call((1, 1, 1, 1), FIRST_PLACES, info, front, deps=(back_mine[0], *back_got))
    back_far = weight_far(back_mine, back_got, deps=(front_other[0],))
    back_below, back_above = up_y(back_far[0]), down_y(back_far[1])
    front_got = [swap_core(v) for v in front_other[:3]]
    front_mine = weight_call((1, 1, 1, 1), SECOND_PLACES, info, front, deps=(front_other[0],))
    terms = (info, projected, grad_hidden, rows, stats, qkv_full, fc1_full)
    *far_parts, far_sums = normed_call((0,), *terms, back_sum, deps=(back_far[0], front_mine[0], got_up, got_down))
    from_below, from_above = up_z(far_parts[0]), down_z(far_parts[1])
    *normed_parts, normed_sums = normed_call((1, 2, 3), *terms, far_sums, deps=front_got)
    out_own, out_sent = last(info, out_parts[2], got_up, got_down, deps=(normed_sums,))
    out_got = swap_h(out_sent)
    up, down = near(
        normed_parts[0], normed_parts[1], from_below, from_above, normed_sums, deps=(out_sent, back_below, back_above)
    )
    got_up, got_down = up_z(up), down_z(down)
    far_sums = send(tied(normed_sums, up, out_got), "tensor", Z_FAR)
    sent = first_near(back_mine, back_got, back_below, back_above, front_mine, front_got, deps=(up,))
    back_up, back_down = up_y(sent[0]), down_y(sent[1])
    local = tokens.astype(F32)
    out = (local + (out_own + out_got.astype(F32)) + vectors[2] + vectors[3]).astype(BF)
    grad_own, grad_sent, sums = grad_last(
        info, normed_parts[2], got_up, got_down, normed_sums, far_sums, deps=(out_got,)
    )
    grad_got = swap_h(grad_sent)
    sent = second_near(front_mine, front_got, back_up, back_down, deps=(grad_sent,))
    front_up, front_down = up_y(sent[0]), down_y(sent[1])
    back_own, back_sent = weight_last(info, back_mine, back_got, back_up, back_down, deps=(sent[0],))
    back_last = swap_x(back_sent)
    front_got.append(swap_core(tied(front_other[3], back_last)))
    small = call(small_kernel, shape(4, D, F32), 4, deps=(back_last,))(sums, grad_got, projected_sums, hidden_sums)
    small = added(small, send(small, "dp", CORE_SWAP))
    front_own, front_sent = weight_last(
        info, front_mine, front_got, front_up, front_down, deps=(grad_got, back_last, small)
    )
    front_last = swap_x(front_sent)
    small = added(
        small, *(send(tied(small, front_sent), "dp", perm) for perm in (Y_UP, Y_DOWN, Y_FAR)), deps=(front_last,)
    )
    small = added(small, send(small, "dp", X_SWAP))
    vector_sum, bias_sum = small[:3], small[3]
    grad_normed = grad_own + grad_got[:ROWS].astype(F32)
    back_grad = back_own + back_last.astype(F32)
    front_grad = front_own + front_last.astype(F32)

    local_centred = local - jnp.mean(local, -1, keepdims=True)
    local_inverse = lax.rsqrt(jnp.mean(local_centred * local_centred, -1, keepdims=True) + EPSILON)
    local_standard = local_centred * local_inverse
    back_local = cotangent.astype(F32)
    grad_standard = grad_normed * vectors[0]
    input_grad = back_local + local_inverse * (
        grad_standard
        - jnp.mean(grad_standard, -1, keepdims=True)
        - local_standard * jnp.mean(grad_standard * local_standard, -1, keepdims=True)
    )

    vector_grad = jnp.concatenate([vector_sum, vector_sum[2:3]], 0)

    attn_grad = jnp.stack(
        [front_grad[:, :HC], front_grad[:, HC : 2 * HC], front_grad[:, 2 * HC : 3 * HC], back_grad[:, :HC]]
    )
    mlp_grad = jnp.stack([front_grad[:, 3 * HC :], back_grad[:, HC:]])
    qkv_grad = bias_sum[: 3 * HC].reshape(3, HC)
    fc1_grad = bias_sum[3 * HC : 3 * HC + FC]
    attn_out = adamw(attn_weight, attn_grad, attn_first, attn_second, 0.04, 0.1)
    mlp_out = adamw(mlp_weight, mlp_grad, mlp_first, mlp_second, 0.04, 0.1)
    qkv_out = adamw(qkv_bias, qkv_grad, qkv_first, qkv_second, 0.3, 0.0)
    fc1_out = adamw(fc1_bias, fc1_grad, fc1_first, fc1_second, 0.3, 0.0)
    vector_out = adamw(vectors, vector_grad, vector_first, vector_second, 0.2, 0.0)
    return (out, input_grad, *attn_out, *mlp_out, *qkv_out, *fc1_out, *vector_out)


def solution(mesh):
    rows = P(("dp", "tensor"), None)
    weight = P(None, "dp", "tensor")
    qkv = P(None, "tensor")
    fc1 = P("tensor")
    return jax.shard_map(
        per_device,
        mesh=mesh,
        in_specs=(rows, rows, weight, weight, qkv, fc1, P()) + (weight, weight, qkv, fc1, P()) * 2,
        out_specs=(rows, rows) + (weight,) * 8 + (qkv,) * 4 + (fc1,) * 4 + (P(),) * 4,
        check_vma=False,
    )
```

```python
import functools

import jax
import jax.numpy as jnp
import numpy as np
from jax import lax
from jax.experimental import pallas as pl
from jax.experimental.pallas import tpu as pltpu
from jax.sharding import PartitionSpec as P

D = 2048
HD = 64
ROT = 32
LEN = 1024
STEP = 10
HEADS = 4
HC = HEADS * HD
FC = 1024
ROWS = 128
HALF = ROWS // 2
BQ = 256

EPSILON = 1e-05
SCALE = 0.125
BETA_ONE = 0.9
BETA_TWO = 0.999
ADAM_EPSILON = 1e-08
BF = jnp.bfloat16
LIMITS = dict(send=8, assemble=5, qkv=7, hidden=9, out=9, grad=8, normed=11, weight=6, forward=11, backward=12)
TIMES = dict(qkv=4.0, hidden=6.0, out=6.0, grad=5.5, normed=9.0, weight=5.0, forward=5.0, backward=8.0)
DECLARED = 0.3
F32 = jnp.float32


def dp_perm(move):
    pairs = []
    for x in range(2):
        for y in range(4):
            for c in range(2):
                nx, ny, nc = move(x, y, c)
                pairs.append(((x * 4 + y) * 2 + c, (nx * 4 + ny % 4) * 2 + nc))
    return pairs


def tensor_perm(move):
    pairs = []
    for z in range(4):
        for h in range(2):
            nz, nh = move(z, h)
            pairs.append((z * 2 + h, (nz % 4) * 2 + nh))
    return pairs


Y_UP = dp_perm(lambda x, y, c: (x, y + 1, c))
Y_DOWN = dp_perm(lambda x, y, c: (x, y - 1, c))
X_SWAP = dp_perm(lambda x, y, c: (1 - x, y, c))
CORE_SWAP = dp_perm(lambda x, y, c: (x, y, 1 - c))
Z_UP = tensor_perm(lambda z, h: (z + 1, h))
Z_DOWN = tensor_perm(lambda z, h: (z - 1, h))
Y_FAR = dp_perm(lambda x, y, c: (x, y + 2, c))
Z_FAR = tensor_perm(lambda z, h: (z + 2, h))
H_SWAP = tensor_perm(lambda z, h: (z, 1 - h))


def at(array, index, axis):
    return lax.dynamic_index_in_dim(array, index, axis, keepdims=False)


def up_z(v):
    return lax.ppermute(v, "tensor", Z_UP)


def down_z(v):
    return lax.ppermute(v, "tensor", Z_DOWN)


def swap_h(v):
    return lax.ppermute(v, "tensor", H_SWAP)


def up_y(v):
    return lax.ppermute(v, "dp", Y_UP)


def down_y(v):
    return lax.ppermute(v, "dp", Y_DOWN)


def swap_x(v):
    return lax.ppermute(v, "dp", X_SWAP)


def swap_core(v):
    return lax.ppermute(v, "dp", CORE_SWAP)


SMEM = pl.BlockSpec(memory_space=pltpu.SMEM)
VMEM = pl.BlockSpec(memory_space=pltpu.VMEM)


ANY = pl.BlockSpec(memory_space=pl.ANY)


def part(arrays, k):
    for held in arrays:
        if k < held.shape[0]:
            return pl.BlockSpec((1, *held.shape[1:]), lambda i: (k, 0, 0)), held
        k -= held.shape[0]


def call(kernel, out_shape, mebibytes, in_specs=None, scratch_shapes=(), us=1.0, deps=()):
    def run(*args):
        specs = list(in_specs or [VMEM] * len(args))
        gridded = any(spec.index_map is not None for spec in specs)

        def fit(spec, array):
            if gridded and spec is VMEM:
                return pl.BlockSpec(array.shape, lambda i: (0,) * len(array.shape))
            return spec

        def body(*refs):
            kernel(*refs[: len(args)], *refs[len(args) + len(deps) :])

        return pl.pallas_call(
            body,
            out_shape=out_shape,
            grid=(1,) if gridded else (),
            out_specs=jax.tree.map(lambda out: fit(VMEM, out), out_shape),
            in_specs=[fit(spec, arg) for spec, arg in zip(specs, args)] + [ANY] * len(deps),
            scratch_shapes=scratch_shapes,
            compiler_params=pltpu.CompilerParams(vmem_limit_bytes=mebibytes * 1024 * 1024),
            cost_estimate=pl.CostEstimate(
                flops=int(us * DECLARED * 1.1e9), bytes_accessed=1000, transcendentals=0
            ),
        )(*args, *deps)

    return run


def nothing_kernel(*refs):
    pass


def tied(value, *deps):
    return pl.pallas_call(
        nothing_kernel,
        out_shape=jax.ShapeDtypeStruct(value.shape, value.dtype),
        in_specs=[ANY] * (1 + len(deps)),
        out_specs=ANY,
        input_output_aliases={0: 0},
        compiler_params=pltpu.CompilerParams(vmem_limit_bytes=1024 * 1024),
        cost_estimate=pl.CostEstimate(flops=1000, bytes_accessed=1000, transcendentals=0),
    )(value, *deps)


def shape(rows, columns, dtype=BF):
    return jax.ShapeDtypeStruct((rows, columns), dtype)


def normalized(block, vectors, normed, stats, at):
    inputs = block.astype(F32)
    mean = jnp.mean(inputs, -1, keepdims=True)
    centred = inputs - mean
    inverse = lax.rsqrt(jnp.mean(centred * centred, -1, keepdims=True) + EPSILON)
    normed[at, :] = (centred * inverse * vectors[0:1, :] + vectors[1:2, :]).astype(BF)
    lane = lax.broadcasted_iota(jnp.int32, (ROWS, 128), 1)
    stats[at, :] = jnp.where(lane < 64, mean, inverse)


def norm_first_kernel(own, swapped, below, above, vectors, normed, stats):
    for i, block in enumerate((own, swapped, below, above)):
        normalized(block[...], vectors, normed, stats, slice(i * ROWS, (i + 1) * ROWS))


def norm_second_kernel(below, above, vectors, normed, stats):
    far = jnp.concatenate([below[ROWS:, :], above[ROWS:, :]], 0)
    for i, block in enumerate((below[:ROWS, :], above[:ROWS, :], far)):
        normalized(block, vectors, normed, stats, slice(i * ROWS, (i + 1) * ROWS))


def norm_last_kernel(info, below, above, vectors, normed_a, stats_a, normed_b, stats_b, normed, stats):
    places = At(info, ROW_PLACES)
    at = [pl.ds(pl.multiple_of(places[i] * ROWS, ROWS), ROWS) for i in range(8)]
    normalized(jnp.concatenate([below[:HALF, :], above[:HALF, :]], 0), vectors, normed, stats, at[7])
    for i in range(7):
        held, held_stats, k = (normed_a, stats_a, i) if i < 4 else (normed_b, stats_b, i - 4)
        normed[at[i], :] = held[k * ROWS : (k + 1) * ROWS, :]
        stats[at[i], :] = held_stats[k * ROWS : (k + 1) * ROWS, :]


def rows_kernel(skipped, info, own, swapped, below, above, below_mid, above_mid, first, second, rows):
    places = At(info, ROW_PLACES)
    far = jnp.concatenate([below_mid[ROWS:, :], above_mid[ROWS:, :]], 0)
    last = jnp.concatenate([first[:HALF, :], second[:HALF, :]], 0)
    near = [ref[skipped : skipped + ROWS, :] for ref in (below, above)]
    blocks = (own[...], swapped[...], *near, below_mid[:ROWS, :], above_mid[:ROWS, :], far, last)
    for i, block in enumerate(blocks):
        rows[pl.ds(pl.multiple_of(places[i] * ROWS, ROWS), ROWS), :] = block


def rows_call(skipped, info, *blocks, deps=()):
    return call(
        functools.partial(rows_kernel, skipped), shape(LEN, D), 12, [SMEM] + [VMEM] * 8, deps=deps
    )(info, *blocks)


def beside(message, wide, rows):
    done = 0
    for piece in wide:
        message[done : done + piece.shape[0], : piece.shape[1]] = piece
        done += piece.shape[0]
    columns, middle = wide[0].shape[1], rows.shape[1] // 2
    message[:ROWS, columns:] = rows[:, :middle]
    message[ROWS:, columns:] = rows[:, middle:]


def apart(message, columns):
    return jnp.concatenate([message[:ROWS, columns:], message[ROWS:, columns:]], 1)


def stack(out, *pieces):
    done = 0
    for piece in pieces:
        out[done : done + piece.shape[0], :] = piece
        done += piece.shape[0]


def send_second_kernel(swapped, below, above, qkv_own, qkv_swapped, rest_own, up, down, pair, rest):
    stack(up, swapped[...], below[:HALF, :])
    stack(down, swapped[...], above[HALF:, :])
    stack(pair, qkv_own[...], qkv_swapped[...])
    rest[...] = rest_own[...]


def send_third_kernel(
    below_mid, above_mid, qkv_below, qkv_above, rest_own, rest_swapped, backs, up, down, message_up, message_down, backs_out
):
    stack(up, below_mid[:HALF, :], backs[...])
    stack(down, above_mid[HALF:ROWS, :], backs[...])
    pair = rest_own[:, :FC], rest_swapped[:, :FC]
    beside(message_up, pair, qkv_below[:ROWS, :])
    beside(message_down, pair, qkv_above[ROWS:, :])
    backs_out[...] = backs[...]


def send_fourth_kernel(
    below_last,
    above_last,
    message_below,
    message_above,
    backs_swapped,
    rest_own,
    rest_swapped,
    qkv_pair,
    qkv_below,
    qkv_above,
    up,
    down,
    message_up,
    message_down,
    qkv_mine,
):
    stack(up, backs_swapped[...], below_last[HALF:ROWS, :])
    stack(down, backs_swapped[...], above_last[ROWS:, :])
    pair = rest_own[:, FC:], rest_swapped[:, FC:]
    beside(message_up, pair, message_below[:ROWS, :FC])
    beside(message_down, pair, message_above[ROWS:, :FC])
    stack(qkv_mine, qkv_pair[...], qkv_above[...], apart(message_below, FC), apart(message_above, FC), qkv_below[...])


def send_fifth_kernel(
    below_backs,
    above_backs,
    own_first,
    below_first,
    above_first,
    own_second,
    below_second,
    above_second,
    up,
    down,
    far_up,
    far_down,
    fc1_mine,
    back_mine,
):
    up[...] = below_backs[:HALF, :]
    down[...] = above_backs[HALF:ROWS, :]
    columns = HC + FC
    far_up[...] = below_second[:ROWS, :columns]
    far_down[...] = above_second[ROWS:, :columns]
    stack(
        fc1_mine,
        own_first[:, :FC],
        above_first[:, :FC],
        apart(below_second, columns),
        apart(above_second, columns),
        below_first[:, :FC],
    )
    stack(back_mine, own_second[:, :columns], above_second[:, :columns], below_second[:, :columns])


def send_sixth_kernel(far, far_swapped, mine):
    stack(mine, far[...], far_swapped[...])


PLACES, BACK_PLACES, FIRST_PLACES, SECOND_PLACES, ROW_PLACES, GROUPS, OWN_X, OWN_H = (0, 16, 32, 40, 48, 56, 60, 61)


def position_table():
    table = np.zeros((128, 64), np.int32)
    for dp in range(16):
        x, y, core = dp // 8, dp // 2 % 4, dp % 2

        def block(step, other_x, c):
            return ((x ^ other_x) * 4 + (y + step) % 4) * 2 + c

        def gathered(steps):
            return [block(step, o, c) for c in (core, 1 - core) for step in steps for o in (0, 1)]

        def grads(c):
            return [(xx * 4 + (y + step) % 4) * 2 + c for step in (2, 1, 3, 0) for xx in (0, 1)]

        for tensor in range(8):
            z, h = tensor // 2, tensor % 2

            def row(step, other):
                return (z + step) % 4 * 2 + (h ^ other)

            rows = [row(0, 0), row(0, 1), row(3, 0), row(1, 0), row(3, 1), row(1, 1), row(2, 0), row(2, 1)]
            groups = [(z + step) % 4 for step in (2, 1, 3, 0)]
            table[dp * 8 + tensor] = [
                *gathered((0, 1, 2, 3)),
                *gathered((0, 1, 3, 2)),
                *grads(1 - core),
                *grads(core),
                *rows,
                *groups,
                x,
                h,
                0,
                0,
            ]
    return table


class At:
    def __init__(self, info, first):
        self.info, self.first = info, first

    def __getitem__(self, i):
        return self.info[self.first + i]


EXTRA = 16


def coded(sums):
    high = sums.astype(BF)
    low = (sums - high.astype(F32)).astype(BF)
    rest = jnp.zeros((EXTRA - 2 * sums.shape[0], sums.shape[1]), F32)
    return jnp.concatenate([high.astype(F32), low.astype(F32), rest], 0).astype(BF)


def decoded(block):
    block = block.astype(F32)
    return block[:3] + block[3:6]


def near_kernel(above, below, from_below, from_above, *refs):
    up, down = refs[-2:]
    up[:ROWS, :] = (above[:ROWS, :].astype(F32) + from_below[...].astype(F32)).astype(BF)
    up[ROWS:256, :] = above[ROWS:, :]
    down[:ROWS, :] = below[:ROWS, :]
    down[ROWS:256, :] = (below[ROWS:, :].astype(F32) + from_above[...].astype(F32)).astype(BF)
    if len(refs) > 2:
        block = coded(refs[0][:3, :])
        up[256:, :] = block
        down[256:, :] = block


def near(above, below, from_below, from_above, *sums, deps=()):
    rows = 256 + EXTRA * len(sums)
    return call(near_kernel, [shape(rows, above.shape[1])] * 2, 12, deps=deps)(
        above, below, from_below, from_above, *sums
    )


def last_kernel(info, here, got_up, got_down, kept, sent):
    own = At(info, OWN_H)[0]
    for out, which in ((kept, own), (sent, 1 - own)):
        at = pl.ds(pl.multiple_of(which * ROWS, ROWS), ROWS)
        total = here[at, :].astype(F32) + got_up[at, :].astype(F32) + got_down[at, :].astype(F32)
        out[...] = total.astype(out.dtype)


def last(info, here, got_up, got_down, deps=()):
    columns = here.shape[1]
    return call(
        last_kernel, [shape(ROWS, columns, F32), shape(ROWS, columns)], 10, [SMEM] + [VMEM] * 3, deps=deps
    )(info, here, got_up, got_down)


def grad_last_kernel(info, here, got_up, got_down, sums, far_sums, kept, sent, total_sums):
    last_kernel(info, here, got_up, got_down, kept, sent.at[:ROWS])
    total = sums[:3, :] + far_sums[:3, :] + decoded(got_up[256:, :]) + decoded(got_down[256:, :])
    total_sums[...] = total
    sent[ROWS:, :] = coded(total)


def grad_last(info, here, got_up, got_down, sums, far_sums, deps=()):
    outs = [shape(ROWS, D, F32), shape(ROWS + EXTRA, D), shape(3, D, F32)]
    return call(grad_last_kernel, outs, 12, [SMEM] + [VMEM] * 5, deps=deps)(
        info, here, got_up, got_down, sums, far_sums
    )


def small_kernel(sums, got, projected, hidden, out):
    out[:3, :] = sums[...] + decoded(got[ROWS:, :])
    rest = jnp.zeros((1, D - 3 * HC - FC), F32)
    out[3:, :] = jnp.concatenate([projected[...], hidden[...], rest], 1)


def plus(mine, got):
    return mine.astype(F32) + got.astype(F32)


def weight_far_kernel(mine, got, first, second):
    total = plus(mine[0], got[0]).astype(BF)
    first[...] = total[:ROWS]
    second[...] = total[ROWS:]


def weight_far(mine, got, deps=()):
    columns = mine[0].shape[2]
    spec, held = part(got, 0)
    return call(weight_far_kernel, [shape(ROWS, columns)] * 2, 14, [VMEM, spec], deps=deps)(mine[0], held)


def weight_near_kernel(above, below, got_above, got_below, from_below, from_above, up, down):
    columns = above.shape[2]
    up[:ROWS, :columns] = (plus(above[0, :ROWS], got_above[0, :ROWS]) + from_below[...].astype(F32)).astype(BF)
    up[ROWS:, :columns] = plus(above[0, ROWS:], got_above[0, ROWS:]).astype(BF)
    down[:ROWS, :columns] = plus(below[0, :ROWS], got_below[0, :ROWS]).astype(BF)
    down[ROWS:, :columns] = (plus(below[0, ROWS:], got_below[0, ROWS:]) + from_above[...].astype(F32)).astype(BF)


def first_near_kernel(above, below, got_above, got_below, from_below, from_above, front, front_got, up, down):
    weight_near_kernel(above, below, got_above, got_below, from_below, from_above, up, down)
    columns = above.shape[2]
    far = plus(front[0], front_got[0]).astype(BF)
    middle = far.shape[1] // 2
    for message, rows in ((up, far[:ROWS]), (down, far[ROWS:])):
        message[:ROWS, columns:] = rows[:, :middle]
        message[ROWS:, columns:] = rows[:, middle:]


def first_near(mine, got, from_below, from_above, front, front_got, deps=()):
    columns, more = mine[0].shape[2], front[0].shape[2]
    (spec, above), (spec2, below), (spec3, far) = part(got, 1), part(got, 2), part(front_got, 0)
    specs = [VMEM, VMEM, spec, spec2, VMEM, VMEM, VMEM, spec3]
    return call(first_near_kernel, [shape(256, columns + more // 2)] * 2, 22, specs, deps=deps)(
        mine[1], mine[2], above, below, from_below, from_above, front[0], far
    )


def second_near_kernel(above, below, got_above, got_below, message_below, message_above, up, down):
    columns = message_below.shape[1] - above.shape[2] // 2
    far = apart(message_below, columns), apart(message_above, columns)
    weight_near_kernel(above, below, got_above, got_below, *far, up, down)


def second_near(mine, got, message_below, message_above, deps=()):
    (spec, above), (spec2, below) = part(got, 1), part(got, 2)
    specs = [VMEM, VMEM, spec, spec2, VMEM, VMEM]
    return call(second_near_kernel, [shape(256, mine[0].shape[2])] * 2, 22, specs, deps=deps)(
        mine[1], mine[2], above, below, message_below, message_above
    )


def weight_last_kernel(info, mine, got, got_up, got_down, kept, sent):
    columns, own = mine.shape[2], At(info, OWN_X)[0]
    for out, which in ((kept, own), (sent, 1 - own)):
        at = pl.ds(pl.multiple_of(which * ROWS, ROWS), ROWS)
        total = plus(mine[0, at, :], got[0, at, :]) + plus(got_up[at, :columns], got_down[at, :columns])
        out[...] = total.astype(out.dtype)


def weight_last(info, mine, got, got_up, got_down, deps=()):
    columns = mine[0].shape[2]
    spec, here = part(got, 3)
    specs = [SMEM, VMEM, spec, VMEM, VMEM]
    return call(weight_last_kernel, [shape(ROWS, columns, F32), shape(ROWS, columns)], 16, specs, deps=deps)(
        info, mine[3], here, got_up, got_down
    )


def add_kernel(first, *refs):
    total = first[...]
    for ref in refs[:-1]:
        total = total + ref[...]
    refs[-1][...] = total


def added(*values, deps=()):
    return call(add_kernel, jax.ShapeDtypeStruct(values[0].shape, F32), 4, deps=deps)(*values)


def send(v, axes, perm):
    return lax.ppermute(v, axes, perm)


def rotary_tables():
    half = ROT // 2
    position = np.arange(LEN, dtype=np.float32)
    frequency = np.float32(10000.0) ** (-np.arange(half, dtype=np.float32) * np.float32(2.0 / ROT))
    angle = (position[:, None] * frequency[None, :].astype(np.float32)).astype(np.float32)
    cosine, sine = np.cos(angle), np.sin(angle)
    rest = np.ones((LEN, HD - ROT), np.float32)
    none = np.zeros((LEN, half), np.float32)
    same = np.concatenate([cosine, cosine, rest] * 2, 1)
    ahead = np.concatenate([-sine, none, 0 * rest] * 2, 1)
    behind = np.concatenate([none, sine, 0 * rest] * 2, 1)
    return jnp.asarray(np.concatenate([same, ahead, behind], 1).astype(np.float32))


def rotated(values, tables, sign):
    wide = [jnp.concatenate([tables[:, j * 128 : (j + 1) * 128]] * 2, 1) for j in range(3)]
    half = ROT // 2
    return values * wide[0] + sign * (
        pltpu.roll(values, HC - half, 1) * wide[1] + pltpu.roll(values, half, 1) * wide[2]
    )


WIDE = 256


def assemble_kernel(first, info, *refs):
    places, out = At(info, first), refs[-1]
    done = 0
    for source in refs[:-1]:
        for i in range(source.shape[0] // ROWS):
            start = pl.multiple_of(places[done] * ROWS, ROWS)
            out[pl.ds(start, ROWS), :] = source[i * ROWS : (i + 1) * ROWS, :]
            done += 1


def assembled(first, info, *sources, deps=()):
    specs = [SMEM] + [VMEM] * len(sources)
    return call(
        functools.partial(assemble_kernel, first),
        shape(D, sources[0].shape[1]),
        LIMITS["assemble"],
        specs,
        us=2.0,
        deps=deps,
    )(info, *sources)


def qkv_kernel(rows, weights, bias, tables, heads):
    for j in range(3):
        part = slice(j * HC, (j + 1) * HC)
        pre = nn(rows[...], weights[:, part]) + bias[j : j + 1]
        heads[:, part] = (rotated(pre, tables, 1.0) if j < 2 else pre).astype(BF)


def qkv_call(normed, weights, bias, tables, deps=()):
    return call(qkv_kernel, shape(LEN, 3 * HC), LIMITS["qkv"], us=TIMES["qkv"], deps=deps)(normed, weights, bias, tables)


ROOT = 0.7978845608028654
CUBIC = 0.044715


def hidden_kernel(rows, weights, bias, activated, slope):
    for j in range(FC // WIDE):
        part = slice(j * WIDE, (j + 1) * WIDE)
        hidden = nn(rows[...], weights[:, part]) + bias[:, part]
        square = hidden * hidden
        bent = jnp.tanh(ROOT * (hidden + CUBIC * (square * hidden)))
        half = 0.5 * (1.0 + bent)
        activated[:, part] = (hidden * half).astype(BF)
        slope[:, part] = (
            half + (0.5 * ROOT) * hidden * (1.0 - bent * bent) * (1.0 + (3.0 * CUBIC) * square)
        ).astype(BF)


def hidden_call(normed, weights, bias, deps=()):
    return call(hidden_kernel, [shape(LEN, FC)] * 2, LIMITS["hidden"], us=TIMES["hidden"], deps=deps)(
        normed, weights, bias.reshape(1, FC)
    )


def out_kernel(steps, info, attended, activated, weights, *parts):
    groups = At(info, GROUPS)
    for i, r in enumerate(steps):
        here = pl.ds(pl.multiple_of(groups[r] * 256, 256), 256)
        rows = jnp.concatenate([attended[here, :], activated[here, :]], 1)
        low = nt(rows, weights[...]).astype(BF)
        if r == 0:
            parts[0][...] = low[:ROWS]
            parts[1][...] = low[ROWS:]
        else:
            parts[i][...] = low


def out_call(steps, info, attended, activated, weights, deps=()):
    return call(
        functools.partial(out_kernel, steps),
        [shape(ROWS, D)] * 2 if steps == (0,) else [shape(256, D)] * len(steps),
        LIMITS["out"],
        [SMEM] + [VMEM] * 3,
        us=TIMES["out"] * len(steps) / 4,
        deps=deps,
    )(info, attended, activated, weights)


def grad_kernel(backs, slope, weights, grad_attended, grad_hidden, sums):
    for j in range((HC + FC) // WIDE):
        grad = nn(backs[...], weights[:, j * WIDE : (j + 1) * WIDE])
        if j == 0:
            grad_attended[...] = grad.astype(BF)
        else:
            part = slice((j - 1) * WIDE, j * WIDE)
            low = (grad * slope[:, part].astype(F32)).astype(BF)
            grad_hidden[:, part] = low
            sums[:, part] = jnp.sum(low.astype(F32), 0, keepdims=True)


def grad_call(backs, slope, weights, deps=()):
    return call(
        grad_kernel, [shape(LEN, HC), shape(LEN, FC), shape(1, FC, F32)], LIMITS["grad"], us=TIMES["grad"], deps=deps
    )(backs, slope, weights)


def normed_kernel(steps, info, projected, hidden, rows, stats, weights, weights2, before, *refs):
    parts, sums = refs[:-1], refs[-1]
    groups = At(info, GROUPS)
    for n in range(2):
        columns = slice(n * D // 2, (n + 1) * D // 2)
        first, second = before[0:1, columns], before[1:2, columns]
        for i, r in enumerate(steps):
            here = pl.ds(pl.multiple_of(groups[r] * 256, 256), 256)
            grad = nt(projected[here, :], weights[columns, :]) + nt(hidden[here, :], weights2[columns, :])
            low = grad.astype(BF)
            if r == 0:
                parts[0][:, columns] = low[:ROWS]
                parts[1][:, columns] = low[ROWS:]
            else:
                parts[i][:, columns] = low
            standard = (rows[here, columns].astype(F32) - stats[here, 0:1]) * stats[here, 64:65]
            first = first + jnp.sum(grad * standard, 0, keepdims=True)
            second = second + jnp.sum(grad, 0, keepdims=True)
        sums[0:1, columns] = first
        sums[1:2, columns] = second
    sums[2:, :] = before[2:, :]


def normed_call(steps, info, projected, hidden, rows, stats, weights, weights2, before, deps=()):
    parts = [shape(ROWS, D)] * 2 if steps == (0,) else [shape(256, D)] * len(steps)
    return call(
        functools.partial(normed_kernel, steps),
        parts + [shape(4, D, F32)],
        LIMITS["normed"],
        [SMEM] + [VMEM] * 7,
        us=TIMES["normed"] * len(steps) / 4,
        deps=deps,
    )(info, projected, hidden, rows, stats, weights, weights2, before)


def weight_kernel(counts, parts, first, info, *refs):
    places, outs, refs = At(info, first), refs[-len(parts) :], list(refs[: -len(parts)])
    outs = [ref.at[k] for ref, size in zip(outs, parts) for k in range(size)]
    done = 0
    for count in counts:
        left, rights, refs = refs[0], refs[1 : 1 + count], refs[1 + count :]
        for step in range(2):
            turned = jnp.concatenate(
                [left[:, pl.ds(pl.multiple_of(places[4 * step + j] * ROWS, ROWS), ROWS)] for j in range(4)], 1
            ).T
            column = done
            for right in rights:
                for j in range(right.shape[1] // WIDE):
                    term = nn(turned, right[:, j * WIDE : (j + 1) * WIDE]).astype(BF)
                    outs[2 * step][:, column : column + WIDE] = term[:256]
                    outs[2 * step + 1][:, column : column + WIDE] = term[256:]
                    column += WIDE
        done = column


def weight_call(parts, first, info, *terms, deps=()):
    columns = sum(r.shape[1] for term in terms for r in term[1:])
    flat = [r for term in terms for r in term]
    outs = [jax.ShapeDtypeStruct((size, 256, columns), BF) for size in parts]
    return call(
        functools.partial(weight_kernel, [len(term) - 1 for term in terms], parts, first),
        outs,
        LIMITS["weight"],
        [SMEM] + [VMEM] * len(flat),
        us=TIMES["weight"] * columns / 2304,
        deps=deps,
    )(info, *flat)


def nt(left, right):
    return lax.dot_general(left, right, (((1,), (1,)), ((), ())), preferred_element_type=F32)


def nn(left, right):
    return lax.dot_general(left, right, (((1,), (0,)), ((), ())), preferred_element_type=F32)


POWER = SCALE * 1.4426950408889634


def by_head(block, lane):
    return jnp.concatenate([jnp.where(lane == h, block, jnp.zeros((), BF)) for h in range(HEADS)], 0)


def seen_mask():
    key = lax.broadcasted_iota(jnp.int32, (BQ, BQ), 0)
    query = lax.broadcasted_iota(jnp.int32, (BQ, BQ), 1)
    return jnp.concatenate([key <= query] * HEADS, 1)


def forward_kernel(heads, attended, logsum, out_t, values_t):
    queries, keys, values = (heads.at[:, j * HC : (j + 1) * HC] for j in range(3))
    values_t[...] = values[...].T
    lane = lax.broadcasted_iota(jnp.int32, (BQ, HC), 1) // HD
    seen = seen_mask()
    for q in range(LEN // BQ):
        here = slice(q * BQ, (q + 1) * BQ)
        query = by_head(queries[here, :], lane)
        blocks = []
        largest = None
        for k in range(q + 1):
            block = nt(keys[k * BQ : (k + 1) * BQ, :], query)
            if k == q:
                block = jnp.where(seen, block, -1e30)
            blocks.append(block)
            top = jnp.max(block, 0, keepdims=True)
            largest = top if largest is None else jnp.maximum(largest, top)
        total = jnp.zeros((1, HEADS * BQ), F32)
        found = [jnp.zeros((HD, BQ), F32)] * HEADS
        for k in range(q + 1):
            powers = jnp.exp2((blocks[k] - largest) * POWER)
            total = total + jnp.sum(powers, 0, keepdims=True)
            low = powers.astype(BF)
            for h in range(HEADS):
                found[h] = found[h] + nn(
                    values_t[h * HD : (h + 1) * HD, k * BQ : (k + 1) * BQ], low[:, h * BQ : (h + 1) * BQ]
                )
        scale = 1.0 / total
        base = largest * POWER + jnp.log2(total)
        for h in range(HEADS):
            out_t[h * HD : (h + 1) * HD, here] = found[h] * scale[:, h * BQ : (h + 1) * BQ]
            logsum[h : h + 1, here] = base[:, h * BQ : (h + 1) * BQ]
    attended[...] = out_t[...].T.astype(BF)


def forward_call(heads, deps=()):
    return call(
        forward_kernel,
        [shape(LEN, HC), shape(8, LEN, F32), shape(HC, LEN, F32)],
        LIMITS["forward"],
        scratch_shapes=[pltpu.VMEM((HC, LEN), BF)],
        us=TIMES["forward"],
        deps=deps,
    )(heads)


def backward_kernel(
    heads, grads, logsum, out_t, tables, out, sums, keys_t, query_grads, key_grads, value_grads
):
    queries, keys, values = (heads.at[:, j * HC : (j + 1) * HC] for j in range(3))
    keys_t[...] = keys[...].T
    turned = grads[...].astype(F32).T * out_t[...]
    lane = lax.broadcasted_iota(jnp.int32, (BQ, HC), 1) // HD
    seen = seen_mask()
    for q in reversed(range(LEN // BQ)):
        here = slice(q * BQ, (q + 1) * BQ)
        query = by_head(queries[here, :], lane)
        grad = by_head(grads[here, :], lane)
        base = jnp.concatenate([logsum[h : h + 1, here] for h in range(HEADS)], 1)
        dots = jnp.concatenate(
            [jnp.sum(turned[h * HD : (h + 1) * HD, here], 0, keepdims=True) for h in range(HEADS)], 1
        )
        found = [jnp.zeros((HD, BQ), F32)] * HEADS
        for k in range(q + 1):
            there = slice(k * BQ, (k + 1) * BQ)
            probs = jnp.exp2(nt(keys[there, :], query) * POWER - base)
            if k == q:
                probs = jnp.where(seen, probs, 0.0)
            score = (probs * (nt(values[there, :], grad) - dots)).astype(BF)
            value_grad, key_grad = nn(probs.astype(BF), grad), nn(score, query)
            if q == LEN // BQ - 1:
                value_grads[there, :] = value_grad
                key_grads[there, :] = key_grad
            else:
                value_grads[there, :] += value_grad
                key_grads[there, :] += key_grad
            for h in range(HEADS):
                found[h] = found[h] + nn(
                    keys_t[h * HD : (h + 1) * HD, there], score[:, h * BQ : (h + 1) * BQ]
                )
        for h in range(HEADS):
            query_grads[h * HD : (h + 1) * HD, here] = found[h]
    parts = (
        rotated(query_grads[...].T * SCALE, tables, -1.0),
        rotated(key_grads[...] * SCALE, tables, -1.0),
        value_grads[...],
    )
    for j, part in enumerate(parts):
        low = part.astype(BF)
        out[:, j * HC : (j + 1) * HC] = low
        sums[:, j * HC : (j + 1) * HC] = jnp.sum(low.astype(F32), 0, keepdims=True)


def backward_call(heads, grads, logsum, out_t, tables, deps=()):
    return call(
        backward_kernel,
        [shape(LEN, 3 * HC), shape(1, 3 * HC, F32)],
        LIMITS["backward"],
        scratch_shapes=[pltpu.VMEM((HC, LEN), BF), pltpu.VMEM((HC, LEN), F32)] + [pltpu.VMEM((LEN, HC), F32)] * 2,
        us=TIMES["backward"],
        deps=deps,
    )(heads, grads, logsum, out_t, tables)


def adamw(param, grad, first, second, rate, decay):
    first_new = BETA_ONE * first + (1.0 - BETA_ONE) * grad
    second_new = BETA_TWO * second + (1.0 - BETA_TWO) * grad * grad
    ratio = (
        first_new
        / (1.0 - BETA_ONE**STEP)
        / (jnp.sqrt(second_new / (1.0 - BETA_TWO**STEP)) + ADAM_EPSILON)
    )
    return (grad, first_new, second_new, param - rate * (ratio + decay * param))


def side_by_side(stack):
    return jnp.concatenate([stack[j] for j in range(stack.shape[0])], 1)


def per_device(
    tokens,
    cotangent,
    attn_weight,
    mlp_weight,
    qkv_bias,
    fc1_bias,
    vectors,
    attn_first,
    mlp_first,
    qkv_first,
    fc1_first,
    vector_first,
    attn_second,
    mlp_second,
    qkv_second,
    fc1_second,
    vector_second,
):
    dp = lax.axis_index("dp")
    tensor = lax.axis_index("tensor")
    info = lax.dynamic_index_in_dim(jnp.asarray(position_table()), dp * 8 + tensor, 0, keepdims=False)
    tables = rotary_tables()
    qkv_own = side_by_side(attn_weight[:3].astype(BF))
    rest_own = jnp.concatenate([mlp_weight[0], attn_weight[3], mlp_weight[1]], 1).astype(BF)

    columns = HC + FC

    back_sum = jnp.pad(jnp.sum(cotangent.astype(F32), 0, keepdims=True), ((2, 1), (0, 0)))

    swapped = swap_h(tokens)
    below_own, above_own = up_z(tokens), down_z(tokens)
    qkv_swapped = swap_x(qkv_own)
    sent = call(
        send_second_kernel, [shape(192, D)] * 2 + [shape(256, 3 * HC), shape(ROWS, HC + 2 * FC)], LIMITS["send"], deps=(info, back_sum)
    )(swapped, below_own, above_own, qkv_own, qkv_swapped, rest_own)
    below_mid, above_mid = up_z(sent[0]), down_z(sent[1])
    qkv_pair = sent[2]
    qkv_below, qkv_above = up_y(qkv_pair), down_y(qkv_pair)
    rest_swapped = swap_x(sent[3])
    normed_a = call(norm_first_kernel, [shape(512, D), shape(512, 128, F32)], 8, deps=(qkv_pair,))(
        tokens, swapped, below_own, above_own, vectors
    )
    sent = call(
        send_third_kernel,
        [shape(192, D)] * 2 + [shape(256, FC + 3 * HC // 2)] * 2 + [shape(ROWS, D)],
        LIMITS["send"],
        deps=(normed_a[1],),
    )(below_mid, above_mid, qkv_below, qkv_above, rest_own, rest_swapped, cotangent)
    below_last, above_last = up_z(sent[0]), down_z(sent[1])
    own_first = sent[2]
    below_first, above_first = up_y(sent[2]), down_y(sent[3])
    backs_swapped = swap_h(sent[4])
    normed_b = call(norm_second_kernel, [shape(384, D), shape(384, 128, F32)], 8, deps=(own_first,))(
        below_mid, above_mid, vectors
    )
    sent = call(
        send_fourth_kernel,
        [shape(192, D)] * 2 + [shape(256, columns + FC // 2)] * 2 + [shape(8 * ROWS, 3 * HC)],
        LIMITS["send"],
        deps=(normed_b[1],),
    )(
        below_last,
        above_last,
        below_first,
        above_first,
        backs_swapped,
        rest_own,
        rest_swapped,
        qkv_pair,
        qkv_below,
        qkv_above,
    )
    below_backs, above_backs = up_z(sent[0]), down_z(sent[1])
    own_second = sent[2]
    below_second, above_second = up_y(sent[2]), down_y(sent[3])
    qkv_mine = sent[4]
    qkv_other = swap_core(qkv_mine)
    normed, stats = call(
        norm_last_kernel, [shape(LEN, D), shape(LEN, 128, F32)], 12, [SMEM] + [VMEM] * 7, deps=(qkv_mine,)
    )(info, below_last, above_last, vectors, *normed_a, *normed_b)
    qkv_full = assembled(PLACES, info, qkv_mine, qkv_other, deps=(stats,))
    heads = qkv_call(normed, qkv_full, qkv_bias, tables)
    attended, logsum, attended_t = forward_call(heads)
    rows = rows_call(
        0,
        info,
        tokens,
        swapped,
        below_own,
        above_own,
        below_mid,
        above_mid,
        below_last,
        above_last,
        deps=(logsum,),
    )
    sent = call(
        send_fifth_kernel,
        [shape(HALF, D)] * 2 + [shape(ROWS, columns)] * 2 + [shape(8 * ROWS, FC), shape(6 * ROWS, columns)],
        LIMITS["send"],
        deps=(logsum, rows),
    )(below_backs, above_backs, own_first, below_first, above_first, own_second, below_second, above_second)
    first_backs, second_backs = up_z(sent[0]), down_z(sent[1])
    back_far, back_far_swapped = up_y(sent[2]), down_y(sent[3])
    fc1_mine, back_mine = sent[4:]
    fc1_other = swap_core(fc1_mine)
    back_other = swap_core(back_mine)
    fc1_full = assembled(PLACES, info, fc1_mine, fc1_other)
    activated, slope = hidden_call(normed, fc1_full, fc1_bias)
    far_mine = call(
        send_sixth_kernel, shape(256, columns), LIMITS["send"], deps=(slope, first_backs, second_backs, back_other)
    )(back_far, back_far_swapped)
    far_other = swap_core(far_mine)
    backs = rows_call(
        HALF,
        info,
        cotangent,
        backs_swapped,
        below_last,
        above_last,
        below_backs,
        above_backs,
        first_backs,
        second_backs,
        deps=(far_mine,),
    )
    back_full = assembled(BACK_PLACES, info, back_mine, far_mine, back_other, far_other, deps=(backs,))
    out_far = out_call((0,), info, attended, activated, back_full)
    from_below, from_above = up_z(out_far[0]), down_z(out_far[1])
    out_parts = out_call((1, 2, 3), info, attended, activated, back_full, deps=(out_far[0],))
    grad_attended, grad_hidden, hidden_sums = grad_call(backs, slope, back_full, deps=(out_parts[0],))
    back = (backs, attended, activated)
    (back_other,) = weight_call((4,), FIRST_PLACES, info, back, deps=(hidden_sums,))
    up, down = near(out_parts[0], out_parts[1], from_below, from_above, deps=(back_other,))
    got_up, got_down = up_z(up), down_z(down)
    back_got = (swap_core(tied(back_other, up)),)
    projected, projected_sums = backward_call(heads, grad_attended, logsum, attended_t, tables, deps=(up,))
    back_mine = weight_call((1, 1, 1, 1), SECOND_PLACES, info, back, deps=(projected_sums,))
    front = (normed, projected, grad_hidden)
    front_other = weight_call((1, 1, 1, 1), FIRST_PLACES, info, front, deps=(back_mine[0], *back_got))
    back_far = weight_far(back_mine, back_got, deps=(front_other[0],))
    back_below, back_above = up_y(back_far[0]), down_y(back_far[1])
    front_got = [swap_core(v) for v in front_other[:3]]
    front_mine = weight_call((1, 1, 1, 1), SECOND_PLACES, info, front, deps=(front_other[0],))
    terms = (info, projected, grad_hidden, rows, stats, qkv_full, fc1_full)
    *far_parts, far_sums = normed_call((0,), *terms, back_sum, deps=(back_far[0], front_mine[0]))
    from_below, from_above = up_z(far_parts[0]), down_z(far_parts[1])
    *normed_parts, normed_sums = normed_call((1, 2, 3), *terms, far_sums, deps=(*front_got, got_up, got_down))
    out_own, out_sent = last(info, out_parts[2], got_up, got_down, deps=(normed_sums,))
    out_got = swap_h(out_sent)
    up, down = near(
        normed_parts[0], normed_parts[1], from_below, from_above, normed_sums, deps=(out_sent, back_below, back_above)
    )
    got_up, got_down = up_z(up), down_z(down)
    far_sums = send(tied(normed_sums, up, out_got), "tensor", Z_FAR)
    sent = first_near(back_mine, back_got, back_below, back_above, front_mine, front_got, deps=(up,))
    back_up, back_down = up_y(sent[0]), down_y(sent[1])
    local = tokens.astype(F32)
    out = (local + (out_own + out_got.astype(F32)) + vectors[2] + vectors[3]).astype(BF)
    grad_own, grad_sent, sums = grad_last(
        info, normed_parts[2], got_up, got_down, normed_sums, far_sums, deps=(out_got,)
    )
    grad_got = swap_h(grad_sent)
    sent = second_near(front_mine, front_got, back_up, back_down, deps=(grad_sent,))
    front_up, front_down = up_y(sent[0]), down_y(sent[1])
    back_own, back_sent = weight_last(info, back_mine, back_got, back_up, back_down, deps=(sent[0],))
    back_last = swap_x(back_sent)
    front_got.append(swap_core(tied(front_other[3], back_last)))
    small = call(small_kernel, shape(4, D, F32), 4, deps=(back_last,))(sums, grad_got, projected_sums, hidden_sums)
    small = added(small, send(small, "dp", CORE_SWAP))
    front_own, front_sent = weight_last(
        info, front_mine, front_got, front_up, front_down, deps=(grad_got, back_last, small)
    )
    front_last = swap_x(front_sent)
    small = added(
        small, *(send(tied(small, front_sent), "dp", perm) for perm in (Y_UP, Y_DOWN, Y_FAR)), deps=(front_last,)
    )
    small = added(small, send(small, "dp", X_SWAP))
    vector_sum, bias_sum = small[:3], small[3]
    grad_normed = grad_own + grad_got[:ROWS].astype(F32)
    back_grad = back_own + back_last.astype(F32)
    front_grad = front_own + front_last.astype(F32)

    local_centred = local - jnp.mean(local, -1, keepdims=True)
    local_inverse = lax.rsqrt(jnp.mean(local_centred * local_centred, -1, keepdims=True) + EPSILON)
    local_standard = local_centred * local_inverse
    back_local = cotangent.astype(F32)
    grad_standard = grad_normed * vectors[0]
    input_grad = back_local + local_inverse * (
        grad_standard
        - jnp.mean(grad_standard, -1, keepdims=True)
        - local_standard * jnp.mean(grad_standard * local_standard, -1, keepdims=True)
    )

    vector_grad = jnp.concatenate([vector_sum, vector_sum[2:3]], 0)

    attn_grad = jnp.stack(
        [front_grad[:, :HC], front_grad[:, HC : 2 * HC], front_grad[:, 2 * HC : 3 * HC], back_grad[:, :HC]]
    )
    mlp_grad = jnp.stack([front_grad[:, 3 * HC :], back_grad[:, HC:]])
    qkv_grad = bias_sum[: 3 * HC].reshape(3, HC)
    fc1_grad = bias_sum[3 * HC : 3 * HC + FC]
    attn_out = adamw(attn_weight, attn_grad, attn_first, attn_second, 0.04, 0.1)
    mlp_out = adamw(mlp_weight, mlp_grad, mlp_first, mlp_second, 0.04, 0.1)
    qkv_out = adamw(qkv_bias, qkv_grad, qkv_first, qkv_second, 0.3, 0.0)
    fc1_out = adamw(fc1_bias, fc1_grad, fc1_first, fc1_second, 0.3, 0.0)
    vector_out = adamw(vectors, vector_grad, vector_first, vector_second, 0.2, 0.0)
    return (out, input_grad, *attn_out, *mlp_out, *qkv_out, *fc1_out, *vector_out)


def solution(mesh):
    rows = P(("dp", "tensor"), None)
    weight = P(None, "dp", "tensor")
    qkv = P(None, "tensor")
    fc1 = P("tensor")
    return jax.shard_map(
        per_device,
        mesh=mesh,
        in_specs=(rows, rows, weight, weight, qkv, fc1, P()) + (weight, weight, qkv, fc1, P()) * 2,
        out_specs=(rows, rows) + (weight,) * 8 + (qkv,) * 4 + (fc1,) * 4 + (P(),) * 4,
        check_vma=False,
    )
```
